32 devices in a mesh: rows: 16 (over z, y, core), pos: 2 (over x).
Axes of the slice: x: 2, y: 2, z: 4, core: 2. Of those that a mesh axis runs over, the one named last changes fastest.
Arguments:
- tokens: bfloat16 [64, 768, 768], P(('rows', 'pos')), may hold values from -6 to 6
- segments: int32 [64, 768], P(('rows', 'pos')), may hold values from 0 to 1, never falling along the last dimension, each value on 1 to 576 neighbouring positions
- cotangent: bfloat16 [64, 768, 768], P(('rows', 'pos')), may hold values from -6 to 6
- first_gain: float32 [768], replicated, may hold values from 0.5 to 1.5
- first_shift: float32 [768], replicated, may hold values from -1.25 to 1.25
- mixer_weight: bfloat16 [768, 2304], replicated, may hold values from -0.21875 to 0.21875
- mixer_bias: float32 [2304], replicated, may hold values from -1.25 to 1.25
- short_weight: float32 [3, 2304], replicated, may hold values from -3.5 to 3.5
- short_bias: float32 [2304], replicated, may hold values from -1.75 to 1.75
- embed_weight: float32 [33, 64], replicated, may hold values from -1 to 1
- embed_bias: float32 [64], replicated, may hold values from -3 to 3
- embed_omega: float32 [64], replicated, may hold values from 0.25 to 1.75
- inner_weight: float32 [64, 64], replicated, may hold values from -0.75 to 0.75
- inner_bias: float32 [64], replicated, may hold values from -3 to 3
- inner_omega: float32 [64], replicated, may hold values from 0.25 to 1.75
- outer_weight: float32 [64, 64], replicated, may hold values from -0.75 to 0.75
- outer_bias: float32 [64], replicated, may hold values from -3 to 3
- outer_omega: float32 [64], replicated, may hold values from 0.25 to 1.75
- filter_weight: float32 [64, 768], replicated, may hold values from -0.09375 to 0.09375
- skip_gain: float32 [768], replicated, may hold values from -6 to 6
- output_weight: bfloat16 [768, 768], replicated, may hold values from -0.21875 to 0.21875
- output_bias: float32 [768], replicated, may hold values from -1.25 to 1.25
- second_gain: float32 [768], replicated, may hold values from 0.5 to 1.5
- second_shift: float32 [768], replicated, may hold values from -1.25 to 1.25
- expand_weight: bfloat16 [768, 3072], replicated, may hold values from -0.21875 to 0.21875
- expand_bias: float32 [3072], replicated, may hold values from -1.25 to 1.25
- reduce_weight: bfloat16 [3072, 768], replicated, may hold values from -0.109375 to 0.109375
- reduce_bias: float32 [768], replicated, may hold values from -1.25 to 1.25
Outputs:
- block_out: bfloat16 [64, 768, 768], P(('rows', 'pos'))
- tokens_grad: bfloat16 [64, 768, 768], P(('rows', 'pos'))
- first_gain_grad: float32 [768], replicated
- first_shift_grad: float32 [768], replicated
- mixer_weight_grad: float32 [768, 2304], P('rows', 'pos')
- mixer_bias_grad: float32 [2304], replicated
- short_weight_grad: float32 [3, 2304], replicated
- short_bias_grad: float32 [2304], replicated
- embed_weight_grad: float32 [33, 64], replicated
- embed_bias_grad: float32 [64], replicated
- embed_omega_grad: float32 [64], replicated
- inner_weight_grad: float32 [64, 64], replicated
- inner_bias_grad: float32 [64], replicated
- inner_omega_grad: float32 [64], replicated
- outer_weight_grad: float32 [64, 64], replicated
- outer_bias_grad: float32 [64], replicated
- outer_omega_grad: float32 [64], replicated
- filter_weight_grad: float32 [64, 768], replicated
- skip_gain_grad: float32 [768], replicated
- output_weight_grad: float32 [768, 768], P('rows', 'pos')
- output_bias_grad: float32 [768], replicated
- second_gain_grad: float32 [768], replicated
- second_shift_grad: float32 [768], replicated
- expand_weight_grad: float32 [768, 3072], P('rows', 'pos')
- expand_bias_grad: float32 [3072], replicated
- reduce_weight_grad: float32 [3072, 768], P('rows', 'pos')
- reduce_bias_grad: float32 [768], replicated
The draws below stay inside these ranges and needn't reach their ends.
Inputs may be any that keep to these rules, and one draw needn't show every extreme that they name: `segments`: in each row the ids run through all 2 documents in order, each document holding 1 to 576 tokens.
All inputs are finite; a program needn't handle non-finite values.
Results may differ from the reference program's by a relative error of at most 0.012.
Values may be sent and summed in bfloat16 or wider, within the bound.
A program may use at most 384 MiB of HBM per device.

```python
import math
import jax
import jax.numpy as jnp
import numpy as np
from jax import lax

D = 768
FF = 3072
FILT = 64
EMB = 33
SEQ = 768
DOCS = 2
ROW_DEV = 2
MOST_DOC = 576
BATCH = 64
N_ROWS = 16
N_POS = 2


def level_of(own_key, shape, pieces, least, top_value):
    level = 1.0
    for dim, shards_of in pieces:
        heights = jax.random.uniform(jax.random.fold_in(jax.random.fold_in(own_key, 6), dim), (shards_of,), jnp.float32, least / len(pieces), top_value / len(pieces))
        level = level * jnp.repeat(jnp.exp(heights), shape[dim] // shards_of).reshape((-1,) + (1,) * (len(shape) - 1 - dim))
    return level


def split_up(count, total, reach, skew):
    weights = [(1 << 20) // math.isqrt(grade ** skew) + 1 for grade in range(2, count + 1)]
    surplus, holding = total - reach - (count - 1), [1] * (count - 1)
    while surplus > 0:
        candidates = [i for i in range(count - 1) if holding[i] < reach]
        whole, left = sum([weights[i] for i in candidates]), surplus
        for i in candidates:
            addition = min(reach - holding[i], max(1, left * weights[i] // whole), surplus)
            holding[i] = holding[i] + addition
            surplus = surplus - addition
    return np.array([reach] + holding)


def uneven(own_key, count, total, bound, skew):
    if count == 2:
        one = jax.random.randint(own_key, (), max(1, total - bound), min(bound, total - 1) + 1)
        return jnp.stack([one, total - one])
    tallies = jnp.asarray(split_up(count, total, bound, skew), jnp.int32)
    twos = (count - 1) // 2
    source_of, sink = tallies[1:1 + 2 * twos:2], tallies[2:2 + 2 * twos:2]
    margin = jnp.minimum(source_of - 1, bound - sink)
    shifted = jax.random.randint(jax.random.fold_in(own_key, 1), (twos,), 0, 1 << 20) % (margin + 1)
    tallies = tallies.at[1:1 + 2 * twos:2].set(source_of - shifted).at[2:2 + 2 * twos:2].set(sink + shifted)
    return tallies[jax.random.permutation(jax.random.fold_in(own_key, 2), count)]


def normal_values(stream_key, shape, spread, reach, pieces=(), held_as=jnp.bfloat16):
    factor_of = level_of(stream_key, shape, pieces, -0.22, 0.18) if pieces else 1.0
    entries = jax.random.normal(stream_key, shape, jnp.float32) * spread * factor_of
    return jnp.minimum(jnp.maximum(entries, -reach), reach).astype(held_as)


def setup_inputs(seed: int = 0) -> dict:
    arg_keys = jax.random.split(jax.random.key(seed), 29)
    return {
        "tokens": normal_values(arg_keys[0], (BATCH, SEQ, D), 1.0, 6.0, ((0, 32),)),
        "segments": jax.vmap(lambda own: jnp.searchsorted(jnp.cumsum(uneven(own, DOCS, SEQ, MOST_DOC, 2)), jnp.arange(SEQ), side="right"))(jax.random.split(arg_keys[1], BATCH)).reshape((BATCH, SEQ)).astype(jnp.int32),
        "cotangent": normal_values(arg_keys[2], (BATCH, SEQ, D), 1.0, 6.0, ((0, 32),)),
        "first_gain": jnp.clip(1.0 + 0.1 * jax.random.normal(arg_keys[3], (D,), jnp.float32), 0.5, 1.5),
        "first_shift": normal_values(arg_keys[4], (D,), 0.2, 1.25, (), jnp.float32),
        "mixer_weight": normal_values(arg_keys[5], (D, 3 * D), D ** -0.5, 0.21875),
        "mixer_bias": normal_values(arg_keys[6], (3 * D,), 0.2, 1.25, (), jnp.float32),
        "short_weight": normal_values(arg_keys[7], (3, 3 * D), 3 ** -0.5, 3.5, (), jnp.float32),
        "short_bias": normal_values(arg_keys[8], (3 * D,), 0.3, 1.75, (), jnp.float32),
        "embed_weight": normal_values(arg_keys[9], (EMB, FILT), EMB ** -0.5, 1.0, (), jnp.float32),
        "embed_bias": normal_values(arg_keys[10], (FILT,), 0.5, 3.0, (), jnp.float32),
        "embed_omega": jnp.clip(1.0 + 0.15 * jax.random.normal(arg_keys[11], (FILT,), jnp.float32), 0.25, 1.75),
        "inner_weight": normal_values(arg_keys[12], (FILT, FILT), FILT ** -0.5, 0.75, (), jnp.float32),
        "inner_bias": normal_values(arg_keys[13], (FILT,), 0.5, 3.0, (), jnp.float32),
        "inner_omega": jnp.clip(1.0 + 0.15 * jax.random.normal(arg_keys[14], (FILT,), jnp.float32), 0.25, 1.75),
        "outer_weight": normal_values(arg_keys[15], (FILT, FILT), FILT ** -0.5, 0.75, (), jnp.float32),
        "outer_bias": normal_values(arg_keys[16], (FILT,), 0.5, 3.0, (), jnp.float32),
        "outer_omega": jnp.clip(1.0 + 0.15 * jax.random.normal(arg_keys[17], (FILT,), jnp.float32), 0.25, 1.75),
        "filter_weight": normal_values(arg_keys[18], (FILT, D), (FILT * FILT) ** -0.5, 0.09375, (), jnp.float32),
        "skip_gain": normal_values(arg_keys[19], (D,), 1.0, 6.0, (), jnp.float32),
        "output_weight": normal_values(arg_keys[20], (D, D), D ** -0.5, 0.21875),
        "output_bias": normal_values(arg_keys[21], (D,), 0.2, 1.25, (), jnp.float32),
        "second_gain": jnp.clip(1.0 + 0.1 * jax.random.normal(arg_keys[22], (D,), jnp.float32), 0.5, 1.5),
        "second_shift": normal_values(arg_keys[23], (D,), 0.2, 1.25, (), jnp.float32),
        "expand_weight": normal_values(arg_keys[24], (D, FF), D ** -0.5, 0.21875),
        "expand_bias": normal_values(arg_keys[25], (FF,), 0.2, 1.25, (), jnp.float32),
        "reduce_weight": normal_values(arg_keys[26], (FF, D), FF ** -0.5, 0.109375),
        "reduce_bias": normal_values(arg_keys[27], (D,), 0.2, 1.25, (), jnp.float32),
    }


@jax.custom_vjp
def low(v):
    return lax.optimization_barrier(v.astype(jnp.bfloat16)).astype(jnp.float32)

@jax.custom_vjp
def low_back(v):
    return v

def low_keep(v):
    return (low(v), None)

def low_pass(kept, grad):
    return (grad,)

def back_keep(v):
    return (v, None)

def back_low(kept, grad):
    return (low(grad),)
low.defvjp(low_keep, low_pass)
low_back.defvjp(back_keep, back_low)
EPSILON = 1e-05
HIGHEST = lax.Precision.HIGHEST

def tables(length):
    size = 2 * length
    freqs = jnp.arange(length + 1, dtype=jnp.int32)
    places = jnp.arange(length, dtype=jnp.int32)
    turns = freqs[:, None] * places[None, :] % size
    angle = turns.astype(jnp.float32) * (2.0 * math.pi / size)
    cosine = jnp.cos(angle)
    sine = jnp.sin(angle[1:length])
    forward = jnp.concatenate([cosine, sine], axis=0).astype(jnp.bfloat16)
    weights = jnp.where((freqs == 0) | (freqs == length), 1.0, 2.0).astype(jnp.float32)
    inverse = jnp.concatenate([cosine * weights[:, None], 2.0 * sine], axis=0).T.astype(jnp.bfloat16)
    return (forward, inverse)

def pad_sine(part):
    zeros = jnp.zeros_like(part[..., :1, :])
    return jnp.concatenate([zeros, part, zeros], axis=-2)

def spectral_product(first, second, length):
    real_one = first[..., :length + 1, :]
    imag_one = pad_sine(first[..., length + 1:, :])
    real_two = second[..., :length + 1, :]
    imag_two = pad_sine(second[..., length + 1:, :])
    real = real_one * real_two - imag_one * imag_two
    imag = real_one * imag_two + imag_one * real_two
    return jnp.concatenate([real, imag[..., 1:length, :]], axis=-2)

def filter_values(places, length, params):
    embed_weight, embed_bias, embed_omega, inner_weight, inner_bias, inner_omega, outer_weight, outer_bias, outer_omega, filter_weight = params
    bands_count = (embed_weight.shape[0] - 1) // 2
    tnorm = places.astype(jnp.float32) / (length - 1)
    wave = places.astype(jnp.float32) * (2.0 * math.pi / length)
    bands = jnp.linspace(0.0001, bands_count - 1, bands_count).astype(jnp.float32)
    phase = wave[:, None] * bands[None, :]
    embedded = jnp.concatenate([tnorm[:, None], jnp.cos(phase), -jnp.sin(phase)], axis=1)
    state = jnp.sin(embed_omega * (jnp.dot(embedded, embed_weight, precision=HIGHEST) + embed_bias))
    state = jnp.sin(inner_omega * (jnp.dot(state, inner_weight, precision=HIGHEST) + inner_bias))
    state = jnp.sin(outer_omega * (jnp.dot(state, outer_weight, precision=HIGHEST) + outer_bias))
    width = filter_weight.shape[1]
    rates = jnp.abs(jnp.linspace(math.log(0.01) / 1.5, math.log(0.01) / 0.3, width)).astype(jnp.float32)
    window = jnp.exp(-tnorm[:, None] * rates[None, :])
    return jnp.dot(state, filter_weight, precision=HIGHEST) * window

def layer_norm(value, gain, shift):
    mean = lax.optimization_barrier(jnp.mean(value, axis=-1, keepdims=True))
    centered = value - mean
    variance = lax.optimization_barrier(jnp.mean(centered * centered, axis=-1, keepdims=True))
    return centered * lax.rsqrt(variance + EPSILON) * gain + shift

def lag_masks(segment_rows):
    columns = [jnp.ones(segment_rows.shape, jnp.float32)]
    for delay in (1, 2):
        earlier = jnp.pad(segment_rows, ((0, 0), (delay, 0)), constant_values=-1)[:, :-delay]
        columns.append((earlier == segment_rows).astype(jnp.float32))
    return jnp.stack(columns, axis=-1)

def short_conv(proj, same, short_weight, short_bias):
    result = short_bias + short_weight[0] * proj
    for delay in (1, 2):
        moved = jnp.pad(proj, ((0, 0), (delay, 0), (0, 0)))[:, :-delay, :]
        result = result + short_weight[delay] * moved * same[:, :, delay:delay + 1]
    return result

def block_forward(params, inputs, segment_rows, forward, inverse):
    first_gain, first_shift, mixer_weight, mixer_bias, short_weight, short_bias, embed_weight, embed_bias, embed_omega, inner_weight, inner_bias, inner_omega, outer_weight, outer_bias, outer_omega, filter_weight, skip_gain, output_weight, output_bias, second_gain, second_shift, expand_weight, expand_bias, reduce_weight, reduce_bias = params
    length = inputs.shape[1]
    width = inputs.shape[2]
    size = 2 * length
    forward_wide = forward.astype(jnp.float32)
    inverse_wide = inverse.astype(jnp.float32)
    places = jnp.arange(length, dtype=jnp.int32)
    kernel = low(filter_values(places, length, (embed_weight, embed_bias, embed_omega, inner_weight, inner_bias, inner_omega, outer_weight, outer_bias, outer_omega, filter_weight)))
    spectrum = low_back(jnp.dot(forward_wide, kernel, precision=HIGHEST))
    normed = low(layer_norm(inputs, first_gain, first_shift))
    proj = low_back(jnp.einsum('rld,de->rle', normed, mixer_weight, precision=HIGHEST) + mixer_bias)
    mixed = short_conv(proj, lag_masks(segment_rows), short_weight, short_bias)
    gate_out = mixed[..., :width]
    gate_in = mixed[..., width:2 * width]
    value = mixed[..., 2 * width:]
    inner = value * gate_in
    inner_low = low(inner)
    conv = jnp.zeros_like(inner)
    for document in range(DOCS):
        member = (segment_rows == document).astype(jnp.float32)[..., None]
        trans = low_back(jnp.einsum('ml,rld->rmd', forward_wide, inner_low * member, precision=HIGHEST))
        product = low(spectral_product(trans, spectrum, length))
        conv = conv + member * jnp.einsum('lm,rmd->rld', inverse_wide, product, precision=HIGHEST)
    conv = low_back(conv / size)
    longconv = conv + skip_gain * inner
    mixer = low(gate_out * longconv)
    attn = low_back(jnp.einsum('rle,ed->rld', mixer, output_weight, precision=HIGHEST) + output_bias)
    hidden = inputs + attn
    normed2 = low(layer_norm(hidden, second_gain, second_shift))
    expand = low_back(jnp.einsum('rld,df->rlf', normed2, expand_weight, precision=HIGHEST) + expand_bias)
    active = low(jax.nn.gelu(expand, approximate=False))
    reduced = low_back(jnp.einsum('rlf,fd->rld', active, reduce_weight, precision=HIGHEST) + reduce_bias)
    return hidden + reduced

def reference(tokens, segments, cotangent, first_gain, first_shift, mixer_weight, mixer_bias, short_weight, short_bias, embed_weight, embed_bias, embed_omega, inner_weight, inner_bias, inner_omega, outer_weight, outer_bias, outer_omega, filter_weight, skip_gain, output_weight, output_bias, second_gain, second_shift, expand_weight, expand_bias, reduce_weight, reduce_bias):
    params = tuple((item.astype(jnp.float32) for item in (first_gain, first_shift, mixer_weight, mixer_bias, short_weight, short_bias, embed_weight, embed_bias, embed_omega, inner_weight, inner_bias, inner_omega, outer_weight, outer_bias, outer_omega, filter_weight, skip_gain, output_weight, output_bias, second_gain, second_shift, expand_weight, expand_bias, reduce_weight, reduce_bias)))
    forward, inverse = tables(SEQ)
    groups = N_ROWS * N_POS
    token_groups = tokens.reshape(groups, ROW_DEV, SEQ, D)
    segment_groups = segments.reshape(groups, ROW_DEV, SEQ)
    upstream_groups = cotangent.reshape(groups, ROW_DEV, SEQ, D)

    def one_group(totals, group):
        inputs, segment_rows, upstream = group

        def run(prm, values):
            return block_forward(prm, values, segment_rows, forward, inverse)
        result, pull = jax.vjp(run, params, inputs.astype(jnp.float32))
        param_grads, input_grad = pull(upstream.astype(jnp.float32))
        totals = jax.tree.map(lambda left, right: left + right, totals, param_grads)
        return (totals, (result.astype(jnp.bfloat16), input_grad.astype(jnp.bfloat16)))
    zeros = jax.tree.map(jnp.zeros_like, params)
    totals, (outputs, input_grads) = lax.scan(one_group, zeros, (token_groups, segment_groups, upstream_groups))
    return (outputs.reshape(BATCH, SEQ, D), input_grads.reshape(BATCH, SEQ, D), totals[0], totals[1], totals[2], totals[3], totals[4], totals[5], totals[6], totals[7], totals[8], totals[9], totals[10], totals[11], totals[12], totals[13], totals[14], totals[15], totals[16], totals[17], totals[18], totals[19], totals[20], totals[21], totals[22], totals[23], totals[24])
```

```python
import functools
import math

import jax
import jax.numpy as jnp
import numpy as np
from jax import lax
from jax.experimental import pallas as pl
from jax.experimental.pallas import tpu as pltpu
from jax.sharding import PartitionSpec as P

f32 = jnp.float32
bf = jnp.bfloat16
HI = lax.Precision.HIGHEST
DOCS = 2
EPSILON = 1e-5
ROOT3 = math.sqrt(3.0) / 2
LANES = 128


def nt(a,b,precision=None): return lax.dot_general(a,b,(((1,),(1,)),((),())),precision=precision,preferred_element_type=f32)
def nn(a,b,precision=None): return lax.dot_general(a,b,(((1,),(0,)),((),())),precision=precision,preferred_element_type=f32)
def tn(a,b,precision=None): return lax.dot_general(a,b,(((0,),(0,)),((),())),precision=precision,preferred_element_type=f32)
def norm_stats(x):
    mean=jnp.mean(x,axis=-1,keepdims=True)
    c=x-mean
    var=jnp.mean(c*c,axis=-1,keepdims=True)
    rs=lax.rsqrt(var+EPSILON)
    return c*rs, rs
def sum0(v): return jnp.sum(v,axis=0,keepdims=True)

def radix_tables(length):
    n=length//3; m=2*length
    place=np.arange(n)
    def angle(freqs): return 2*np.pi*((freqs[:,None]*place[None,:])%m)/m
    half=angle(6*np.arange(n//2))
    sine=np.sin(half); sine[0]=np.cos(np.pi*place)
    t0=np.concatenate([np.cos(half),sine],0)
    odd=angle(6*np.arange(n//2)+3)
    t3=np.concatenate([np.cos(odd),np.sin(odd)],0)
    both=[]
    for k in (1,2):
        a=angle(6*np.arange(n)+k)
        c,s=np.cos(a),np.sin(a)
        both.append(np.block([[c,-s],[s,c]]))
    ts=[t0,t3,both[0],both[1]]
    low=lambda v: jnp.asarray(v.astype(np.float32)).astype(bf)
    return [low(t) for t in ts],[low(t.T) for t in ts]

def filter_inputs(length,emb,width):
    bands_count=(emb-1)//2
    places=np.arange(length,dtype=np.float32)
    tn_=places/np.float32(length-1)
    wave=places*np.float32(2.0*math.pi/length)
    bands=np.linspace(0.0001,bands_count-1,bands_count).astype(np.float32)
    phase=(wave[:,None]*bands[None,:]).astype(np.float32)
    z=np.concatenate([tn_[:,None],np.cos(phase),-np.sin(phase)],1).astype(np.float32)
    pad=(-emb)%8
    zt=np.concatenate([z.T,np.zeros((pad,length),np.float32)],0)
    rates=np.abs(np.linspace(math.log(0.01)/1.5,math.log(0.01)/0.3,width)).astype(np.float32)[None,:]
    return jnp.asarray(zt),jnp.asarray(rates)

def sin_cos(x):
    k=jnp.floor(x*(1.0/math.pi)+0.5)
    r=x-k*3.140625
    r=r-k*0.0009670257568359375
    r=r-k*6.2771141529083251953e-07
    odd=k-2.0*jnp.floor(k*0.5)
    sign=1.0-2.0*odd
    q=r*r
    s=1.0+q*(-1/6+q*(1/120+q*(-1/5040+q*(1/362880+q*(-1/39916800+q*(1/6227020800))))))
    c=1.0+q*(-1/2+q*(1/24+q*(-1/720+q*(1/40320+q*(-1/3628800+q*(1/479001600-q*(1/87178291200)))))))
    return r*s*sign, c*sign

def column(row):
    n=row.shape[1]
    i=lax.broadcasted_iota(jnp.int32,(n,n),0); j=lax.broadcasted_iota(jnp.int32,(n,n),1)
    return jnp.sum(jnp.where(i==j,row,0.0),axis=1,keepdims=True)

def spread(x0,x1,x2):
    s=x1+x2; d=x1-x2
    y0=(x0+s).astype(bf); y3=(x0-d).astype(bf)
    y1=jnp.concatenate([(x0+0.5*d).astype(bf),(ROOT3*s).astype(bf)],0)
    y2=jnp.concatenate([(x0-0.5*s).astype(bf),(ROOT3*d).astype(bf)],0)
    return y0,y3,y1,y2
def gather(v0,v3,v1,v2):
    n=v0.shape[0]
    v1r,v1i,v2r,v2i=v1[:n],v1[n:],v2[:n],v2[n:]
    even=v0+v3
    a=0.5*(v1r-v2r); b=ROOT3*(v1i+v2i)
    x0=even+v1r+v2r
    x1=(v0-v3)+a+b
    x2=even-0.5*(v1r+v2r)+ROOT3*(v1i-v2i)
    return x0,x1,x2

def fwd_kernel(rows_here,tok_ref,mask_ref,g1_ref,s1_ref,wg_ref,wi_ref,wv_ref,bg_ref,bi_ref,bv_ref,
        swg_ref,swi_ref,swv_ref,sbg_ref,sbi_ref,sbv_ref,skip_ref,
        zt_ref,ew_ref,eb_ref,eo_ref,iw_ref,ib_ref,io_ref,ow_ref,ob_ref,oo_ref,fw_ref,rate_ref,
        t0,t3,t1,t2,u0,u3,u1,u2,
        proj_ref,mixed_ref,long_ref,mix_ref,trans_ref,spec_ref,state_ref,nt_ref,
        n_s,e_s):
    c=pl.program_id(0)
    L=tok_ref.shape[0]//rows_here
    N=L//3
    @pl.when(c==0)
    def _():
        TT=256
        def body(i,k):
            rows=pl.ds(pl.multiple_of(i*TT,TT),TT)
            xh,_=norm_stats(tok_ref[rows,:].astype(f32))
            n_s[rows,:]=(xh*g1_ref[...]+s1_ref[...]).astype(bf)
            return k
        lax.fori_loop(0,tok_ref.shape[0]//TT,body,0)
        for i in range(tok_ref.shape[0]//TT):
            nt_ref[:,i*TT:(i+1)*TT]=n_s[i*TT:(i+1)*TT,:].T
        e_s[...]=jnp.zeros_like(e_s)
        e_s[0:ew_ref.shape[0],:]=ew_ref[...]
        pre=tn(e_s[...],zt_ref[...],HI)+column(eb_ref[...])
        e1,c1=sin_cos(column(eo_ref[...])*pre)
        state_ref[0]=e1; state_ref[1]=c1; state_ref[2]=pre
        pre=tn(iw_ref[...],e1,HI)+column(ib_ref[...])
        e2,c2=sin_cos(column(io_ref[...])*pre)
        state_ref[3]=e2; state_ref[4]=c2; state_ref[5]=pre
        pre=tn(ow_ref[...],e2,HI)+column(ob_ref[...])
        e3,c3=sin_cos(column(oo_ref[...])*pre)
        state_ref[6]=e3; state_ref[7]=c3; state_ref[8]=pre
    tnorm=lax.broadcasted_iota(jnp.int32,(L,fw_ref.shape[1]),0).astype(f32)*(1.0/(L-1))
    kern=tn(state_ref[6],fw_ref[...],HI)*jnp.exp(-tnorm*rate_ref[...])
    k=kern.astype(bf).astype(f32)
    y0,y3,y1,y2=spread(k[0:N],k[N:2*N],k[2*N:])
    first=lax.broadcasted_iota(jnp.int32,(N//2,fw_ref.shape[1]),0)==0
    half=jnp.where(first,0.5,1.0)
    q0=nn(t0[...],y0); q3=nn(t3[...],y3); q1=nn(t1[...],y1); q2=nn(t2[...],y2)
    H=N//2
    spec_ref[0:H]=q0[0:H]*half
    spec_ref[H:N]=jnp.where(first,0.0,q0[H:])
    spec_ref[6*N:6*N+H]=jnp.where(first,0.5*q0[H:],q0[0:H])
    spec_ref[N:2*N]=q3
    spec_ref[2*N:4*N]=q1
    spec_ref[4*N:6*N]=q2
    def one_row(r,carry):
        rows=pl.ds(pl.multiple_of(r*L,L),L)
        n=n_s[rows,:]
        m0=mask_ref[rows,0:1]; same1=mask_ref[rows,1:2]; same2=mask_ref[rows,2:3]
        m1=1.0-m0
        mixed=[]
        for i,(w,b,sw,sb) in enumerate(((wg_ref,bg_ref,swg_ref,sbg_ref),(wi_ref,bi_ref,swi_ref,sbi_ref),(wv_ref,bv_ref,swv_ref,sbv_ref))):
            p=nn(n,w[...])+b[...]
            proj_ref[i,rows,:]=p.astype(bf)
            m=sb[...]+sw[0:1,:]*p+sw[1:2,:]*(pltpu.roll(p,1,0)*same1)+sw[2:3,:]*(pltpu.roll(p,2,0)*same2)
            mixed_ref[i,rows,:]=m.astype(bf)
            mixed.append(m)
        inner=mixed[2]*mixed[1]
        low=inner.astype(bf).astype(f32)
        xa=low*m0
        conv=None
        for d,(m,x) in enumerate(((m0,xa),(m1,low-xa))):
            y0,y3,y1,y2=spread(x[0:N],x[N:2*N],x[2*N:])
            parts=[]
            for (t,u,y,off,n2) in ((t0,u0,y0,0,H),(t3,u3,y3,N,H),(t1,u1,y1,2*N,N),(t2,u2,y2,4*N,N)):
                p=nn(t[...],y)
                trans_ref[r,d,off:off+2*n2,:]=p.astype(bf)
                pa=p[:n2]; pb=p[n2:]
                qa=spec_ref[off:off+n2]; qb=spec_ref[off+n2:off+2*n2]
                qc=spec_ref[6*N:6*N+n2] if off==0 else qa
                ra=(pa*qa-pb*qb).astype(bf); rb=(pa*qb+pb*qc).astype(bf)
                parts.append(nn(u[...],jnp.concatenate([ra,rb],0)))
            y=jnp.concatenate(gather(*parts),0)
            conv=m*y if conv is None else conv+m*y
        longconv=conv*(2.0/(2*L))+skip_ref[...]*inner
        long_ref[rows,:]=longconv.astype(bf)
        mix_ref[rows,:]=(mixed[0]*longconv).astype(bf)
        return carry
    lax.fori_loop(0,rows_here,one_row,0)

def forward_mixer(tok,mask,g1,s1,wm,mb,sw,sb,skip,filt,zt,rates,tabs,tabst,rows_here,CH=256):
    T,D=tok.shape; L=T//rows_here; N=L//3; J=D//CH
    ew,eb,eo,iw,ib,io,ow,ob,oo,fw=filt
    full=lambda a: pl.BlockSpec(a.shape,lambda j:(0,)*a.ndim,pipeline_mode=pl.Buffered(1))
    col=lambda r,k: pl.BlockSpec((r,CH),lambda j,k=k:(0,k*J+j))
    sds=jax.ShapeDtypeStruct
    F=ew.shape[1]
    ins=[tok,mask,g1,s1,wm,wm,wm,mb,mb,mb,sw,sw,sw,sb,sb,sb,skip,zt,ew,eb,eo,iw,ib,io,ow,ob,oo,fw,rates]+tabs+tabst
    specs=[full(tok),full(mask),full(g1),full(s1)]+[col(D,k) for k in range(3)]+[col(1,k) for k in range(3)]+[col(3,k) for k in range(3)]+[col(1,k) for k in range(3)]+[col(1,0)]
    specs+=[full(a) for a in (zt,ew,eb,eo,iw,ib,io,ow,ob,oo)]+[col(F,0),col(1,0)]+[full(a) for a in tabs+tabst]
    return pl.pallas_call(functools.partial(fwd_kernel,rows_here),grid=(J,),in_specs=specs,
      out_specs=[pl.BlockSpec((3,T,CH),lambda j:(0,0,j)),pl.BlockSpec((3,T,CH),lambda j:(0,0,j)),col(T,0),col(T,0),
        pl.BlockSpec((rows_here,DOCS,2*L,CH),lambda j:(0,0,0,j)),col(2*L+N//2,0),pl.BlockSpec((9,F,L),lambda j:(0,0,0)),pl.BlockSpec((D,T),lambda j:(0,0))],
      out_shape=[sds((3,T,D),bf),sds((3,T,D),bf),sds((T,D),bf),sds((T,D),bf),sds((rows_here,DOCS,2*L,D),bf),sds((2*L+N//2,D),f32),sds((9,F,L),f32),sds((D,T),bf)],
      scratch_shapes=[pltpu.VMEM((T,D),bf),pltpu.VMEM((zt.shape[0],F),f32)],
      compiler_params=pltpu.CompilerParams(vmem_limit_bytes=62*2**20),
      cost_estimate=pl.CostEstimate(flops=10*T*D*D+T*D*6000,bytes_accessed=40*2**20,transcendentals=L*D),name="mixer_forward")(*ins)

def bwd_kernel(rows_here,dat_ref,tok_ref,mask_ref,g1_ref,wo_ref,long_ref,mixed_ref,proj_ref,trans_ref,spec_ref,nt_ref,
        wg_ref,wi_ref,wv_ref,swg_ref,swi_ref,swv_ref,skip_ref,
        state_ref,zt_ref,iw_ref,ow_ref,eo_ref,io_ref,oo_ref,fw_ref,rate_ref,
        t0,t3,t1,t2,u0,u3,u1,u2,
        tg_ref,wgrad_ref,sg_ref,vec_ref,gew_ref,giw_ref,gow_ref,gfw_ref,gsm_ref,
        dn,de3,dp_s,ds_s):
    c=pl.program_id(0); J=pl.num_programs(0)
    T=tok_ref.shape[0]; L=T//rows_here; N=L//3; H=N//2; CH=long_ref.shape[1]
    @pl.when(c==0)
    def _():
        dn[...]=jnp.zeros_like(dn); de3[...]=jnp.zeros_like(de3)
    ds_s[...]=jnp.zeros_like(ds_s); sg_ref[...]=jnp.zeros_like(sg_ref)
    def add(off,v): ds_s[off:off+v.shape[0],:]+=v
    def one_row(r,carry):
        rows=pl.ds(pl.multiple_of(r*L,L),L)
        m0=mask_ref[rows,0:1]; same1=mask_ref[rows,1:2]; same2=mask_ref[rows,2:3]
        m1=1.0-m0
        dm=nt(dat_ref[rows,:],wo_ref[...])
        gate_out=mixed_ref[0,rows,:].astype(f32); gate_in=mixed_ref[1,rows,:].astype(f32); value=mixed_ref[2,rows,:].astype(f32)
        d_go=dm*long_ref[rows,:].astype(f32)
        d_long=dm*gate_out
        sg_ref[0,5:6,:]+=sum0(d_long*(value*gate_in))
        xa=d_long*m0
        d_conv=None
        for d,(m,x) in enumerate(((m0,xa),(m1,d_long-xa))):
            y0,y3,y1,y2=spread(x[0:N],x[N:2*N],x[2*N:])
            parts=[]
            for s,(t,u,y,off,n2) in enumerate(((t0,u0,y0,0,H),(t3,u3,y3,N,H),(t1,u1,y1,2*N,N),(t2,u2,y2,4*N,N))):
                g=nn(t[...],y)
                ga=g[:n2]; gb=g[n2:]
                qa=spec_ref[off:off+n2]; qb=spec_ref[off+n2:off+2*n2]
                qc=spec_ref[6*N:6*N+n2] if off==0 else qa
                pa=trans_ref[r,d,off:off+n2,:].astype(f32); pb=trans_ref[r,d,off+n2:off+2*n2,:].astype(f32)
                da=(ga*qa+gb*qb).astype(bf); db=(gb*qc-ga*qb).astype(bf)
                if s==0:
                    add(0,ga*pa); add(6*N,gb*pb)
                else:
                    add(off,ga*pa+gb*pb)
                add(off+n2,gb*pa-ga*pb)
                parts.append(nn(u[...],jnp.concatenate([da,db],0)))
            y=jnp.concatenate(gather(*parts),0)
            d_conv=m*y if d_conv is None else d_conv+m*y
        d_inner=skip_ref[...]*d_long+d_conv*(2.0/(2*L))
        for i,(dmx,w,sw) in enumerate(((d_go,wg_ref,swg_ref),(d_inner*value,wi_ref,swi_ref),(d_inner*gate_in,wv_ref,swv_ref))):
            a1=pltpu.roll(dmx*same1,L-1,0); a2=pltpu.roll(dmx*same2,L-2,0)
            dp=(sw[0:1,:]*dmx+sw[1:2,:]*a1+sw[2:3,:]*a2).astype(bf)
            p=proj_ref[i,rows,:].astype(f32)
            for k,v in enumerate((p*dmx,p*a1,p*a2,dmx,dp.astype(f32))):
                sg_ref[i,k:k+1,:]+=sum0(v)
            dp_s[i,rows,:]=dp
            dn[rows,:]+=nt(dp,w[...])
        return carry
    lax.fori_loop(0,rows_here,one_row,0)
    for i in range(3):
        part=nn(nt_ref[...],dp_s[i]).astype(bf)
        for h in range(CH//LANES): wgrad_ref[i,h]=part[:,h*LANES:(h+1)*LANES]
    first=lax.broadcasted_iota(jnp.int32,(H,CH),0)==0
    half=jnp.where(first,0.5,1.0)
    d8=ds_s[6*N:6*N+H]
    z0=half*(ds_s[0:H]+jnp.where(first,0.0,d8))
    z1=jnp.where(first,0.5*d8,ds_s[H:N])
    scale=2.0/(2*L)
    low=lambda a: (a*scale).astype(bf)
    parts=[nn(u0[...],low(jnp.concatenate([z0,z1],0))),nn(u3[...],low(ds_s[N:2*N])),nn(u1[...],low(ds_s[2*N:4*N])),nn(u2[...],low(ds_s[4*N:6*N]))]
    tnorm=lax.broadcasted_iota(jnp.int32,(L,CH),0).astype(f32)*(1.0/(L-1))
    gk=jnp.concatenate(gather(*parts),0)*jnp.exp(-tnorm*rate_ref[...])
    gfw_ref[...]=nn(state_ref[6],gk,HI)
    de3[...]+=nt(fw_ref[...],gk,HI)
    @pl.when(c==J-1)
    def _():
        TT=256
        def body(i,k):
            rows=pl.ds(pl.multiple_of(i*TT,TT),TT)
            xh,rs=norm_stats(tok_ref[rows,:].astype(f32))
            d=dn[rows,:]
            gd=d*g1_ref[...]
            a=jnp.mean(gd,axis=-1,keepdims=True); b=jnp.mean(gd*xh,axis=-1,keepdims=True)
            tg_ref[rows,:]=(dat_ref[rows,:].astype(f32)+rs*(gd-a-xh*b)).astype(bf)
            return (k[0]+sum0(d*xh),k[1]+sum0(d))
        z=jnp.zeros((1,tok_ref.shape[1]),f32)
        a,b=lax.fori_loop(0,T//TT,body,(z,z))
        vec_ref[pl.ds(0,1),:]=a; vec_ref[pl.ds(1,1),:]=b
        ones=jnp.ones((8,L),f32)
        flat=lambda v: nt(ones,v,HI)
        g=de3[...]*state_ref[7]
        gsm_ref[0]=flat(g*state_ref[8])
        g=g*column(oo_ref[...])
        gsm_ref[1]=flat(g)
        gow_ref[...]=nt(state_ref[3],g,HI)
        g=nn(ow_ref[...],g,HI)*state_ref[4]
        gsm_ref[2]=flat(g*state_ref[5])
        g=g*column(io_ref[...])
        gsm_ref[3]=flat(g)
        giw_ref[...]=nt(state_ref[0],g,HI)
        g=nn(iw_ref[...],g,HI)*state_ref[1]
        gsm_ref[4]=flat(g*state_ref[2])
        g=g*column(eo_ref[...])
        gsm_ref[5]=flat(g)
        gew_ref[...]=nt(zt_ref[...],g,HI)

def backward_mixer(dat,tok,mask,g1,wo,longc,mixed,proj,trans,spec,ntr,wm,sw,skip,state,filt,zt,rates,tabs,tabst,rows_here,CH=256):
    T,D=tok.shape; L=T//rows_here; N=L//3; J=D//CH
    ew,eb,eo,iw,ib,io,ow,ob,oo,fw=filt
    F=ew.shape[1]; sds=jax.ShapeDtypeStruct
    full=lambda a: pl.BlockSpec(a.shape,lambda j:(0,)*a.ndim,pipeline_mode=pl.Buffered(1))
    col=lambda r,k: pl.BlockSpec((r,CH),lambda j,k=k:(0,k*J+j))
    cube=lambda a: pl.BlockSpec(a.shape[:-1]+(CH,),lambda j:(0,)*(a.ndim-1)+(j,))
    one=lambda *s: pl.BlockSpec(s,lambda j:(0,)*len(s))
    ins=[dat,tok,mask,g1,wo,longc,mixed,proj,trans,spec,ntr,wm,wm,wm,sw,sw,sw,skip,state,zt,iw,ow,eo,io,oo,fw,rates]+tabs+tabst
    specs=[full(dat),full(tok),full(mask),full(g1),pl.BlockSpec((CH,D),lambda j:(j,0)),col(T,0),cube(mixed),cube(proj),cube(trans),cube(spec),full(ntr)]
    specs+=[col(D,k) for k in range(3)]+[col(3,k) for k in range(3)]+[col(1,0)]
    specs+=[full(a) for a in (state,zt,iw,ow,eo,io,oo)]+[col(F,0),col(1,0)]+[full(a) for a in tabs+tabst]
    return pl.pallas_call(functools.partial(bwd_kernel,rows_here),grid=(J,),in_specs=specs,
      out_specs=[one(T,D),pl.BlockSpec((3,CH//LANES,D,LANES),lambda j:(0,j,0,0)),pl.BlockSpec((3,8,CH),lambda j:(0,0,j)),one(8,D),one(zt.shape[0],F),one(F,F),one(F,F),col(F,0),one(6,8,F)],
      out_shape=[sds((T,D),bf),sds((3,D//LANES,D,LANES),bf),sds((3,8,D),f32),sds((8,D),f32),sds((zt.shape[0],F),f32),sds((F,F),f32),sds((F,F),f32),sds((F,D),f32),sds((6,8,F),f32)],
      scratch_shapes=[pltpu.VMEM((T,D),f32),pltpu.VMEM((F,L),f32),pltpu.VMEM((3,T,CH),bf),pltpu.VMEM((6*N+N//2,CH),f32)],
      compiler_params=pltpu.CompilerParams(vmem_limit_bytes=62*2**20),
      cost_estimate=pl.CostEstimate(flops=16*T*D*D+T*D*7000,bytes_accessed=50*2**20,transcendentals=L*D),name="mixer_backward")(*ins)


def gelu_parts(e):
    u=jnp.abs(e)
    d=1.0+(0.3275911/math.sqrt(2))*u
    t=pl.reciprocal(d,approx=True)
    t=t*(2.0-d*t)
    ex=jnp.exp(e*e*(-0.5))
    poly=t*(0.5*0.254829592+t*(0.5*-0.284496736+t*(0.5*1.421413741+t*(0.5*-1.453152027+t*(0.5*1.061405429)))))
    q=poly*ex
    phi=jnp.where(e>=0,1.0-q,q)
    return phi, phi+e*ex*(1/math.sqrt(2*math.pi))
def mlp_kernel(FC,TT,mix_ref,tok_ref,cot_ref,wo_ref,bo_ref,g2_ref,s2_ref,we_ref,be_ref,wr_ref,br_ref,
           out_ref,dat_ref,wog_ref,weg_ref,wrg_ref,beg_ref,vec_ref,
           hid,acc,dn2,n2,n2t,cott,act,de):
    j=pl.program_id(0); J=pl.num_programs(0)
    T=tok_ref.shape[0]; D=tok_ref.shape[1]
    nt_tiles=T//TT
    @pl.when(j==0)
    def _():
        def body(i,c):
            rows=pl.ds(pl.multiple_of(i*TT,TT),TT)
            h=tok_ref[rows,:].astype(f32)+nn(mix_ref[rows,:],wo_ref[...])+bo_ref[...]
            hid[rows,:]=h
            xh,rs=norm_stats(h)
            n=(xh*g2_ref[...]+s2_ref[...]).astype(bf)
            n2[rows,:]=n
            acc[rows,:]=h+br_ref[...]
            dn2[rows,:]=jnp.zeros((TT,D),f32)
            return c
        lax.fori_loop(0,nt_tiles,body,0)
        for i in range(nt_tiles):
            rows=pl.ds(i*TT,TT)
            n2t[:,rows]=n2[rows,:].T
            cott[:,rows]=cot_ref[rows,:].T
    def tile(i,c):
        rows=pl.ds(pl.multiple_of(i*TT,TT),TT)
        e=nn(n2[rows,:],we_ref[...])+be_ref[...]
        da=nt(cot_ref[rows,:],wr_ref[...])
        phi,dphi=gelu_parts(e)
        a=(e*phi).astype(bf)
        dd=(da*dphi).astype(bf)
        act[rows,:]=a
        de[rows,:]=dd
        acc[rows,:]+=nn(a,wr_ref[...])
        dn2[rows,:]+=nt(dd,we_ref[...])
        return c+jnp.sum(dd.astype(f32),axis=0,keepdims=True)
    beg_ref[...]=lax.fori_loop(0,nt_tiles,tile,jnp.zeros((1,FC),f32))
    def grads(i,c):
        rows=pl.ds(pl.multiple_of(i*256,256),256)
        back=nn(cott[rows,:],act[...]).astype(bf).T
        for h in range(256//LANES): wrg_ref[i*(256//LANES)+h]=back[:,h*LANES:(h+1)*LANES]
        ahead=nn(n2t[rows,:],de[...]).astype(bf)
        for h in range(FC//LANES): weg_ref[h,rows,:]=ahead[:,h*LANES:(h+1)*LANES]
        return c
    lax.fori_loop(0,D//256,grads,0)
    @pl.when(j==J-1)
    def _():
        def body(i,c):
            rows=pl.ds(pl.multiple_of(i*TT,TT),TT)
            out_ref[rows,:]=acc[rows,:].astype(bf)
            xh,rs=norm_stats(hid[rows,:])
            dn=dn2[rows,:]
            gd=dn*g2_ref[...]
            m1=jnp.mean(gd,axis=-1,keepdims=True)
            m2=jnp.mean(gd*xh,axis=-1,keepdims=True)
            cot=cot_ref[rows,:].astype(f32)
            dh=cot+rs*(gd-m1-xh*m2)
            dl=dh.astype(bf)
            dat_ref[rows,:]=dl
            dlf=dl.astype(f32)
            s=lambda v: jnp.sum(v,axis=0,keepdims=True)
            return (c[0]+s(dn*xh),c[1]+s(dn),c[2]+s(dlf),c[3]+s(cot))
        z=jnp.zeros((1,D),f32)
        r=lax.fori_loop(0,nt_tiles,body,(z,z,z,z))
        for k in range(4): vec_ref[pl.ds(k,1),:]=r[k]
        for i in range(nt_tiles):
            rows=pl.ds(i*TT,TT)
            n2t[:,rows]=mix_ref[rows,:].T
        def og(i,c):
            rows=pl.ds(pl.multiple_of(i*256,256),256)
            part=nn(n2t[rows,:],dat_ref[...]).astype(bf)
            for h in range(D//LANES): wog_ref[h,rows,:]=part[:,h*LANES:(h+1)*LANES]
            return c
        lax.fori_loop(0,D//256,og,0)
def mlp(mix,tok,cot,wo,bo,g2,s2,we,be,wr,br,FC=1024,TT=512):
    T,D=tok.shape; FF=we.shape[1]; J=FF//FC
    full=lambda a: pl.BlockSpec(a.shape,lambda j:(0,0),pipeline_mode=pl.Buffered(1))
    one=lambda r,c: pl.BlockSpec((r,c),lambda j:(0,0))
    return pl.pallas_call(functools.partial(mlp_kernel,FC,TT),grid=(J,),
      in_specs=[full(mix),full(tok),full(cot),full(wo),full(bo),full(g2),full(s2),
        pl.BlockSpec((D,FC),lambda j:(0,j)),pl.BlockSpec((1,FC),lambda j:(0,j)),pl.BlockSpec((FC,D),lambda j:(j,0)),full(br)],
      out_specs=[one(T,D),one(T,D),pl.BlockSpec((D//LANES,D,LANES),lambda j:(0,0,0)),pl.BlockSpec((FC//LANES,D,LANES),lambda j:(j,0,0)),pl.BlockSpec((D//LANES,FC,LANES),lambda j:(0,j,0)),pl.BlockSpec((1,FC),lambda j:(0,j)),one(8,D)],
      out_shape=[jax.ShapeDtypeStruct((T,D),bf),jax.ShapeDtypeStruct((T,D),bf),jax.ShapeDtypeStruct((D//LANES,D,LANES),bf),
        jax.ShapeDtypeStruct((FF//LANES,D,LANES),bf),jax.ShapeDtypeStruct((D//LANES,FF,LANES),bf),jax.ShapeDtypeStruct((1,FF),f32),jax.ShapeDtypeStruct((8,D),f32)],
      scratch_shapes=[pltpu.VMEM((T,D),f32),pltpu.VMEM((T,D),f32),pltpu.VMEM((T,D),f32),pltpu.VMEM((T,D),bf),
        pltpu.VMEM((D,T),bf),pltpu.VMEM((D,T),bf),pltpu.VMEM((T,FC),bf),pltpu.VMEM((T,FC),bf)],
      compiler_params=pltpu.CompilerParams(vmem_limit_bytes=62*2**20),
      cost_estimate=pl.CostEstimate(flops=54*T*D*FF//4,bytes_accessed=40*2**20,transcendentals=T*FF),
      name="mlp")(mix,tok,cot,wo,bo,g2,s2,we,be,wr,br)


ROWS_WIDE = 384


def pack_plan(width, hidden, emb, ff, filt_rows):
    return None


def reduce_kernel(sizes, pieces, *refs):
    count = len(pieces)
    ins = refs[:count]
    out_ref, pk, rbuf, red, gath, ss1, rs1, ss2, rs2 = refs[count:]
    rows_n, pos_n = sizes
    n = rows_n * pos_n
    total = pk.shape[0]
    chunk = total // n
    me = lax.axis_index("rows") * pos_n + lax.axis_index("pos") if pos_n > 1 else lax.axis_index("rows")

    def ident(t):
        if pos_n > 1:
            return {"rows": t // pos_n, "pos": t % pos_n}
        return {"rows": t}

    barrier = pltpu.get_barrier_semaphore()

    def greet(k, carry):
        t = lax.rem(me + k, n)
        pl.semaphore_signal(barrier, inc=1, device_id=ident(t), device_id_type=pl.DeviceIdType.MESH)
        return carry

    lax.fori_loop(1, n, greet, 0)
    pk[...] = jnp.zeros_like(pk)
    for ref, place in zip(ins, pieces):
        place(ref, pk)
    pl.semaphore_wait(barrier, n - 1)

    def part(t):
        return pl.ds(pl.multiple_of(t * chunk, chunk), chunk)

    def scatter(t, src_t, slot):
        return pltpu.make_async_remote_copy(
            src_ref=pk.at[part(src_t), :], dst_ref=rbuf.at[slot], send_sem=ss1.at[src_t],
            recv_sem=rs1.at[slot], device_id=ident(t), device_id_type=pl.DeviceIdType.MESH)

    def send1(k, carry):
        t = lax.rem(me + k, n)
        scatter(t, t, me).start()
        return carry

    lax.fori_loop(1, n, send1, 0)
    rbuf[me] = pk[part(me), :]

    def wait1(k, carry):
        t = lax.rem(me + k, n)
        scatter(t, t, t).wait()
        return carry

    lax.fori_loop(1, n, wait1, 0)
    acc = rbuf[0]
    for s in range(1, n):
        acc = acc + rbuf[s]
    red[...] = acc
    gath[part(me), :] = acc

    def spread_copy(t, slot):
        return pltpu.make_async_remote_copy(
            src_ref=red, dst_ref=gath.at[part(slot), :], send_sem=ss2.at[t],
            recv_sem=rs2.at[slot], device_id=ident(t), device_id_type=pl.DeviceIdType.MESH)

    def send2(k, carry):
        t = lax.rem(me + k, n)
        spread_copy(t, me).start()
        return carry

    lax.fori_loop(1, n, send2, 0)

    def wait2(k, carry):
        t = lax.rem(me + k, n)
        spread_copy(t, t).wait()
        return carry

    lax.fori_loop(1, n, wait2, 0)
    out_ref[...] = gath[...]


def layout_of(width, hidden, emb, ff):
    per = width // ROWS_WIDE
    at = {}
    row = 0
    at["filter"] = row
    row += hidden * per
    at["square"] = row
    row += hidden
    for name, vectors in (("vec1", 2), ("vec2", 4), ("sgrad", 3 * 5), ("skip", 1), ("ebias", ff // width)):
        at[name] = row
        row += vectors * per
    at["small"] = row
    row += 6
    return at, row


def all_reduce_small(sizes, beg, vec2, sgrad, vec1, gew, giw, gow, gfw, gsm):
    width = vec1.shape[1]
    hidden = giw.shape[0]
    per = width // ROWS_WIDE
    at, used = layout_of(width, hidden, gew.shape[0], beg.shape[1])
    n = sizes[0] * sizes[1]
    total = -(-used // (8 * n)) * 8 * n

    def put(pk, row, value):
        for h in range(per):
            pk[row + h:row + h + 1, :] = value[:, h * ROWS_WIDE:(h + 1) * ROWS_WIDE]

    def p_beg(ref, pk):
        for k in range(ref.shape[1] // width):
            put(pk, at["ebias"] + k * per, ref[:, k * width:(k + 1) * width])

    def p_vec2(ref, pk):
        for k in range(4):
            put(pk, at["vec2"] + k * per, ref[k:k + 1, :])

    def p_sg(ref, pk):
        for i in range(3):
            for k in range(5):
                put(pk, at["sgrad"] + (i * 5 + k) * per, ref[i, k:k + 1, :])
        put(pk, at["skip"], ref[0, 5:6, :])

    def p_vec1(ref, pk):
        for k in range(2):
            put(pk, at["vec1"] + k * per, ref[k:k + 1, :])

    def square(lane):
        def place(ref, pk):
            r = min(ref.shape[0], hidden)
            pk[at["square"]:at["square"] + r, lane:lane + hidden] = ref[0:r, :]
        return place

    def p_fw(ref, pk):
        for h in range(per):
            pk[at["filter"] + h * hidden:at["filter"] + (h + 1) * hidden, :] = ref[:, h * ROWS_WIDE:(h + 1) * ROWS_WIDE]

    def p_small(ref, pk):
        for k in range(6):
            pk[at["small"] + k:at["small"] + k + 1, 0:hidden] = ref[k, 0:1, :]

    places = (p_beg, p_vec2, p_sg, p_vec1, square(0), square(128), square(256), p_fw, p_small)
    args = (beg, vec2, sgrad, vec1, gew, giw, gow, gfw, gsm)
    vm = pl.BlockSpec(memory_space=pltpu.VMEM)
    chunk = total // n
    return pl.pallas_call(
        functools.partial(reduce_kernel, sizes, places),
        out_shape=jax.ShapeDtypeStruct((total, ROWS_WIDE), f32),
        in_specs=[vm] * len(args), out_specs=vm,
        scratch_shapes=[pltpu.VMEM((total, ROWS_WIDE), f32), pltpu.VMEM((n, chunk, ROWS_WIDE), f32),
            pltpu.VMEM((chunk, ROWS_WIDE), f32), pltpu.VMEM((total, ROWS_WIDE), f32)]
            + [pltpu.SemaphoreType.DMA((n,))] * 4,
        compiler_params=pltpu.CompilerParams(collective_id=0, has_side_effects=True, vmem_limit_bytes=32 * 2**20),
        name="sum_small")(*args)


def unpack_small(packed, width, hidden, emb, ff):
    per = width // ROWS_WIDE
    at, _ = layout_of(width, hidden, emb, ff)

    def kernel(pk, *outs):
        (fg, fs, mb, sw, sb, ew, eb, eo, iw, ib, io, ow, ob, oo, fw, sk, obias, sg, ss, eb2, rb) = outs

        def get(ref, r, lane, row):
            for h in range(per):
                ref[r:r + 1, lane + h * ROWS_WIDE:lane + (h + 1) * ROWS_WIDE] = pk[row + h:row + h + 1, :]

        get(fg, 0, 0, at["vec1"]); get(fs, 0, 0, at["vec1"] + per)
        for i in range(3):
            base = at["sgrad"] + i * 5 * per
            for k in range(3):
                get(sw, k, i * width, base + k * per)
            get(sb, 0, i * width, base + 3 * per)
            get(mb, 0, i * width, base + 4 * per)
        q = at["square"]
        ew[...] = pk[q:q + emb, 0:hidden]
        iw[...] = pk[q:q + hidden, 128:128 + hidden]
        ow[...] = pk[q:q + hidden, 256:256 + hidden]
        for k, ref in enumerate((oo, ob, io, ib, eo, eb)):
            ref[...] = pk[at["small"] + k:at["small"] + k + 1, 0:hidden]
        for h in range(per):
            fw[:, h * ROWS_WIDE:(h + 1) * ROWS_WIDE] = pk[at["filter"] + h * hidden:at["filter"] + (h + 1) * hidden, :]
        get(sk, 0, 0, at["skip"])
        for k, ref in enumerate((sg, ss, obias, rb)):
            get(ref, 0, 0, at["vec2"] + k * per)
        for k in range(ff // width):
            get(eb2, 0, k * width, at["ebias"] + k * per)

    s = lambda *d: jax.ShapeDtypeStruct(d, f32)
    shapes = [s(1, width), s(1, width), s(1, 3 * width), s(3, 3 * width), s(1, 3 * width), s(emb, hidden), s(1, hidden), s(1, hidden),
        s(hidden, hidden), s(1, hidden), s(1, hidden), s(hidden, hidden), s(1, hidden), s(1, hidden), s(hidden, width),
        s(1, width), s(1, width), s(1, width), s(1, width), s(1, ff), s(1, width)]
    vm = pl.BlockSpec(memory_space=pltpu.VMEM)
    return pl.pallas_call(kernel, out_shape=shapes, in_specs=[vm], out_specs=[vm] * len(shapes), name="unpack_small")(packed)


def bits_of(n):
    return n.bit_length() - 1


def scatter_blocks(grad, rows_n, pos_n, order):
    blocks, height, wide = grad.shape
    if blocks % pos_n:
        flat = grad.transpose(1, 0, 2).reshape(height, blocks * wide)
        wide = blocks * wide // pos_n
        blocks = pos_n
        grad = flat.reshape(height, blocks, wide).transpose(1, 0, 2)
    high = height // rows_n
    rbits, pbits = bits_of(rows_n), bits_of(pos_n)
    acc = grad.reshape((2,) * pbits + (blocks // pos_n,) + (2,) * rbits + (high, wide))
    alive = [("pos", b) for b in reversed(range(pbits))] + [None] + [("rows", b) for b in reversed(range(rbits))]
    stages = [s for s in order(rbits, pbits)]
    for count, (axis, bit) in enumerate(stages):
        dim = alive.index((axis, bit))
        mine = (lax.axis_index(axis) >> bit) & 1
        size = rows_n if axis == "rows" else pos_n
        send = lax.dynamic_index_in_dim(acc, 1 - mine, dim, keepdims=False)
        keep = lax.dynamic_index_in_dim(acc, mine, dim, keepdims=False)
        got = lax.ppermute(send, axis, [(i, i ^ (1 << bit)) for i in range(size)])
        acc = keep.astype(f32) + got.astype(f32)
        if count < len(stages) - 1:
            acc = acc.astype(bf)
        alive.pop(dim)
    acc = acc.astype(f32)
    return acc.transpose(1, 0, 2).reshape(high, -1)


def order_a(rbits, pbits):
    rest = [("rows", b) for b in range(1, rbits)]
    return [("rows", 0)] + [("pos", b) for b in range(pbits)] + rest


def order_b(rbits, pbits):
    rest = [("rows", b) for b in range(2, rbits)]
    return [("rows", 0), ("rows", 1)] + [("pos", b) for b in range(pbits)] + rest


def lag_columns(segments):
    earlier = lambda k: jnp.pad(segments, ((0, 0), (k, 0)), constant_values=-1)[:, :-k] == segments
    first = segments == 0
    stack = jnp.stack([first, earlier(1), earlier(2)] + [first] * 5, axis=-1)
    return stack.astype(f32).reshape(-1, 8)


def on_device(sizes, tokens, segments, cotangent, first_gain, first_shift, mixer_weight, mixer_bias, short_weight, short_bias,
        embed_weight, embed_bias, embed_omega, inner_weight, inner_bias, inner_omega, outer_weight, outer_bias, outer_omega,
        filter_weight, skip_gain, output_weight, output_bias, second_gain, second_shift, expand_weight, expand_bias,
        reduce_weight, reduce_bias):
    rows_n, pos_n = sizes
    rows_here, length, width = tokens.shape
    emb, hidden = embed_weight.shape
    ff = expand_weight.shape[1]
    row = lambda a: a.reshape(1, -1)
    tok = tokens.reshape(-1, width)
    cot = cotangent.reshape(-1, width)
    mask = lag_columns(segments)
    filt = [embed_weight, row(embed_bias), row(embed_omega), inner_weight, row(inner_bias), row(inner_omega), outer_weight,
        row(outer_bias), row(outer_omega), filter_weight]
    tabs, tabst = radix_tables(length)
    zt, rates = filter_inputs(length, emb, width)
    proj, mixed, longc, mix, trans, spec, state, ntr = forward_mixer(
        tok, mask, row(first_gain), row(first_shift), mixer_weight, row(mixer_bias), short_weight, row(short_bias),
        row(skip_gain), filt, zt, rates, tabs, tabst, rows_here)
    out, dat, wog, weg, wrg, beg, vec2 = mlp(
        mix, tok, cot, output_weight, row(output_bias), row(second_gain), row(second_shift), expand_weight,
        row(expand_bias), reduce_weight, row(reduce_bias))
    tgrad, wmg, sgrad, vec1, gew, giw, gow, gfw, gsm = backward_mixer(
        dat, tok, mask, row(first_gain), output_weight, longc, mixed, proj, trans, spec, ntr, mixer_weight, short_weight,
        row(skip_gain), state, filt, zt, rates, tabs, tabst, rows_here)
    group = sizes if rows_n * pos_n <= 32 else (rows_n, 1)
    packed = all_reduce_small(group, beg, vec2, sgrad, vec1, gew, giw, gow, gfw, gsm)
    if group != tuple(sizes):
        packed = lax.psum(packed, "pos")
    (fg, fs, mb, sw, sb, ew, eb, eo, iw, ib, io, ow, ob, oo, fw, sk, obias, sg, ss, eb2, rb) = unpack_small(
        packed, width, hidden, emb, ff)
    flat = lambda a: a.reshape(-1)
    e_grad = scatter_blocks(weg, rows_n, pos_n, order_a)
    r_grad = scatter_blocks(wrg, rows_n, pos_n, order_b)
    o_grad = scatter_blocks(wog, rows_n, pos_n, order_a)
    blocks = wmg.shape[0] * wmg.shape[1]
    m_grad = scatter_blocks(wmg.reshape(blocks, width, -1), rows_n, pos_n, order_b)
    return (out.reshape(tokens.shape), tgrad.reshape(tokens.shape), flat(fg), flat(fs), m_grad, flat(mb), sw, flat(sb), ew,
        flat(eb), flat(eo), iw, flat(ib), flat(io), ow, flat(ob), flat(oo), fw, flat(sk), o_grad, flat(obias), flat(sg),
        flat(ss), e_grad, flat(eb2), r_grad, flat(rb))


def solution(mesh):
    both = ("rows", "pos")
    rows3 = P(both, None, None)
    grid = P("rows", "pos")
    in_specs = (rows3, P(both, None), rows3) + (P(),) * 25
    out_specs = (rows3, rows3, P(), P(), grid) + (P(),) * 14 + (grid, P(), P(), P(), grid, P(), grid, P())
    sizes = (mesh.shape["rows"], mesh.shape["pos"])
    return jax.shard_map(
        functools.partial(on_device, sizes), mesh=mesh, in_specs=in_specs, out_specs=out_specs, check_vma=False)
```

```python
import functools
import math

import jax
import jax.numpy as jnp
import numpy as np
from jax import lax
from jax.experimental import pallas as pl
from jax.experimental.pallas import tpu as pltpu
from jax.sharding import PartitionSpec as P

f32 = jnp.float32
bf = jnp.bfloat16
HI = lax.Precision.HIGHEST
MESH = pl.DeviceIdType.MESH
DOCS = 2
EPSILON = 1e-5
ROOT3 = math.sqrt(3.0) / 2
LANES = 128
CHUNK = 256
PACK = 384
VMEM_BYTES = 62 * 2**20


def nt(a, b, precision=None):
    return lax.dot_general(a, b, (((1,), (1,)), ((), ())), precision=precision, preferred_element_type=f32)


def nn(a, b, precision=None):
    return lax.dot_general(a, b, (((1,), (0,)), ((), ())), precision=precision, preferred_element_type=f32)


def tn(a, b, precision=None):
    return lax.dot_general(a, b, (((0,), (0,)), ((), ())), precision=precision, preferred_element_type=f32)


def norm_stats(x):
    mean = jnp.mean(x, axis=-1, keepdims=True)
    centered = x - mean
    variance = jnp.mean(centered * centered, axis=-1, keepdims=True)
    scale = lax.rsqrt(variance + EPSILON)
    return centered * scale, scale


def sum0(v):
    return jnp.sum(v, axis=0, keepdims=True)


def as_row(ref):
    return ref[...].reshape(1, -1)


def radix_tables(length):
    n = length // 3
    m = 2 * length
    place = np.arange(n)

    def angle(freqs):
        return 2 * np.pi * ((freqs[:, None] * place[None, :]) % m) / m

    even = angle(6 * np.arange(n // 2))
    sine = np.sin(even)
    sine[0] = np.cos(np.pi * place)
    odd = angle(6 * np.arange(n // 2) + 3)
    out = [np.concatenate([np.cos(even), sine], 0), np.concatenate([np.cos(odd), np.sin(odd)], 0)]
    for k in (1, 2):
        turn = angle(6 * np.arange(n) + k)
        c, s = np.cos(turn), np.sin(turn)
        out.append(np.block([[c, -s], [s, c]]))
    low = lambda v: jnp.asarray(v.astype(np.float32)).astype(bf)
    return [low(t) for t in out], [low(t.T) for t in out]


def spread(x0, x1, x2):
    s = x1 + x2
    d = x1 - x2
    y0 = (x0 + s).astype(bf)
    y3 = (x0 - d).astype(bf)
    y1 = jnp.concatenate([(x0 + 0.5 * d).astype(bf), (ROOT3 * s).astype(bf)], 0)
    y2 = jnp.concatenate([(x0 - 0.5 * s).astype(bf), (ROOT3 * d).astype(bf)], 0)
    return y0, y3, y1, y2


def gather(v0, v3, v1, v2):
    n = v0.shape[0]
    v1r, v1i, v2r, v2i = v1[:n], v1[n:], v2[:n], v2[n:]
    even = v0 + v3
    a = 0.5 * (v1r - v2r)
    b = ROOT3 * (v1i + v2i)
    x0 = even + v1r + v2r
    x1 = (v0 - v3) + a + b
    x2 = even - 0.5 * (v1r + v2r) + ROOT3 * (v1i - v2i)
    return x0, x1, x2


def filter_inputs(length, emb, width):
    bands_count = (emb - 1) // 2
    places = np.arange(length, dtype=np.float32)
    tnorm = places / np.float32(length - 1)
    wave = places * np.float32(2.0 * math.pi / length)
    bands = np.linspace(0.0001, bands_count - 1, bands_count).astype(np.float32)
    phase = (wave[:, None] * bands[None, :]).astype(np.float32)
    z = np.concatenate([tnorm[:, None], np.cos(phase), -np.sin(phase)], 1).astype(np.float32)
    zt = np.concatenate([z.T, np.zeros(((-emb) % 8, length), np.float32)], 0)
    rates = np.abs(np.linspace(math.log(0.01) / 1.5, math.log(0.01) / 0.3, width)).astype(np.float32)[None, :]
    return jnp.asarray(zt), jnp.asarray(rates)


def window(length, rate):
    tnorm = lax.broadcasted_iota(jnp.int32, (length, rate.shape[1]), 0).astype(f32) * (1.0 / (length - 1))
    return jnp.exp(-tnorm * rate)


def sin_cos(x):
    k = jnp.floor(x * (1.0 / math.pi) + 0.5)
    r = x - k * 3.140625
    r = r - k * 0.0009670257568359375
    r = r - k * 6.2771141529083251953e-07
    sign = 1.0 - 2.0 * (k - 2.0 * jnp.floor(k * 0.5))
    q = r * r
    s = 1.0 + q * (-1 / 6 + q * (1 / 120 + q * (-1 / 5040 + q * (1 / 362880 + q * (-1 / 39916800 + q * (1 / 6227020800))))))
    c = 1.0 + q * (-1 / 2 + q * (1 / 24 + q * (-1 / 720 + q * (1 / 40320 + q * (-1 / 3628800 + q * (1 / 479001600 - q * (1 / 87178291200)))))))
    return r * s * sign, c * sign


def column(ref):
    v = as_row(ref)
    n = v.shape[1]
    i = lax.broadcasted_iota(jnp.int32, (n, n), 0)
    j = lax.broadcasted_iota(jnp.int32, (n, n), 1)
    return jnp.sum(jnp.where(i == j, v, 0.0), axis=1, keepdims=True)


def token_masks(seg, length, wide):
    edge = jnp.sum((seg == 0).astype(jnp.int32), axis=1, keepdims=True)
    t = lax.broadcasted_iota(jnp.int32, (length, wide), 0)
    one = jnp.logical_and(t != 0, t != edge)
    two = jnp.logical_and(jnp.logical_and(one, t != 1), t != edge + 1)
    return t < edge, one, two


def specs_of(length, n):
    return ((0, 0, n // 2), (1, n, n // 2), (2, 2 * n, n), (3, 4 * n, n))


def forward_kernel(tok_ref, seg_ref, g1_ref, s1_ref, wg_ref, wi_ref, wv_ref, mb_ref, swg_ref, swi_ref, swv_ref, sb_ref,
        skip_ref, zt_ref, ew_ref, eb_ref, eo_ref, iw_ref, ib_ref, io_ref, ow_ref, ob_ref, oo_ref, fw_ref, rate_ref,
        t0, t3, t1, t2, u0, u3, u1, u2,
        proj_ref, mixed_ref, long_ref, mix_ref, trans_ref, spec_ref, state_ref, nt_ref, normed, padded):
    c = pl.program_id(0)
    r = pl.program_id(1)
    length, width = tok_ref.shape
    n = length // 3
    half = n // 2
    wide = fw_ref.shape[1]
    rows = pl.ds(pl.multiple_of(r * length, length), length)
    tables = ((t0, u0), (t3, u3), (t1, u1), (t2, u2))

    @pl.when(c == 0)
    def _():
        step = 256
        for i in range(length // step):
            part = slice(i * step, (i + 1) * step)
            xhat, _ = norm_stats(tok_ref[part, :].astype(f32))
            low = (xhat * as_row(g1_ref) + as_row(s1_ref)).astype(bf)
            normed[pl.ds(pl.multiple_of(r * length + i * step, step), step), :] = low
            nt_ref[:, part] = low.T

    @pl.when(jnp.logical_and(c == 0, r == 0))
    def _():
        padded[...] = jnp.zeros_like(padded)
        padded[0:ew_ref.shape[0], :] = ew_ref[...]
        pre = tn(padded[...], zt_ref[...], HI) + column(eb_ref)
        e1, c1 = sin_cos(column(eo_ref) * pre)
        state_ref[0] = e1
        state_ref[1] = c1
        state_ref[2] = pre
        pre = tn(iw_ref[...], e1, HI) + column(ib_ref)
        e2, c2 = sin_cos(column(io_ref) * pre)
        state_ref[3] = e2
        state_ref[4] = c2
        state_ref[5] = pre
        pre = tn(ow_ref[...], e2, HI) + column(ob_ref)
        e3, c3 = sin_cos(column(oo_ref) * pre)
        state_ref[6] = e3
        state_ref[7] = c3
        state_ref[8] = pre

    @pl.when(r == 0)
    def _():
        kernel = tn(state_ref[6], fw_ref[...], HI) * window(length, rate_ref[...])
        k = kernel.astype(bf).astype(f32)
        y0, y3, y1, y2 = spread(k[0:n], k[n:2 * n], k[2 * n:])
        first = lax.broadcasted_iota(jnp.int32, (half, wide), 0) == 0
        q0 = nn(t0[...], y0)
        spec_ref[0:half] = q0[0:half] * jnp.where(first, 0.5, 1.0)
        spec_ref[half:n] = jnp.where(first, 0.0, q0[half:])
        spec_ref[6 * n:6 * n + half] = jnp.where(first, 0.5 * q0[half:], q0[0:half])
        spec_ref[n:2 * n] = nn(t3[...], y3)
        spec_ref[2 * n:4 * n] = nn(t1[...], y1)
        spec_ref[4 * n:6 * n] = nn(t2[...], y2)

    edge, one, two = token_masks(seg_ref[pl.ds(r, 1), :], length, wide)
    low = normed[rows, :]
    mixed = []
    for i, (w, sw) in enumerate(((wg_ref, swg_ref), (wi_ref, swi_ref), (wv_ref, swv_ref))):
        at = pl.ds(pl.multiple_of(i * width + c * wide, wide), wide)
        p = nn(low, w[...]) + mb_ref[at].reshape(1, wide)
        proj_ref[i] = p.astype(bf)
        m = (sb_ref[at].reshape(1, wide) + sw[0:1, :] * p + sw[1:2, :] * jnp.where(one, pltpu.roll(p, 1, 0), 0.0)
            + sw[2:3, :] * jnp.where(two, pltpu.roll(p, 2, 0), 0.0))
        mixed_ref[i] = m.astype(bf)
        mixed.append(m)
    inner = mixed[2] * mixed[1]
    inner_low = inner.astype(bf).astype(f32)
    conv = None
    for d in range(DOCS):
        x = jnp.where(edge, inner_low, 0.0) if d == 0 else jnp.where(edge, 0.0, inner_low)
        ys = spread(x[0:n], x[n:2 * n], x[2 * n:])
        parts = []
        for s, off, m in specs_of(length, n):
            t, u = tables[s]
            p = nn(t[...], ys[s])
            trans_ref[0, d, off:off + 2 * m, :] = p.astype(bf)
            pa, pb = p[:m], p[m:]
            qa, qb = spec_ref[off:off + m], spec_ref[off + m:off + 2 * m]
            qc = spec_ref[6 * n:6 * n + m] if s == 0 else qa
            prod = jnp.concatenate([(pa * qa - pb * qb).astype(bf), (pa * qb + pb * qc).astype(bf)], 0)
            parts.append(nn(u[...], prod))
        y = jnp.concatenate(gather(*parts), 0)
        conv = y if d == 0 else jnp.where(edge, conv, y)
    longconv = conv * (1.0 / length) + skip_ref[pl.ds(pl.multiple_of(c * wide, wide), wide)].reshape(1, wide) * inner
    long_ref[...] = longconv.astype(bf)
    mix_ref[...] = (mixed[0] * longconv).astype(bf)


def whole_spec(a):
    return pl.BlockSpec(a.shape, lambda *_: (0,) * a.ndim, pipeline_mode=pl.Buffered(1))


def fixed_spec(*shape):
    return pl.BlockSpec(shape, lambda *_: (0,) * len(shape))


def column_spec(rows, k, count):
    return pl.BlockSpec((rows, CHUNK), lambda c, r: (0, k * count + c))


def part_spec(length):
    return pl.BlockSpec((length, CHUNK), lambda c, r: (r, c))


def stack_spec(count, length):
    return pl.BlockSpec((count, length, CHUNK), lambda c, r: (0, r, c))


def vector_chunk():
    return pl.BlockSpec((CHUNK,), lambda c, r: (c,))


def forward_mixer(tok, segments, g1, s1, wm, mb, sw, sb, skip, filt, zt, rates, tabs, tabst):
    rows_here, length = segments.shape
    total, width = tok.shape
    n = length // 3
    count = width // CHUNK
    fw = filt[-1]
    hidden = fw.shape[0]
    sds = jax.ShapeDtypeStruct
    ins = [tok, segments, g1, s1, wm, wm, wm, mb, sw, sw, sw, sb, skip, zt, *filt, rates, *tabs, *tabst]
    specs = [pl.BlockSpec((length, width), lambda c, r: (jnp.where(c == 0, r, rows_here - 1), 0))]
    specs += [whole_spec(a) for a in (segments, g1, s1)]
    specs += [column_spec(width, k, count) for k in range(3)] + [whole_spec(mb)] + [column_spec(3, k, count) for k in range(3)]
    specs += [whole_spec(sb), whole_spec(skip), whole_spec(zt)] + [whole_spec(a) for a in filt[:-1]]
    specs += [column_spec(hidden, 0, count), column_spec(1, 0, count)] + [whole_spec(a) for a in (*tabs, *tabst)]
    return pl.pallas_call(
        forward_kernel, grid=(count, rows_here), in_specs=specs,
        out_specs=[stack_spec(3, length), stack_spec(3, length), part_spec(length), part_spec(length),
            pl.BlockSpec((1, DOCS, 2 * length, CHUNK), lambda c, r: (r, 0, 0, c)), column_spec(2 * length + n // 2, 0, count),
            fixed_spec(9, hidden, length),
            pl.BlockSpec((width, length), lambda c, r: (0, jnp.where(c == 0, r, rows_here - 1)))],
        out_shape=[sds((3, total, width), bf), sds((3, total, width), bf), sds((total, width), bf), sds((total, width), bf),
            sds((rows_here, DOCS, 2 * length, width), bf), sds((2 * length + n // 2, width), f32),
            sds((9, hidden, length), f32), sds((width, total), bf)],
        scratch_shapes=[pltpu.VMEM((total, width), bf), pltpu.VMEM((zt.shape[0], hidden), f32)],
        compiler_params=pltpu.CompilerParams(vmem_limit_bytes=VMEM_BYTES),
        cost_estimate=pl.CostEstimate(
            flops=total * width * (6 * width + 4 * 2 * 5 * n), bytes_accessed=40 * total * width, transcendentals=0),
        name="mixer_forward")(*ins)


def gelu_parts(e):
    d = 1.0 + (0.3275911 / math.sqrt(2)) * jnp.abs(e)
    t = pl.reciprocal(d, approx=True)
    t = t * (2.0 - d * t)
    bell = jnp.exp(e * e * (-0.5))
    poly = t * (0.5 * 0.254829592 + t * (0.5 * -0.284496736 + t * (0.5 * 1.421413741 + t * (0.5 * -1.453152027 + t * (0.5 * 1.061405429)))))
    tail = poly * bell
    phi = jnp.where(e >= 0, 1.0 - tail, tail)
    return phi, phi + e * bell * (1 / math.sqrt(2 * math.pi))


def mlp_kernel(mix_ref, tok_ref, cot_ref, wo_ref, bo_ref, g2_ref, s2_ref, we_ref, be_ref, wr_ref, br_ref,
        out_ref, dat_ref, wog_ref, weg_ref, wrg_ref, beg_ref, vec_ref, hid, acc, dn2, n2, n2t, cott, act, de):
    j = pl.program_id(0)
    total, width = tok_ref.shape
    part_ff = we_ref.shape[1]
    step = 512
    steps = total // step

    def at(i, size=step):
        return pl.ds(pl.multiple_of(i * size, size), size)

    @pl.when(j == 0)
    def _():
        def body(i, carry):
            rows = at(i)
            h = tok_ref[rows, :].astype(f32) + nn(mix_ref[rows, :], wo_ref[...]) + as_row(bo_ref)
            hid[rows, :] = h
            xhat, _ = norm_stats(h)
            n2[rows, :] = (xhat * as_row(g2_ref) + as_row(s2_ref)).astype(bf)
            acc[rows, :] = h + as_row(br_ref)
            dn2[rows, :] = jnp.zeros((step, width), f32)
            return carry

        lax.fori_loop(0, steps, body, 0)
        for i in range(steps):
            rows = slice(i * step, (i + 1) * step)
            n2t[:, rows] = n2[rows, :].T
            cott[:, rows] = cot_ref[rows, :].T

    def tile(i, carry):
        rows = at(i)
        e = nn(n2[rows, :], we_ref[...]) + be_ref[pl.ds(pl.multiple_of(j * part_ff, part_ff), part_ff)].reshape(1, part_ff)
        da = nt(cot_ref[rows, :], wr_ref[...])
        phi, slope = gelu_parts(e)
        a = (e * phi).astype(bf)
        d = (da * slope).astype(bf)
        act[rows, :] = a
        de[rows, :] = d
        acc[rows, :] += nn(a, wr_ref[...])
        dn2[rows, :] += nt(d, we_ref[...])
        return carry + sum0(d.astype(f32))

    beg_ref[...] = lax.fori_loop(0, steps, tile, jnp.zeros((1, part_ff), f32))

    def grads(i, carry):
        rows = at(i, 256)
        back = nn(cott[rows, :], act[...]).astype(bf).T
        for h in range(256 // LANES):
            wrg_ref[i * (256 // LANES) + h] = back[:, h * LANES:(h + 1) * LANES]
        ahead = nn(n2t[rows, :], de[...]).astype(bf)
        for h in range(part_ff // LANES):
            weg_ref[h, rows, :] = ahead[:, h * LANES:(h + 1) * LANES]
        return carry

    lax.fori_loop(0, width // 256, grads, 0)

    @pl.when(j == pl.num_programs(0) - 1)
    def _():
        def body(i, carry):
            rows = at(i)
            out_ref[rows, :] = acc[rows, :].astype(bf)
            xhat, scale = norm_stats(hid[rows, :])
            dn = dn2[rows, :]
            gd = dn * as_row(g2_ref)
            m1 = jnp.mean(gd, axis=-1, keepdims=True)
            m2 = jnp.mean(gd * xhat, axis=-1, keepdims=True)
            cot = cot_ref[rows, :].astype(f32)
            low = (cot + scale * (gd - m1 - xhat * m2)).astype(bf)
            dat_ref[rows, :] = low
            return (carry[0] + sum0(dn * xhat), carry[1] + sum0(dn), carry[2] + sum0(low.astype(f32)), carry[3] + sum0(cot))

        zero = jnp.zeros((1, width), f32)
        sums = lax.fori_loop(0, steps, body, (zero,) * 4)
        for k in range(4):
            vec_ref[k:k + 1, :] = sums[k]
        for i in range(steps):
            rows = slice(i * step, (i + 1) * step)
            n2t[:, rows] = mix_ref[rows, :].T

        def weights(i, carry):
            rows = at(i, 256)
            part = nn(n2t[rows, :], dat_ref[...]).astype(bf)
            for h in range(width // LANES):
                wog_ref[h, rows, :] = part[:, h * LANES:(h + 1) * LANES]
            return carry

        lax.fori_loop(0, width // 256, weights, 0)


def mlp(mix, tok, cot, wo, bo, g2, s2, we, be, wr, br, part_ff=1024):
    total, width = tok.shape
    ff = we.shape[1]
    part_ff = min(part_ff, ff)
    sds = jax.ShapeDtypeStruct
    blocks = width // LANES
    return pl.pallas_call(
        mlp_kernel, grid=(ff // part_ff,),
        in_specs=[whole_spec(a) for a in (mix, tok, cot, wo, bo, g2, s2)]
            + [pl.BlockSpec((width, part_ff), lambda j: (0, j)), whole_spec(be), pl.BlockSpec((part_ff, width), lambda j: (j, 0)),
                whole_spec(br)],
        out_specs=[fixed_spec(total, width), fixed_spec(total, width), fixed_spec(blocks, width, LANES),
            pl.BlockSpec((part_ff // LANES, width, LANES), lambda j: (j, 0, 0)),
            pl.BlockSpec((blocks, part_ff, LANES), lambda j: (0, j, 0)), pl.BlockSpec((1, part_ff), lambda j: (0, j)),
            fixed_spec(8, width)],
        out_shape=[sds((total, width), bf), sds((total, width), bf), sds((blocks, width, LANES), bf),
            sds((ff // LANES, width, LANES), bf), sds((blocks, ff, LANES), bf), sds((1, ff), f32), sds((8, width), f32)],
        scratch_shapes=[pltpu.VMEM((total, width), f32)] * 3 + [pltpu.VMEM((total, width), bf)]
            + [pltpu.VMEM((width, total), bf)] * 2 + [pltpu.VMEM((total, part_ff), bf)] * 2,
        compiler_params=pltpu.CompilerParams(vmem_limit_bytes=VMEM_BYTES),
        cost_estimate=pl.CostEstimate(
            flops=12 * total * width * ff + 4 * total * width * width, bytes_accessed=30 * total * width,
            transcendentals=total * ff),
        name="mlp")(mix, tok, cot, wo, bo, g2, s2, we, be, wr, br)


def backward_kernel(dat_ref, tok_ref, seg_ref, g1_ref, wo_ref, long_ref, mixed_ref, proj_ref, trans_ref, spec_ref, nt_ref,
        wg_ref, wi_ref, wv_ref, swg_ref, swi_ref, swv_ref, skip_ref, state_ref, zt_ref, iw_ref, ow_ref, eo_ref, io_ref,
        oo_ref, fw_ref, rate_ref, t0, t3, t1, t2, u0, u3, u1, u2,
        tg_ref, wgrad_ref, sg_ref, vec_ref, gew_ref, giw_ref, gow_ref, gfw_ref, gsm_ref, dn, de3, dp_s, ds_s):
    c = pl.program_id(0)
    r = pl.program_id(1)
    chunks = pl.num_programs(0)
    last_row = pl.num_programs(1) - 1
    length, wide = long_ref.shape
    n = length // 3
    half = n // 2
    rows = pl.ds(pl.multiple_of(r * length, length), length)
    tables = ((t0, u0), (t3, u3), (t1, u1), (t2, u2))

    @pl.when(r == 0)
    def _():
        ds_s[...] = jnp.zeros_like(ds_s)
        sg_ref[...] = jnp.zeros_like(sg_ref)

    @pl.when(jnp.logical_and(c == 0, r == 0))
    def _():
        dn[...] = jnp.zeros_like(dn)
        de3[...] = jnp.zeros_like(de3)
        vec_ref[...] = jnp.zeros_like(vec_ref)

    def add(off, v):
        ds_s[off:off + v.shape[0], :] += v

    edge, one, two = token_masks(seg_ref[pl.ds(r, 1), :], length, wide)
    dm = nt(dat_ref[rows, :], wo_ref[...])
    gate_out = mixed_ref[0].astype(f32)
    gate_in = mixed_ref[1].astype(f32)
    value = mixed_ref[2].astype(f32)
    d_gate = dm * long_ref[...].astype(f32)
    d_long = dm * gate_out
    sg_ref[0, 5:6, :] += sum0(d_long * (value * gate_in))
    d_conv = None
    for d in range(DOCS):
        x = jnp.where(edge, d_long, 0.0) if d == 0 else jnp.where(edge, 0.0, d_long)
        ys = spread(x[0:n], x[n:2 * n], x[2 * n:])
        parts = []
        for s, off, m in specs_of(length, n):
            t, u = tables[s]
            g = nn(t[...], ys[s])
            ga, gb = g[:m], g[m:]
            qa, qb = spec_ref[off:off + m], spec_ref[off + m:off + 2 * m]
            qc = spec_ref[6 * n:6 * n + m] if s == 0 else qa
            pa, pb = trans_ref[0, d, off:off + m, :].astype(f32), trans_ref[0, d, off + m:off + 2 * m, :].astype(f32)
            back = jnp.concatenate([(ga * qa + gb * qb).astype(bf), (gb * qc - ga * qb).astype(bf)], 0)
            if s == 0:
                add(0, ga * pa)
                add(6 * n, gb * pb)
            else:
                add(off, ga * pa + gb * pb)
            add(off + m, gb * pa - ga * pb)
            parts.append(nn(u[...], back))
        y = jnp.concatenate(gather(*parts), 0)
        d_conv = y if d == 0 else jnp.where(edge, d_conv, y)
    d_inner = skip_ref[pl.ds(pl.multiple_of(c * wide, wide), wide)].reshape(1, wide) * d_long + d_conv * (1.0 / length)
    grads = (d_gate, d_inner * value, d_inner * gate_in)
    for i, (dmx, w, sw) in enumerate(zip(grads, (wg_ref, wi_ref, wv_ref), (swg_ref, swi_ref, swv_ref))):
        a1 = pltpu.roll(jnp.where(one, dmx, 0.0), length - 1, 0)
        a2 = pltpu.roll(jnp.where(two, dmx, 0.0), length - 2, 0)
        dp = (sw[0:1, :] * dmx + sw[1:2, :] * a1 + sw[2:3, :] * a2).astype(bf)
        p = proj_ref[i].astype(f32)
        for k, v in enumerate((p * dmx, p * a1, p * a2, dmx, dp.astype(f32))):
            sg_ref[i, k:k + 1, :] += sum0(v)
        dp_s[i, rows, :] = dp
        dn[rows, :] += nt(dp, w[...])

    @pl.when(r == last_row)
    def _():
        for i in range(3):
            part = nn(nt_ref[...], dp_s[i]).astype(bf)
            for h in range(wide // LANES):
                wgrad_ref[i, h] = part[:, h * LANES:(h + 1) * LANES]
        first = lax.broadcasted_iota(jnp.int32, (half, wide), 0) == 0
        extra = ds_s[6 * n:6 * n + half]
        ds_s[0:half] = jnp.where(first, 0.5, 1.0) * (ds_s[0:half] + jnp.where(first, 0.0, extra))
        ds_s[half:n] = jnp.where(first, 0.5 * extra, ds_s[half:n])
        parts = [nn(tables[s][1][...], (ds_s[off:off + 2 * m] * (1.0 / length)).astype(bf)) for s, off, m in specs_of(length, n)]
        gk = jnp.concatenate(gather(*parts), 0) * window(length, rate_ref[...])
        gfw_ref[...] = nn(state_ref[6], gk, HI)
        de3[...] += nt(fw_ref[...], gk, HI)

    @pl.when(c == chunks - 1)
    def _():
        step = 256
        g1 = as_row(g1_ref)
        for i in range(length // step):
            part = slice(i * step, (i + 1) * step)
            there = pl.ds(pl.multiple_of(r * length + i * step, step), step)
            xhat, scale = norm_stats(tok_ref[part, :].astype(f32))
            d = dn[there, :]
            gd = d * g1
            a = jnp.mean(gd, axis=-1, keepdims=True)
            b = jnp.mean(gd * xhat, axis=-1, keepdims=True)
            tg_ref[part, :] = (dat_ref[there, :].astype(f32) + scale * (gd - a - xhat * b)).astype(bf)
            vec_ref[0:1, :] += sum0(d * xhat)
            vec_ref[1:2, :] += sum0(d)

    @pl.when(jnp.logical_and(c == chunks - 1, r == last_row))
    def _():
        ones = jnp.ones((8, length), f32)
        flat = lambda v: nt(ones, v, HI)
        g = de3[...] * state_ref[7]
        gsm_ref[0] = flat(g * state_ref[8])
        g = g * column(oo_ref)
        gsm_ref[1] = flat(g)
        gow_ref[...] = nt(state_ref[3], g, HI)
        g = nn(ow_ref[...], g, HI) * state_ref[4]
        gsm_ref[2] = flat(g * state_ref[5])
        g = g * column(io_ref)
        gsm_ref[3] = flat(g)
        giw_ref[...] = nt(state_ref[0], g, HI)
        g = nn(iw_ref[...], g, HI) * state_ref[1]
        gsm_ref[4] = flat(g * state_ref[2])
        g = g * column(eo_ref)
        gsm_ref[5] = flat(g)
        gew_ref[...] = nt(zt_ref[...], g, HI)


def backward_mixer(dat, tok, segments, g1, wo, longc, mixed, proj, trans, spec, ntr, wm, sw, skip, state, filt, zt, rates,
        tabs, tabst):
    rows_here, length = segments.shape
    total, width = tok.shape
    n = length // 3
    count = width // CHUNK
    ew, eb, eo, iw, ib, io, ow, ob, oo, fw = filt
    hidden = fw.shape[0]
    sds = jax.ShapeDtypeStruct
    late = lambda c, r: (jnp.where(c == count - 1, r, 0), 0)
    ins = [dat, tok, segments, g1, wo, longc, mixed, proj, trans, spec, ntr, wm, wm, wm, sw, sw, sw, skip, state, zt,
        iw, ow, eo, io, oo, fw, rates, *tabs, *tabst]
    specs = [whole_spec(dat), pl.BlockSpec((length, width), late), whole_spec(segments), whole_spec(g1),
        pl.BlockSpec((CHUNK, width), lambda c, r: (c, 0)), part_spec(length), stack_spec(3, length), stack_spec(3, length),
        pl.BlockSpec((1, DOCS, 2 * length, CHUNK), lambda c, r: (r, 0, 0, c)), column_spec(2 * length + n // 2, 0, count),
        whole_spec(ntr)]
    specs += [column_spec(width, k, count) for k in range(3)] + [column_spec(3, k, count) for k in range(3)]
    specs += [whole_spec(a) for a in (skip, state, zt, iw, ow, eo, io, oo)]
    specs += [column_spec(hidden, 0, count), column_spec(1, 0, count)] + [whole_spec(a) for a in (*tabs, *tabst)]
    return pl.pallas_call(
        backward_kernel, grid=(count, rows_here), in_specs=specs,
        out_specs=[pl.BlockSpec((length, width), late),
            pl.BlockSpec((3, CHUNK // LANES, width, LANES), lambda c, r: (0, c, 0, 0)),
            pl.BlockSpec((3, 8, CHUNK), lambda c, r: (0, 0, c)), fixed_spec(8, width), fixed_spec(zt.shape[0], hidden),
            fixed_spec(hidden, hidden), fixed_spec(hidden, hidden), column_spec(hidden, 0, count), fixed_spec(6, 8, hidden)],
        out_shape=[sds((total, width), bf), sds((3, width // LANES, width, LANES), bf), sds((3, 8, width), f32),
            sds((8, width), f32), sds((zt.shape[0], hidden), f32), sds((hidden, hidden), f32), sds((hidden, hidden), f32),
            sds((hidden, width), f32), sds((6, 8, hidden), f32)],
        scratch_shapes=[pltpu.VMEM((total, width), f32), pltpu.VMEM((hidden, length), f32), pltpu.VMEM((3, total, CHUNK), bf),
            pltpu.VMEM((6 * n + n // 2, CHUNK), f32)],
        compiler_params=pltpu.CompilerParams(vmem_limit_bytes=VMEM_BYTES),
        cost_estimate=pl.CostEstimate(
            flops=total * width * (14 * width + 4 * 2 * 5 * n), bytes_accessed=50 * total * width, transcendentals=0),
        name="mixer_backward")(*ins)


def bits_of(n):
    return n.bit_length() - 1


def order_of(rows_n, pos_n, first):
    rows = [("rows", b) for b in range(1, bits_of(rows_n))]
    pos = [("pos", b) for b in range(bits_of(pos_n))]
    return [("rows", 0)] + (pos + rows if first == "pos" else rows[:1] + pos + rows[1:])


def scatter_blocks(grad, rows_n, pos_n, first):
    blocks, height, wide = grad.shape
    if blocks % pos_n:
        flat = grad.transpose(1, 0, 2).reshape(height, blocks * wide)
        wide = blocks * wide // pos_n
        blocks = pos_n
        grad = flat.reshape(height, blocks, wide).transpose(1, 0, 2)
    high = height // rows_n
    rbits, pbits = bits_of(rows_n), bits_of(pos_n)
    acc = grad.reshape((2,) * pbits + (blocks // pos_n,) + (2,) * rbits + (high, wide))
    alive = [("pos", b) for b in reversed(range(pbits))] + [None] + [("rows", b) for b in reversed(range(rbits))]
    for axis, bit in order_of(rows_n, pos_n, first):
        dim = alive.index((axis, bit))
        mine = (lax.axis_index(axis) >> bit) & 1
        size = rows_n if axis == "rows" else pos_n
        send = lax.dynamic_index_in_dim(acc, 1 - mine, dim, keepdims=False)
        keep = lax.dynamic_index_in_dim(acc, mine, dim, keepdims=False)
        got = lax.ppermute(send, axis, [(i, i ^ (1 << bit)) for i in range(size)])
        acc = (keep.astype(f32) + got.astype(f32)).astype(bf)
        alive.pop(dim)
    return acc


def pack_places(width, hidden, emb, ff):
    per = width // PACK
    at = {"filter": 0, "square": hidden * per}
    row = at["square"] + hidden
    for name, vectors in (("vec1", 2), ("vec2", 4), ("sgrad", 15), ("skip", 1), ("ebias", ff // width)):
        at[name] = row
        row += vectors * per
    at["small"] = row
    return at, row + 6


def pack_small(at, pk, beg, vec2, sgrad, vec1, gew, giw, gow, gfw, gsm):
    width = vec1.shape[1]
    hidden = giw.shape[0]
    per = width // PACK

    def put(row, value):
        for h in range(per):
            pk[row + h:row + h + 1, :] = value[:, h * PACK:(h + 1) * PACK]

    for k in range(beg.shape[1] // width):
        put(at["ebias"] + k * per, beg[:, k * width:(k + 1) * width])
    for k in range(4):
        put(at["vec2"] + k * per, vec2[k:k + 1, :])
    for i in range(3):
        for k in range(5):
            put(at["sgrad"] + (i * 5 + k) * per, sgrad[i, k:k + 1, :])
    put(at["skip"], sgrad[0, 5:6, :])
    for k in range(2):
        put(at["vec1"] + k * per, vec1[k:k + 1, :])
    for lane, ref in ((0, gew), (128, giw), (256, gow)):
        high = min(ref.shape[0], hidden)
        pk[at["square"]:at["square"] + high, lane:lane + hidden] = ref[0:high, :]
    for h in range(per):
        pk[at["filter"] + h * hidden:at["filter"] + (h + 1) * hidden, :] = gfw[:, h * PACK:(h + 1) * PACK]
    for k in range(6):
        pk[at["small"] + k:at["small"] + k + 1, 0:hidden] = gsm[k, 0:1, :]


class Halving:
    def __init__(self, ref, blocks, alive, order, got, sums, send_sem, recv_sem):
        self.ref, self.blocks, self.alive, self.order = ref, blocks, list(alive), order
        self.got, self.sums, self.send_sem, self.recv_sem = got, sums, send_sem, recv_sem
        self.copy = None

    def pick(self, dim, which):
        start, count = self.blocks
        index = [slice(None)] * len(self.alive)
        index[self.alive.index(None)] = pl.ds(start, count)
        index[dim] = which
        return tuple(index)

    def start(self, stage):
        axis, bit = self.order[stage]
        dim = self.alive.index((axis, bit))
        place = lax.axis_index(axis)
        mine = (place // (1 << bit)) % 2
        self.keep = self.pick(dim, mine)
        self.copy = pltpu.make_async_remote_copy(
            src_ref=self.ref.at[self.pick(dim, 1 - mine)], dst_ref=self.got[stage], send_sem=self.send_sem.at[stage],
            recv_sem=self.recv_sem.at[stage], device_id={axis: place + (1 - 2 * mine) * (1 << bit)}, device_id_type=MESH)
        self.copy.start()
        self.alive.pop(dim)

    def finish(self, stage):
        self.copy.wait()
        kept, got, out = self.ref.at[self.keep], self.got[stage], self.sums[stage]
        split = self.alive.index(None)

        def add(lead):
            def body(b, carry):
                at = lead + (b,)
                out[at] = (kept[at].astype(f32) + got[at].astype(f32)).astype(bf)
                return carry

            lax.fori_loop(0, self.blocks[1], body, 0)

        leads = [()]
        for d in range(split):
            leads = [lead + (k,) for lead in leads for k in range(2)]
        for lead in leads:
            add(lead)
        self.ref, self.blocks = out, (0, self.blocks[1])


def job_shapes(shape, blocks, alive, order):
    dims = list(alive)
    now = [blocks if d is None else 2 for d in dims] + list(shape[-2:])
    out = []
    for step in order:
        k = dims.index(step)
        dims.pop(k)
        now.pop(k)
        out.append(tuple(now))
    return out


def exchange_kernel(sizes, at, plan, count, *refs):
    rows_n, pos_n = sizes
    n = rows_n * pos_n
    small = refs[:9]
    grads = refs[9:9 + count]
    pos = 9 + count
    packed_out = refs[pos]
    outs = refs[pos + 1:pos + 1 + len(plan)]
    scratch = list(refs[pos + 1 + len(plan):])
    pk, rbuf, red, gath, ss1, rs1, ss2, rs2 = scratch[:8]
    rest = scratch[8:]
    jobs = []
    for (src, blocks, alive, order), out in zip(plan, outs):
        m = len(order)
        got, sums = rest[:m], rest[m:2 * m - 1] + [out]
        jobs.append(Halving(grads[src], blocks, alive, order, got, sums, rest[2 * m - 1], rest[2 * m]))
        rest = rest[2 * m + 1:]
    me = lax.axis_index("rows") * pos_n + lax.axis_index("pos")
    chunk = pk.shape[0] // n

    def ident(t):
        return {"rows": t // pos_n, "pos": t % pos_n}

    def each(f):
        def body(k, carry):
            f(lax.rem(me + k, n))
            return carry

        lax.fori_loop(1, n, body, 0)

    def part(t):
        return pl.ds(pl.multiple_of(t * chunk, chunk), chunk)

    barrier = pltpu.get_barrier_semaphore()
    each(lambda t: pl.semaphore_signal(barrier, inc=1, device_id=ident(t), device_id_type=MESH))
    pk[...] = jnp.zeros_like(pk)
    pack_small(at, pk, *small)
    pl.semaphore_wait(barrier, n - 1)

    def scatter(t, slot):
        return pltpu.make_async_remote_copy(
            src_ref=pk.at[part(t), :], dst_ref=rbuf.at[slot], send_sem=ss1.at[t], recv_sem=rs1.at[slot], device_id=ident(t),
            device_id_type=MESH)

    def publish(t, slot):
        return pltpu.make_async_remote_copy(
            src_ref=red, dst_ref=gath.at[part(slot), :], send_sem=ss2.at[t], recv_sem=rs2.at[slot], device_id=ident(t),
            device_id_type=MESH)

    for job in jobs:
        job.start(0)
    each(lambda t: scatter(t, me).start())
    rbuf[me] = pk[part(me), :]
    stages = max(len(job.order) for job in jobs)
    for stage in range(stages):
        for job in jobs:
            if stage < len(job.order):
                job.finish(stage)
                if stage + 1 < len(job.order):
                    job.start(stage + 1)
        if stage == 0:
            each(lambda t: scatter(t, t).wait())
            total = rbuf[0]
            for s in range(1, n):
                total = total + rbuf[s]
            red[...] = total
            gath[part(me), :] = total
            each(lambda t: publish(t, me).start())
    each(lambda t: publish(t, t).wait())
    packed_out[...] = gath[...]


def exchange(sizes, at, used, small, grads, plan):
    rows_n, pos_n = sizes
    n = rows_n * pos_n
    total = -(-used // (8 * n)) * 8 * n
    chunk = total // n
    vm = pl.BlockSpec(memory_space=pltpu.VMEM)
    scratch = [pltpu.VMEM((total, PACK), f32), pltpu.VMEM((n, chunk, PACK), f32), pltpu.VMEM((chunk, PACK), f32),
        pltpu.VMEM((total, PACK), f32)] + [pltpu.SemaphoreType.DMA((n,))] * 4
    shapes = [jax.ShapeDtypeStruct((total, PACK), f32)]
    for src, (start, blocks), alive, order in plan:
        left = job_shapes(grads[src].shape, blocks, alive, order)
        shapes.append(jax.ShapeDtypeStruct(left[-1], bf))
        scratch += [pltpu.VMEM(s, bf) for s in left] + [pltpu.VMEM(s, bf) for s in left[:-1]]
        scratch += [pltpu.SemaphoreType.DMA((len(order),))] * 2
    return pl.pallas_call(
        functools.partial(exchange_kernel, sizes, at, plan, len(grads)), out_shape=shapes,
        in_specs=[vm] * (9 + len(grads)), out_specs=[vm] * len(shapes), scratch_shapes=scratch,
        compiler_params=pltpu.CompilerParams(collective_id=0, has_side_effects=True, vmem_limit_bytes=VMEM_BYTES),
        name="exchange")(*small, *grads)


def unpack(at, packed, blocks, width, hidden, emb, ff):
    per = width // PACK
    counts = [len(parts) for parts in blocks]
    flat = [p for parts in blocks for p in parts]

    def kernel(pk, *refs):
        ins = list(refs[:len(flat)])
        fg, fs, mb, sw, sb, ew, eb, eo, iw, ib, io, ow, ob, oo, fw, sk, obias, sg, ss, eb2, rb = refs[len(flat):len(flat) + 21]
        outs = refs[len(flat) + 21:]

        def get(ref, lane, row):
            for h in range(per):
                ref[lane + h * PACK:lane + (h + 1) * PACK] = pk[row + h, :]

        get(fg, 0, at["vec1"])
        get(fs, 0, at["vec1"] + per)
        for i in range(3):
            base = at["sgrad"] + i * 5 * per
            for k in range(3):
                for h in range(per):
                    lane = i * width + h * PACK
                    sw[k:k + 1, lane:lane + PACK] = pk[base + k * per + h:base + k * per + h + 1, :]
            get(sb, i * width, base + 3 * per)
            get(mb, i * width, base + 4 * per)
        q = at["square"]
        ew[...] = pk[q:q + emb, 0:hidden]
        iw[...] = pk[q:q + hidden, 128:128 + hidden]
        ow[...] = pk[q:q + hidden, 256:256 + hidden]
        for k, ref in enumerate((oo, ob, io, ib, eo, eb)):
            ref[...] = pk[at["small"] + k, 0:hidden]
        for h in range(per):
            fw[:, h * PACK:(h + 1) * PACK] = pk[at["filter"] + h * hidden:at["filter"] + (h + 1) * hidden, :]
        get(sk, 0, at["skip"])
        for k, ref in enumerate((sg, ss, obias, rb)):
            get(ref, 0, at["vec2"] + k * per)
        for k in range(ff // width):
            get(eb2, k * width, at["ebias"] + k * per)
        for parts, out in zip(counts, outs):
            lane = 0
            for _ in range(parts):
                src = ins.pop(0)
                for b in range(src.shape[0]):
                    out[:, lane:lane + src.shape[2]] = src[b].astype(f32)
                    lane += src.shape[2]

    s = lambda *d: jax.ShapeDtypeStruct(d, f32)
    shapes = [s(width), s(width), s(3 * width), s(3, 3 * width), s(3 * width), s(emb, hidden), s(hidden), s(hidden),
        s(hidden, hidden), s(hidden), s(hidden), s(hidden, hidden), s(hidden), s(hidden), s(hidden, width), s(width), s(width),
        s(width), s(width), s(ff), s(width)]
    shapes += [s(parts[0].shape[1], sum(p.shape[0] for p in parts) * parts[0].shape[2]) for parts in blocks]
    vm = pl.BlockSpec(memory_space=pltpu.VMEM)
    return pl.pallas_call(
        kernel, out_shape=shapes, in_specs=[vm] * (1 + len(flat)), out_specs=[vm] * len(shapes), name="unpack")(packed, *flat)


def on_device(sizes, tokens, segments, cotangent, first_gain, first_shift, mixer_weight, mixer_bias, short_weight, short_bias,
        embed_weight, embed_bias, embed_omega, inner_weight, inner_bias, inner_omega, outer_weight, outer_bias, outer_omega,
        filter_weight, skip_gain, output_weight, output_bias, second_gain, second_shift, expand_weight, expand_bias,
        reduce_weight, reduce_bias):
    rows_n, pos_n = sizes
    length, width = tokens.shape[1:]
    emb, hidden = embed_weight.shape
    ff = expand_weight.shape[1]
    tok = tokens.reshape(-1, width)
    cot = cotangent.reshape(-1, width)
    filt = [embed_weight, embed_bias, embed_omega, inner_weight, inner_bias, inner_omega, outer_weight, outer_bias, outer_omega,
        filter_weight]
    tabs, tabst = radix_tables(length)
    zt, rates = filter_inputs(length, emb, width)
    proj, mixed, longc, mix, trans, spec, state, ntr = forward_mixer(
        tok, segments, first_gain, first_shift, mixer_weight, mixer_bias, short_weight, short_bias, skip_gain, filt, zt, rates,
        tabs, tabst)
    out, dat, wog, weg, wrg, beg, vec2 = mlp(
        mix, tok, cot, output_weight, output_bias, second_gain, second_shift, expand_weight, expand_bias, reduce_weight,
        reduce_bias)
    tgrad, wmg, sgrad, vec1, gew, giw, gow, gfw, gsm = backward_mixer(
        dat, tok, segments, first_gain, output_weight, longc, mixed, proj, trans, spec, ntr, mixer_weight, short_weight,
        skip_gain, state, filt, zt, rates, tabs, tabst)
    wmg = wmg.reshape(3 * width // LANES, width, LANES)
    grads = [wmg, wog, weg, wrg]
    small = (beg, vec2, sgrad, vec1, gew, giw, gow, gfw, gsm)
    at, used = pack_places(width, hidden, emb, ff)
    direct = rows_n * pos_n <= 32 and all(g.shape[0] % pos_n == 0 and g.shape[1] % (16 * rows_n) == 0 for g in grads)
    if direct:
        rbits, pbits = bits_of(rows_n), bits_of(pos_n)
        alive = [("pos", b) for b in reversed(range(pbits))] + [None] + [("rows", b) for b in reversed(range(rbits))]
        grads = [g.reshape((2,) * pbits + (g.shape[0] // pos_n,) + (2,) * rbits + (g.shape[1] // rows_n, LANES)) for g in grads]
        by_pos, by_rows = order_of(rows_n, pos_n, "pos"), order_of(rows_n, pos_n, "rows")
        count = [g.shape[pbits] for g in grads]
        cut = (count[0] + 1) // 2
        plan = [(0, (0, cut), alive, by_pos), (0, (cut, count[0] - cut), alive, by_rows), (1, (0, count[1]), alive, by_rows),
            (2, (0, count[2]), alive, by_pos), (3, (0, count[3]), alive, by_rows)]
        packed, m_a, m_b, o_part, e_part, r_part = exchange(sizes, at, used, small, grads, plan)
        blocks = [[m_a, m_b], [o_part], [e_part], [r_part]]
    else:
        packed = lax.psum(pack_only(at, used, small), ("rows", "pos"))
        blocks = [[scatter_blocks(g, rows_n, pos_n, f)] for g, f in zip(grads, ("pos", "rows", "pos", "rows"))]
    (fg, fs, mb, sw, sb, ew, eb, eo, iw, ib, io, ow, ob, oo, fw, sk, obias, sg, ss, eb2, rb, m_grad, o_grad, e_grad, r_grad) = unpack(
        at, packed, blocks, width, hidden, emb, ff)
    return (out.reshape(tokens.shape), tgrad.reshape(tokens.shape), fg, fs, m_grad, mb, sw, sb, ew, eb, eo, iw, ib, io, ow, ob,
        oo, fw, sk, o_grad, obias, sg, ss, e_grad, eb2, r_grad, rb)


def pack_only(at, used, small):
    def kernel(*refs):
        refs[-1][...] = jnp.zeros_like(refs[-1])
        pack_small(at, refs[-1], *refs[:-1])

    vm = pl.BlockSpec(memory_space=pltpu.VMEM)
    return pl.pallas_call(
        kernel, out_shape=jax.ShapeDtypeStruct((used, PACK), f32), in_specs=[vm] * len(small), out_specs=vm, name="pack")(*small)


def solution(mesh):
    both = ("rows", "pos")
    split = P(both, None, None)
    grid = P("rows", "pos")
    in_specs = (split, P(both, None), split) + (P(),) * 25
    out_specs = (split, split, P(), P(), grid) + (P(),) * 14 + (grid, P(), P(), P(), grid, P(), grid, P())
    sizes = (mesh.shape["rows"], mesh.shape["pos"])
    return jax.shard_map(
        functools.partial(on_device, sizes), mesh=mesh, in_specs=in_specs, out_specs=out_specs, check_vma=False)
```

```python
import functools
import math

import jax
import jax.numpy as jnp
import numpy as np
from jax import lax
from jax.experimental import pallas as pl
from jax.experimental.pallas import tpu as pltpu
from jax.sharding import PartitionSpec as P

f32 = jnp.float32
bf = jnp.bfloat16
HI = lax.Precision.HIGHEST
MESH = pl.DeviceIdType.MESH
DOCS = 2
EPSILON = 1e-5
ROOT3 = math.sqrt(3.0) / 2
LANES = 128
CHUNK = 256
PACK = 384
VMEM_BYTES = 63 * 2**20


def nt(a, b, precision=None):
    return lax.dot_general(a, b, (((1,), (1,)), ((), ())), precision=precision, preferred_element_type=f32)


def nn(a, b, precision=None):
    return lax.dot_general(a, b, (((1,), (0,)), ((), ())), precision=precision, preferred_element_type=f32)


def tn(a, b, precision=None):
    return lax.dot_general(a, b, (((0,), (0,)), ((), ())), precision=precision, preferred_element_type=f32)


def norm_stats(x):
    mean = jnp.mean(x, axis=-1, keepdims=True)
    centered = x - mean
    variance = jnp.mean(centered * centered, axis=-1, keepdims=True)
    scale = lax.rsqrt(variance + EPSILON)
    return centered * scale, scale


def sum0(v):
    return jnp.sum(v, axis=0, keepdims=True)


def as_row(ref):
    return ref[...].reshape(1, -1)


def radix_tables(length):
    n = length // 3
    m = 2 * length
    place = np.arange(n)

    def angle(freqs):
        return 2 * np.pi * ((freqs[:, None] * place[None, :]) % m) / m

    even = angle(6 * np.arange(n // 2))
    sine = np.sin(even)
    sine[0] = np.cos(np.pi * place)
    odd = angle(6 * np.arange(n // 2) + 3)
    out = [np.concatenate([np.cos(even), sine], 0), np.concatenate([np.cos(odd), np.sin(odd)], 0)]
    for k in (1, 2):
        turn = angle(6 * np.arange(n) + k)
        c, s = np.cos(turn), np.sin(turn)
        out.append(np.block([[c, -s], [s, c]]))
    low = lambda v: jnp.asarray(v.astype(np.float32)).astype(bf)
    return [low(t) for t in out], [low(t.T) for t in out]


def spread(x0, x1, x2):
    s = x1 + x2
    d = x1 - x2
    y0 = (x0 + s).astype(bf)
    y3 = (x0 - d).astype(bf)
    y1 = jnp.concatenate([(x0 + 0.5 * d).astype(bf), (ROOT3 * s).astype(bf)], 0)
    y2 = jnp.concatenate([(x0 - 0.5 * s).astype(bf), (ROOT3 * d).astype(bf)], 0)
    return y0, y3, y1, y2


def gather(v0, v3, v1, v2):
    n = v0.shape[0]
    v1r, v1i, v2r, v2i = v1[:n], v1[n:], v2[:n], v2[n:]
    even = v0 + v3
    a = 0.5 * (v1r - v2r)
    b = ROOT3 * (v1i + v2i)
    x0 = even + v1r + v2r
    x1 = (v0 - v3) + a + b
    x2 = even - 0.5 * (v1r + v2r) + ROOT3 * (v1i - v2i)
    return x0, x1, x2


def filter_inputs(length, emb, width):
    bands_count = (emb - 1) // 2
    places = np.arange(length, dtype=np.float32)
    tnorm = places / np.float32(length - 1)
    wave = places * np.float32(2.0 * math.pi / length)
    bands = np.linspace(0.0001, bands_count - 1, bands_count).astype(np.float32)
    phase = (wave[:, None] * bands[None, :]).astype(np.float32)
    z = np.concatenate([tnorm[:, None], np.cos(phase), -np.sin(phase)], 1).astype(np.float32)
    zt = np.concatenate([z.T, np.zeros(((-emb) % 8, length), np.float32)], 0)
    rates = np.abs(np.linspace(math.log(0.01) / 1.5, math.log(0.01) / 0.3, width)).astype(np.float32)[None, :]
    return jnp.asarray(zt), jnp.asarray(rates)


def window(length, rate):
    tnorm = lax.broadcasted_iota(jnp.int32, (length, rate.shape[1]), 0).astype(f32) * (1.0 / (length - 1))
    return jnp.exp(-tnorm * rate)


def sin_cos(x):
    k = jnp.floor(x * (1.0 / math.pi) + 0.5)
    r = x - k * 3.140625
    r = r - k * 0.0009670257568359375
    r = r - k * 6.2771141529083251953e-07
    sign = 1.0 - 2.0 * (k - 2.0 * jnp.floor(k * 0.5))
    q = r * r
    s = 1.0 + q * (-1 / 6 + q * (1 / 120 + q * (-1 / 5040 + q * (1 / 362880 + q * (-1 / 39916800 + q * (1 / 6227020800))))))
    c = 1.0 + q * (-1 / 2 + q * (1 / 24 + q * (-1 / 720 + q * (1 / 40320 + q * (-1 / 3628800 + q * (1 / 479001600 - q * (1 / 87178291200)))))))
    return r * s * sign, c * sign


def column(ref):
    v = as_row(ref)
    n = v.shape[1]
    i = lax.broadcasted_iota(jnp.int32, (n, n), 0)
    j = lax.broadcasted_iota(jnp.int32, (n, n), 1)
    return jnp.sum(jnp.where(i == j, v, 0.0), axis=1, keepdims=True)


def token_masks(seg, length, wide):
    edge = jnp.sum((seg == 0).astype(jnp.int32), axis=1, keepdims=True)
    t = lax.broadcasted_iota(jnp.int32, (length, wide), 0)
    one = jnp.logical_and(t != 0, t != edge)
    two = jnp.logical_and(jnp.logical_and(one, t != 1), t != edge + 1)
    return t < edge, one, two


def specs_of(length, n):
    return ((0, 0, n // 2), (1, n, n // 2), (2, 2 * n, n), (3, 4 * n, n))


def bits_of(n):
    return n.bit_length() - 1


def order_of(rows_n, pos_n, first):
    rows = [("rows", b) for b in range(1, bits_of(rows_n))]
    pos = [("pos", b) for b in range(bits_of(pos_n))]
    return [("rows", 0)] + (pos + rows if first == "pos" else rows[:1] + pos + rows[1:])


def alive_dims(rows_n, pos_n):
    pos = [("pos", b) for b in reversed(range(bits_of(pos_n)))]
    return pos + [None] + [("rows", b) for b in reversed(range(bits_of(rows_n)))]


def partner(step):
    axis, bit = step
    place = lax.axis_index(axis)
    mine = (place // (1 << bit)) % 2
    return mine, {axis: place + (1 - 2 * mine) * (1 << bit)}


def meet(steps):
    barrier = pltpu.get_barrier_semaphore()
    for step in steps:
        pl.semaphore_signal(barrier, inc=1, device_id=partner(step)[1], device_id_type=MESH)
    pl.semaphore_wait(barrier, len(steps))


class Halving:
    def __init__(self, ref, blocks, alive, order, refs, near=None):
        m = len(order)
        self.near = near
        got, sums, self.send_sem, self.recv_sem = refs[:m], refs[m:2 * m], refs[2 * m], refs[2 * m + 1]
        self.order, self.got, self.sums = order, got, sums
        self.stages = []
        alive = list(alive)
        for k, step in enumerate(order):
            self.stages.append((ref, blocks, tuple(alive), alive.index(step)))
            alive.remove(step)
            ref, blocks = sums[k], (0, blocks[1])

    def pick(self, stage, which):
        ref, (start, count), alive, dim = self.stages[stage]
        index = [slice(None)] * len(alive)
        index[alive.index(None)] = pl.ds(start, count)
        index[dim] = which
        return ref.at[tuple(index)]

    def copy(self, stage):
        mine, there = partner(self.order[stage])
        return pltpu.make_async_remote_copy(
            src_ref=self.pick(stage, 1 - mine), dst_ref=self.got[stage], send_sem=self.send_sem.at[stage],
            recv_sem=self.recv_sem.at[stage], device_id=there, device_id_type=MESH)

    def fetch(self):
        return pltpu.make_async_copy(self.pick(0, partner(self.order[0])[0]), self.sums[0], self.near)

    def start(self, stage):
        self.copy(stage).start()
        if stage == 0 and self.near is not None:
            self.fetch().start()

    def finish(self, stage):
        self.copy(stage).wait()
        if stage == 0 and self.near is not None:
            self.fetch().wait()
        _, (_, count), alive, dim = self.stages[stage]
        kept, got, out = self.pick(stage, partner(self.order[stage])[0]), self.got[stage], self.sums[stage]
        if stage == 0 and self.near is not None:
            kept = out
        split = [d for k, d in enumerate(alive) if k != dim].index(None)

        def add(lead):
            def body(b, carry):
                at = lead + (b,)
                out[at] = (kept[at].astype(f32) + got[at].astype(f32)).astype(bf)
                return carry

            lax.fori_loop(0, count, body, 0)

        leads = [()]
        for _ in range(split):
            leads = [lead + (k,) for lead in leads for k in range(2)]
        for lead in leads:
            add(lead)


def job_shapes(shape, blocks, alive, order):
    dims = list(alive)
    now = [blocks if d is None else 2 for d in dims] + list(shape[-2:])
    out = []
    for step in order:
        k = dims.index(step)
        dims.pop(k)
        now.pop(k)
        out.append(tuple(now))
    return out


def job_scratch(left, last):
    sums = left if last else left[:-1]
    return [pltpu.VMEM(s, bf) for s in left] + [pltpu.VMEM(s, bf) for s in sums] + [pltpu.SemaphoreType.DMA((len(left),))] * 2


def grad_shape(blocks, rows, rows_n, pos_n, cores):
    rbits, pbits = bits_of(rows_n), bits_of(pos_n)
    return (2,) * pbits + (blocks // pos_n,) + (2,) * (rbits - (0 if cores else 1)) + (rows // rows_n, LANES)


def forward_kernel(tok_ref, seg_ref, g1_ref, s1_ref, wg_ref, wi_ref, wv_ref, mb_ref, swg_ref, swi_ref, swv_ref, sb_ref,
        skip_ref, zt_ref, ew_ref, eb_ref, eo_ref, iw_ref, ib_ref, io_ref, ow_ref, ob_ref, oo_ref, fw_ref, rate_ref,
        t0, t3, t1, t2, u0, u3, u1, u2,
        proj_ref, mixed_ref, long_ref, mix_ref, trans_ref, spec_ref, state_ref, nt_ref, normed, padded):
    c = pl.program_id(0)
    r = pl.program_id(1)
    length, width = tok_ref.shape
    n = length // 3
    half = n // 2
    wide = fw_ref.shape[1]
    rows = pl.ds(pl.multiple_of(r * length, length), length)
    tables = ((t0, u0), (t3, u3), (t1, u1), (t2, u2))

    @pl.when(c == 0)
    def _():
        step = 256
        for i in range(length // step):
            part = slice(i * step, (i + 1) * step)
            xhat, _ = norm_stats(tok_ref[part, :].astype(f32))
            low = (xhat * as_row(g1_ref) + as_row(s1_ref)).astype(bf)
            normed[pl.ds(pl.multiple_of(r * length + i * step, step), step), :] = low
            nt_ref[:, part] = low.T

    @pl.when(jnp.logical_and(c == 0, r == 0))
    def _():
        padded[...] = jnp.zeros_like(padded)
        padded[0:ew_ref.shape[0], :] = ew_ref[...]
        pre = tn(padded[...], zt_ref[...], HI) + column(eb_ref)
        e1, c1 = sin_cos(column(eo_ref) * pre)
        state_ref[0] = e1
        state_ref[1] = c1
        state_ref[2] = pre
        pre = tn(iw_ref[...], e1, HI) + column(ib_ref)
        e2, c2 = sin_cos(column(io_ref) * pre)
        state_ref[3] = e2
        state_ref[4] = c2
        state_ref[5] = pre
        pre = tn(ow_ref[...], e2, HI) + column(ob_ref)
        e3, c3 = sin_cos(column(oo_ref) * pre)
        state_ref[6] = e3
        state_ref[7] = c3
        state_ref[8] = pre

    @pl.when(r == 0)
    def _():
        kernel = tn(state_ref[6], fw_ref[...], HI) * window(length, rate_ref[...])
        k = kernel.astype(bf).astype(f32)
        y0, y3, y1, y2 = spread(k[0:n], k[n:2 * n], k[2 * n:])
        first = lax.broadcasted_iota(jnp.int32, (half, wide), 0) == 0
        q0 = nn(t0[...], y0)
        spec_ref[0:half] = q0[0:half] * jnp.where(first, 0.5, 1.0)
        spec_ref[half:n] = jnp.where(first, 0.0, q0[half:])
        spec_ref[6 * n:6 * n + half] = jnp.where(first, 0.5 * q0[half:], q0[0:half])
        spec_ref[n:2 * n] = nn(t3[...], y3)
        spec_ref[2 * n:4 * n] = nn(t1[...], y1)
        spec_ref[4 * n:6 * n] = nn(t2[...], y2)

    edge, one, two = token_masks(seg_ref[pl.ds(r, 1), :], length, wide)
    low = normed[rows, :]
    mixed = []
    for i, (w, sw) in enumerate(((wg_ref, swg_ref), (wi_ref, swi_ref), (wv_ref, swv_ref))):
        at = pl.ds(pl.multiple_of(i * width + c * wide, wide), wide)
        p = nn(low, w[...]) + mb_ref[at].reshape(1, wide)
        proj_ref[i] = p.astype(bf)
        m = (sb_ref[at].reshape(1, wide) + sw[0:1, :] * p + sw[1:2, :] * jnp.where(one, pltpu.roll(p, 1, 0), 0.0)
            + sw[2:3, :] * jnp.where(two, pltpu.roll(p, 2, 0), 0.0))
        mixed_ref[i] = m.astype(bf)
        mixed.append(m)
    inner = mixed[2] * mixed[1]
    inner_low = inner.astype(bf).astype(f32)
    conv = None
    for d in range(DOCS):
        x = jnp.where(edge, inner_low, 0.0) if d == 0 else jnp.where(edge, 0.0, inner_low)
        ys = spread(x[0:n], x[n:2 * n], x[2 * n:])
        parts = []
        for s, off, m in specs_of(length, n):
            t, u = tables[s]
            p = nn(t[...], ys[s])
            trans_ref[0, d, off:off + 2 * m, :] = p.astype(bf)
            pa, pb = p[:m], p[m:]
            qa, qb = spec_ref[off:off + m], spec_ref[off + m:off + 2 * m]
            qc = spec_ref[6 * n:6 * n + m] if s == 0 else qa
            prod = jnp.concatenate([(pa * qa - pb * qb).astype(bf), (pa * qb + pb * qc).astype(bf)], 0)
            parts.append(nn(u[...], prod))
        y = jnp.concatenate(gather(*parts), 0)
        conv = y if d == 0 else jnp.where(edge, conv, y)
    longconv = conv * (1.0 / length) + skip_ref[pl.ds(pl.multiple_of(c * wide, wide), wide)].reshape(1, wide) * inner
    long_ref[...] = longconv.astype(bf)
    mix_ref[...] = (mixed[0] * longconv).astype(bf)


def whole_spec(a):
    return pl.BlockSpec(a.shape, lambda *_: (0,) * a.ndim, pipeline_mode=pl.Buffered(1))


def fixed_spec(*shape):
    return pl.BlockSpec(shape, lambda *_: (0,) * len(shape))


def column_spec(rows, k, count):
    return pl.BlockSpec((rows, CHUNK), lambda c, r: (0, k * count + c))


def part_spec(length):
    return pl.BlockSpec((length, CHUNK), lambda c, r: (r, c))


def stack_spec(count, length):
    return pl.BlockSpec((count, length, CHUNK), lambda c, r: (0, r, c))


def vector_chunk():
    return pl.BlockSpec((CHUNK,), lambda c, r: (c,))


def forward_mixer(tok, segments, g1, s1, wm, mb, sw, sb, skip, filt, zt, rates, tabs, tabst):
    rows_here, length = segments.shape
    total, width = tok.shape
    n = length // 3
    count = width // CHUNK
    fw = filt[-1]
    hidden = fw.shape[0]
    sds = jax.ShapeDtypeStruct
    ins = [tok, segments, g1, s1, wm, wm, wm, mb, sw, sw, sw, sb, skip, zt, *filt, rates, *tabs, *tabst]
    specs = [pl.BlockSpec((length, width), lambda c, r: (jnp.where(c == 0, r, rows_here - 1), 0))]
    specs += [whole_spec(a) for a in (segments, g1, s1)]
    specs += [column_spec(width, k, count) for k in range(3)] + [whole_spec(mb)] + [column_spec(3, k, count) for k in range(3)]
    specs += [whole_spec(sb), whole_spec(skip), whole_spec(zt)] + [whole_spec(a) for a in filt[:-1]]
    specs += [column_spec(hidden, 0, count), column_spec(1, 0, count)] + [whole_spec(a) for a in (*tabs, *tabst)]
    return pl.pallas_call(
        forward_kernel, grid=(count, rows_here), in_specs=specs,
        out_specs=[stack_spec(3, length), stack_spec(3, length), part_spec(length), part_spec(length),
            pl.BlockSpec((1, DOCS, 2 * length, CHUNK), lambda c, r: (r, 0, 0, c)), column_spec(2 * length + n // 2, 0, count),
            fixed_spec(9, hidden, length),
            pl.BlockSpec((width, length), lambda c, r: (0, jnp.where(c == 0, r, rows_here - 1)))],
        out_shape=[sds((3, total, width), bf), sds((3, total, width), bf), sds((total, width), bf), sds((total, width), bf),
            sds((rows_here, DOCS, 2 * length, width), bf), sds((2 * length + n // 2, width), f32),
            sds((9, hidden, length), f32), sds((width, total), bf)],
        scratch_shapes=[pltpu.VMEM((total, width), bf), pltpu.VMEM((zt.shape[0], hidden), f32)],
        compiler_params=pltpu.CompilerParams(vmem_limit_bytes=VMEM_BYTES),
        cost_estimate=pl.CostEstimate(
            flops=total * width * (6 * width + 4 * 2 * 5 * n), bytes_accessed=40 * total * width, transcendentals=0),
        name="mixer_forward")(*ins)


def gelu_parts(e):
    d = 1.0 + (0.3275911 / math.sqrt(2)) * jnp.abs(e)
    t = pl.reciprocal(d, approx=True)
    t = t * (2.0 - d * t)
    bell = jnp.exp(e * e * (-0.5))
    poly = t * (0.5 * 0.254829592 + t * (0.5 * -0.284496736 + t * (0.5 * 1.421413741 + t * (0.5 * -1.453152027 + t * (0.5 * 1.061405429)))))
    tail = poly * bell
    phi = jnp.where(e >= 0, 1.0 - tail, tail)
    return phi, phi + e * bell * (1 / math.sqrt(2 * math.pi))


def mlp_kernel(links, mix_ref, tok_ref, cot_ref, wo_ref, bo_ref, g2_ref, s2_ref, we_ref, be_ref, wr_ref, br_ref,
        out_ref, dat_ref, wog_ref, weg_ref, wrg_ref, beg_ref, vec_ref, hid, acc, dn2, n2, n2t, cott, act, de, *pair):
    j = pl.program_id(0)
    last = pl.num_programs(0) - 1
    total, width = tok_ref.shape
    part_ff = we_ref.shape[1]
    step = 512
    steps = total // step

    def at(i, size=step):
        return pl.ds(pl.multiple_of(i * size, size), size)

    core = ("rows", 0)
    if links:
        ahead_s, back_s, ahead_got, back_got, send_sem, recv_sem = pair

        def copies(k):
            mine, there = partner(core)
            slot = lax.rem(k, 2)
            return [
                pltpu.make_async_remote_copy(
                    src_ref=src.at[1 - mine], dst_ref=dst.at[slot], send_sem=send_sem.at[w], recv_sem=recv_sem.at[w, slot],
                    device_id=there, device_id_type=MESH)
                for w, (src, dst) in enumerate(((ahead_s, ahead_got), (back_s, back_got)))]

        def finish(k):
            for copy in copies(k):
                copy.wait()
            mine, _ = partner(core)
            slot = lax.rem(k, 2)
            count = ahead_s.shape[1]

            def add(b, carry):
                weg_ref[k * count + b] = (ahead_s[mine, b].astype(f32) + ahead_got[slot, b].astype(f32)).astype(bf)
                wrg_ref[b, k] = (back_s[mine, b].astype(f32) + back_got[slot, b].astype(f32)).astype(bf)
                return carry

            lax.fori_loop(0, count, add, 0)

    @pl.when(j == 0)
    def _():
        if links:
            meet([core])

        def body(i, carry):
            rows = at(i)
            h = tok_ref[rows, :].astype(f32) + nn(mix_ref[rows, :], wo_ref[...]) + as_row(bo_ref)
            hid[rows, :] = h
            xhat, _ = norm_stats(h)
            n2[rows, :] = (xhat * as_row(g2_ref) + as_row(s2_ref)).astype(bf)
            acc[rows, :] = h + as_row(br_ref)
            dn2[rows, :] = jnp.zeros((step, width), f32)
            return carry

        lax.fori_loop(0, steps, body, 0)
        for i in range(steps):
            rows = slice(i * step, (i + 1) * step)
            n2t[:, rows] = n2[rows, :].T
            cott[:, rows] = cot_ref[rows, :].T

    def tile(i, carry):
        rows = at(i)
        e = nn(n2[rows, :], we_ref[...]) + be_ref[pl.ds(pl.multiple_of(j * part_ff, part_ff), part_ff)].reshape(1, part_ff)
        da = nt(cot_ref[rows, :], wr_ref[...])
        phi, slope = gelu_parts(e)
        a = (e * phi).astype(bf)
        d = (da * slope).astype(bf)
        act[rows, :] = a
        de[rows, :] = d
        acc[rows, :] += nn(a, wr_ref[...])
        dn2[rows, :] += nt(d, we_ref[...])
        return carry + sum0(d.astype(f32))

    beg_ref[...] = lax.fori_loop(0, steps, tile, jnp.zeros((1, part_ff), f32))

    def grads(i, carry):
        rows = at(i, 384)
        back = nn(cott[rows, :], act[...]).astype(bf).T
        ahead = nn(n2t[rows, :], de[...]).astype(bf)
        blocks = 384 // LANES
        if links:
            tall = back_s.shape[3]
            for h in range(blocks):
                for y in range(back_s.shape[2]):
                    for k in range(2):
                        top = (2 * y + k) * tall
                        back_s[k, i * blocks + h, y] = back[top:top + tall, h * LANES:(h + 1) * LANES]
            tall = ahead_s.shape[3]
            groups = 384 // (2 * tall)
            for h in range(part_ff // LANES):
                for g in range(groups):
                    for k in range(2):
                        top = (2 * g + k) * tall
                        ahead_s[k, h, i * groups + g] = ahead[top:top + tall, h * LANES:(h + 1) * LANES]
        else:
            for h in range(blocks):
                wrg_ref[i * blocks + h, pl.ds(pl.multiple_of(j * part_ff, part_ff), part_ff), :] = back[:, h * LANES:(h + 1) * LANES]
            for h in range(part_ff // LANES):
                weg_ref[j * (part_ff // LANES) + h, rows, :] = ahead[:, h * LANES:(h + 1) * LANES]
        return carry

    if links:
        @pl.when(j > 0)
        def _():
            finish(j - 1)

    lax.fori_loop(0, width // 384, grads, 0)
    if links:
        for copy in copies(j):
            copy.start()

    @pl.when(j == last)
    def _():
        def body(i, carry):
            rows = at(i)
            out_ref[rows, :] = acc[rows, :].astype(bf)
            xhat, scale = norm_stats(hid[rows, :])
            dn = dn2[rows, :]
            gd = dn * as_row(g2_ref)
            m1 = jnp.mean(gd, axis=-1, keepdims=True)
            m2 = jnp.mean(gd * xhat, axis=-1, keepdims=True)
            cot = cot_ref[rows, :].astype(f32)
            low = (cot + scale * (gd - m1 - xhat * m2)).astype(bf)
            dat_ref[rows, :] = low
            return (carry[0] + sum0(dn * xhat), carry[1] + sum0(dn), carry[2] + sum0(low.astype(f32)), carry[3] + sum0(cot))

        zero = jnp.zeros((1, width), f32)
        sums = lax.fori_loop(0, steps, body, (zero,) * 4)
        for k in range(4):
            vec_ref[k:k + 1, :] = sums[k]
        for i in range(steps):
            rows = slice(i * step, (i + 1) * step)
            n2t[:, rows] = mix_ref[rows, :].T

        def weights(i, carry):
            rows = at(i, 256)
            part = nn(n2t[rows, :], dat_ref[...]).astype(bf)
            for h in range(width // LANES):
                wog_ref[h, rows, :] = part[:, h * LANES:(h + 1) * LANES]
            return carry

        lax.fori_loop(0, width // 256, weights, 0)
        if links:
            finish(j)


def single(*shape):
    return pl.BlockSpec(shape, lambda *_: (0,) * len(shape), pipeline_mode=pl.Buffered(1))


def mlp(links, mix, tok, cot, wo, bo, g2, s2, we, be, wr, br, part_ff=768):
    total, width = tok.shape
    ff = we.shape[1]
    sds = jax.ShapeDtypeStruct
    blocks = width // LANES
    parts = ff // part_ff
    scratch = [pltpu.VMEM((total, width), f32)] * 3 + [pltpu.VMEM((total, width), bf)]
    scratch += [pltpu.VMEM((width, total), bf)] * 2 + [pltpu.VMEM((total, part_ff), bf)] * 2
    if links:
        rows_n = links[0]
        pairs = rows_n // 2
        ahead = (ff // LANES, pairs, width // rows_n, LANES)
        back = (blocks, parts, pairs // parts, ff // rows_n, LANES)
        for shape in ((part_ff // LANES, *ahead[1:]), (blocks, *back[2:])):
            scratch.append(pltpu.VMEM((2, *shape), bf))
        for shape in ((part_ff // LANES, *ahead[1:]), (blocks, *back[2:])):
            scratch.append(pltpu.VMEM((2, *shape), bf))
        scratch += [pltpu.SemaphoreType.DMA((2,)), pltpu.SemaphoreType.DMA((2, 2))]
    else:
        ahead, back = (ff // LANES, width, LANES), (blocks, ff, LANES)
    side = dict(collective_id=1, has_side_effects=True) if links else {}
    return pl.pallas_call(
        functools.partial(mlp_kernel, links), grid=(parts,),
        in_specs=[whole_spec(a) for a in (mix, tok, cot, wo, bo, g2, s2)]
            + [pl.BlockSpec((width, part_ff), lambda j: (0, j)), whole_spec(be), pl.BlockSpec((part_ff, width), lambda j: (j, 0)),
                whole_spec(br)],
        out_specs=[single(total, width), single(total, width), single(blocks, width, LANES), single(*ahead), single(*back),
            pl.BlockSpec((1, part_ff), lambda j: (0, j)), single(8, width)],
        out_shape=[sds((total, width), bf), sds((total, width), bf), sds((blocks, width, LANES), bf), sds(ahead, bf),
            sds(back, bf), sds((1, ff), f32), sds((8, width), f32)],
        scratch_shapes=scratch,
        compiler_params=pltpu.CompilerParams(vmem_limit_bytes=VMEM_BYTES, **side),
        cost_estimate=pl.CostEstimate(
            flops=12 * total * width * ff + 4 * total * width * width, bytes_accessed=30 * total * width,
            transcendentals=total * ff),
        name="mlp")(mix, tok, cot, wo, bo, g2, s2, we, be, wr, br)


def backward_kernel(links, plan, *refs):
    moved = len(plan)
    grads, refs = refs[:moved], refs[moved:]
    (dat_ref, tok_ref, seg_ref, g1_ref, wo_ref, long_ref, mixed_ref, proj_ref, trans_ref, spec_ref, nt_ref,
        wg_ref, wi_ref, wv_ref, swg_ref, swi_ref, swv_ref, skip_ref, state_ref, zt_ref, iw_ref, ow_ref, eo_ref, io_ref,
        oo_ref, fw_ref, rate_ref, t0, t3, t1, t2, u0, u3, u1, u2,
        tg_ref, wgrad_ref, sg_ref, vec_ref, gew_ref, giw_ref, gow_ref, gfw_ref, gsm_ref) = refs[:44]
    outs, (dn, de3, dp_s, ds_s, *pair) = refs[44:44 + moved], refs[44 + moved:]
    c = pl.program_id(0)
    r = pl.program_id(1)
    chunks = pl.num_programs(0)
    last_row = pl.num_programs(1) - 1
    length, wide = long_ref.shape
    n = length // 3
    half = n // 2
    rows = pl.ds(pl.multiple_of(r * length, length), length)
    tables = ((t0, u0), (t3, u3), (t1, u1), (t2, u2))

    @pl.when(r == 0)
    def _():
        ds_s[...] = jnp.zeros_like(ds_s)
        sg_ref[...] = jnp.zeros_like(sg_ref)

    @pl.when(jnp.logical_and(c == 0, r == 0))
    def _():
        dn[...] = jnp.zeros_like(dn)
        de3[...] = jnp.zeros_like(de3)
        vec_ref[...] = jnp.zeros_like(vec_ref)

    core = ("rows", 0)
    jobs = []
    if links:
        pair_s, pair_got, pair_send, pair_recv = pair[:4]
        rest = list(pair[4:])
        for (alive, order), grad, out in zip(plan, grads, outs):
            m = len(order)
            jobs.append(Halving(grad, (0, grad.shape[alive.index(None)]), alive, order, rest[:2 * m - 1] + [out] + rest[2 * m - 1:2 * m + 1],
                rest[2 * m + 1]))
            rest = rest[2 * m + 2:]

        def pair_copy(k):
            mine, there = partner(core)
            slot = lax.rem(k, 2)
            return pltpu.make_async_remote_copy(
                src_ref=pair_s.at[1 - mine], dst_ref=pair_got.at[slot], send_sem=pair_send, recv_sem=pair_recv.at[slot],
                device_id=there, device_id_type=MESH)

        def pair_finish(k):
            pair_copy(k).wait()
            mine, _ = partner(core)
            slot = lax.rem(k, 2)
            for i in range(3):
                for h in range(wide // LANES):
                    wgrad_ref[i, k * (wide // LANES) + h] = (
                        pair_s[mine, i, h].astype(f32) + pair_got[slot, i, h].astype(f32)).astype(bf)

        step = c * pl.num_programs(1) + r

        def advance(when, stage):
            @pl.when(step == when)
            def _():
                for job in jobs:
                    if stage > 0:
                        job.finish(stage - 1)
                    if stage < len(job.order):
                        job.start(stage)

        @pl.when(step == 0)
        def _():
            meet([core] + list(dict.fromkeys(s for _, order in plan for s in order)))

        for stage, when in enumerate(MOMENTS[:-1]):
            advance(when, stage)

    def add(off, v):
        ds_s[off:off + v.shape[0], :] += v

    edge, one, two = token_masks(seg_ref[pl.ds(r, 1), :], length, wide)
    dm = nt(dat_ref[rows, :], wo_ref[...])
    gate_out = mixed_ref[0].astype(f32)
    gate_in = mixed_ref[1].astype(f32)
    value = mixed_ref[2].astype(f32)
    d_gate = dm * long_ref[...].astype(f32)
    d_long = dm * gate_out
    sg_ref[0, 5:6, :] += sum0(d_long * (value * gate_in))
    d_conv = None
    for d in range(DOCS):
        x = jnp.where(edge, d_long, 0.0) if d == 0 else jnp.where(edge, 0.0, d_long)
        ys = spread(x[0:n], x[n:2 * n], x[2 * n:])
        parts = []
        for s, off, m in specs_of(length, n):
            t, u = tables[s]
            g = nn(t[...], ys[s])
            ga, gb = g[:m], g[m:]
            qa, qb = spec_ref[off:off + m], spec_ref[off + m:off + 2 * m]
            qc = spec_ref[6 * n:6 * n + m] if s == 0 else qa
            pa, pb = trans_ref[0, d, off:off + m, :].astype(f32), trans_ref[0, d, off + m:off + 2 * m, :].astype(f32)
            back = jnp.concatenate([(ga * qa + gb * qb).astype(bf), (gb * qc - ga * qb).astype(bf)], 0)
            if s == 0:
                add(0, ga * pa)
                add(6 * n, gb * pb)
            else:
                add(off, ga * pa + gb * pb)
            add(off + m, gb * pa - ga * pb)
            parts.append(nn(u[...], back))
        y = jnp.concatenate(gather(*parts), 0)
        d_conv = y if d == 0 else jnp.where(edge, d_conv, y)
    d_inner = skip_ref[pl.ds(pl.multiple_of(c * wide, wide), wide)].reshape(1, wide) * d_long + d_conv * (1.0 / length)
    grads = (d_gate, d_inner * value, d_inner * gate_in)
    for i, (dmx, w, sw) in enumerate(zip(grads, (wg_ref, wi_ref, wv_ref), (swg_ref, swi_ref, swv_ref))):
        a1 = pltpu.roll(jnp.where(one, dmx, 0.0), length - 1, 0)
        a2 = pltpu.roll(jnp.where(two, dmx, 0.0), length - 2, 0)
        dp = (sw[0:1, :] * dmx + sw[1:2, :] * a1 + sw[2:3, :] * a2).astype(bf)
        p = proj_ref[i].astype(f32)
        for k, v in enumerate((p * dmx, p * a1, p * a2, dmx, dp.astype(f32))):
            sg_ref[i, k:k + 1, :] += sum0(v)
        dp_s[i, rows, :] = dp
        dn[rows, :] += nt(dp, w[...])

    @pl.when(r == last_row)
    def _():
        if links:
            @pl.when(c > 0)
            def _():
                pair_finish(c - 1)

        for i in range(3):
            part = nn(nt_ref[...], dp_s[i]).astype(bf)
            for h in range(wide // LANES):
                if links:
                    tall = pair_s.shape[4]
                    for g in range(pair_s.shape[3]):
                        for k in range(2):
                            top = (2 * g + k) * tall
                            pair_s[k, i, h, g] = part[top:top + tall, h * LANES:(h + 1) * LANES]
                else:
                    wgrad_ref[i, c * (wide // LANES) + h] = part[:, h * LANES:(h + 1) * LANES]
        if links:
            pair_copy(c).start()
        first = lax.broadcasted_iota(jnp.int32, (half, wide), 0) == 0
        extra = ds_s[6 * n:6 * n + half]
        ds_s[0:half] = jnp.where(first, 0.5, 1.0) * (ds_s[0:half] + jnp.where(first, 0.0, extra))
        ds_s[half:n] = jnp.where(first, 0.5 * extra, ds_s[half:n])
        parts = [nn(tables[s][1][...], (ds_s[off:off + 2 * m] * (1.0 / length)).astype(bf)) for s, off, m in specs_of(length, n)]
        gk = jnp.concatenate(gather(*parts), 0) * window(length, rate_ref[...])
        gfw_ref[...] = nn(state_ref[6], gk, HI)
        de3[...] += nt(fw_ref[...], gk, HI)

    @pl.when(c == chunks - 1)
    def _():
        step = 256
        g1 = as_row(g1_ref)
        for i in range(length // step):
            part = slice(i * step, (i + 1) * step)
            there = pl.ds(pl.multiple_of(r * length + i * step, step), step)
            xhat, scale = norm_stats(tok_ref[part, :].astype(f32))
            d = dn[there, :]
            gd = d * g1
            a = jnp.mean(gd, axis=-1, keepdims=True)
            b = jnp.mean(gd * xhat, axis=-1, keepdims=True)
            tg_ref[part, :] = (dat_ref[there, :].astype(f32) + scale * (gd - a - xhat * b)).astype(bf)
            vec_ref[0:1, :] += sum0(d * xhat)
            vec_ref[1:2, :] += sum0(d)

    @pl.when(jnp.logical_and(c == chunks - 1, r == last_row))
    def _():
        ones = jnp.ones((8, length), f32)
        flat = lambda v: nt(ones, v, HI)
        g = de3[...] * state_ref[7]
        gsm_ref[0] = flat(g * state_ref[8])
        g = g * column(oo_ref)
        gsm_ref[1] = flat(g)
        gow_ref[...] = nt(state_ref[3], g, HI)
        g = nn(ow_ref[...], g, HI) * state_ref[4]
        gsm_ref[2] = flat(g * state_ref[5])
        g = g * column(io_ref)
        gsm_ref[3] = flat(g)
        giw_ref[...] = nt(state_ref[0], g, HI)
        g = nn(iw_ref[...], g, HI) * state_ref[1]
        gsm_ref[4] = flat(g * state_ref[2])
        g = g * column(eo_ref)
        gsm_ref[5] = flat(g)
        gew_ref[...] = nt(zt_ref[...], g, HI)
        if links:
            pair_finish(c)
            for job in jobs:
                job.finish(len(job.order) - 1)


MOMENTS = (0, 3, 5, 6)


def backward_mixer(links, weg, wrg, dat, tok, segments, g1, wo, longc, mixed, proj, trans, spec, ntr, wm, sw, skip, state, filt, zt, rates,
        tabs, tabst):
    rows_here, length = segments.shape
    total, width = tok.shape
    n = length // 3
    count = width // CHUNK
    ew, eb, eo, iw, ib, io, ow, ob, oo, fw = filt
    hidden = fw.shape[0]
    sds = jax.ShapeDtypeStruct
    plan, grads, moved, scratch = [], [], [], []
    wide_blocks = width // LANES
    wm_shape = (3, wide_blocks, width, LANES)
    if links:
        rows_n, pos_n = links
        alive = [d for d in alive_dims(rows_n, pos_n) if d != ("rows", 0)]
        pair = (3, CHUNK // LANES, rows_n // 2, width // rows_n, LANES)
        wm_shape = (3, wide_blocks, *pair[2:])
        scratch = [pltpu.VMEM((2, *pair), bf), pltpu.VMEM((2, *pair), bf), pltpu.SemaphoreType.DMA, pltpu.SemaphoreType.DMA((2,))]
        for grad, rows_of, first in ((weg, width, "pos"), (wrg, wrg.shape[1] * wrg.shape[2] * wrg.shape[3] * 2, "rows")):
            grad = grad.reshape(grad_shape(grad.shape[0], rows_of, rows_n, pos_n, False))
            order = order_of(rows_n, pos_n, first)[1:-1]
            left = job_shapes(grad.shape, grad.shape[alive.index(None)], alive, order)
            plan.append((alive, order))
            grads.append(grad)
            moved.append(left[-1])
            scratch += job_scratch(left, False) + [pltpu.SemaphoreType.DMA]
    side = dict(collective_id=2, has_side_effects=True) if links else {}
    late = lambda c, r: (jnp.where(c == count - 1, r, 0), 0)
    ins = [*grads, dat, tok, segments, g1, wo, longc, mixed, proj, trans, spec, ntr, wm, wm, wm, sw, sw, sw, skip, state, zt,
        iw, ow, eo, io, oo, fw, rates, *tabs, *tabst]
    specs = [pl.BlockSpec(memory_space=pl.ANY) for g in grads] + [whole_spec(dat), pl.BlockSpec((length, width), late, pipeline_mode=pl.Buffered(1)), whole_spec(segments), whole_spec(g1),
        pl.BlockSpec((CHUNK, width), lambda c, r: (c, 0)), part_spec(length), stack_spec(3, length), stack_spec(3, length),
        pl.BlockSpec((1, DOCS, 2 * length, CHUNK), lambda c, r: (r, 0, 0, c)), column_spec(2 * length + n // 2, 0, count),
        whole_spec(ntr)]
    specs += [column_spec(width, k, count) for k in range(3)] + [column_spec(3, k, count) for k in range(3)]
    specs += [whole_spec(a) for a in (skip, state, zt, iw, ow, eo, io, oo)]
    specs += [column_spec(hidden, 0, count), column_spec(1, 0, count)] + [whole_spec(a) for a in (*tabs, *tabst)]
    return pl.pallas_call(
        functools.partial(backward_kernel, links, plan), grid=(count, rows_here), in_specs=specs,
        out_specs=[pl.BlockSpec((length, width), late, pipeline_mode=pl.Buffered(1)),
            single(*wm_shape),
            pl.BlockSpec((3, 8, CHUNK), lambda c, r: (0, 0, c)), fixed_spec(8, width), fixed_spec(zt.shape[0], hidden),
            fixed_spec(hidden, hidden), fixed_spec(hidden, hidden), column_spec(hidden, 0, count), fixed_spec(6, 8, hidden)]
            + [single(*s) for s in moved],
        out_shape=[sds((total, width), bf), sds(wm_shape, bf), sds((3, 8, width), f32),
            sds((8, width), f32), sds((zt.shape[0], hidden), f32), sds((hidden, hidden), f32), sds((hidden, hidden), f32),
            sds((hidden, width), f32), sds((6, 8, hidden), f32)]
            + [sds(s, bf) for s in moved],
        scratch_shapes=[pltpu.VMEM((total, width), f32), pltpu.VMEM((hidden, length), f32), pltpu.VMEM((3, total, CHUNK), bf),
            pltpu.VMEM((6 * n + n // 2, CHUNK), f32)] + scratch,
        compiler_params=pltpu.CompilerParams(vmem_limit_bytes=VMEM_BYTES, **side),
        cost_estimate=pl.CostEstimate(
            flops=total * width * (14 * width + 4 * 2 * 5 * n), bytes_accessed=50 * total * width, transcendentals=0),
        name="mixer_backward")(*ins)


def scatter_blocks(grad, rows_n, pos_n, first):
    blocks, height, wide = grad.shape
    if blocks % pos_n:
        flat = grad.transpose(1, 0, 2).reshape(height, blocks * wide)
        wide = blocks * wide // pos_n
        blocks = pos_n
        grad = flat.reshape(height, blocks, wide).transpose(1, 0, 2)
    high = height // rows_n
    rbits, pbits = bits_of(rows_n), bits_of(pos_n)
    acc = grad.reshape((2,) * pbits + (blocks // pos_n,) + (2,) * rbits + (high, wide))
    alive = alive_dims(rows_n, pos_n)
    for axis, bit in order_of(rows_n, pos_n, first):
        dim = alive.index((axis, bit))
        mine = (lax.axis_index(axis) >> bit) & 1
        size = rows_n if axis == "rows" else pos_n
        send = lax.dynamic_index_in_dim(acc, 1 - mine, dim, keepdims=False)
        keep = lax.dynamic_index_in_dim(acc, mine, dim, keepdims=False)
        got = lax.ppermute(send, axis, [(i, i ^ (1 << bit)) for i in range(size)])
        acc = (keep.astype(f32) + got.astype(f32)).astype(bf)
        alive.pop(dim)
    return acc


def pack_places(width, hidden, emb, ff):
    per = width // PACK
    at = {"filter": 0, "square": hidden * per}
    row = at["square"] + hidden
    for name, vectors in (("vec1", 2), ("vec2", 4), ("sgrad", 15), ("skip", 1), ("ebias", ff // width)):
        at[name] = row
        row += vectors * per
    at["small"] = row
    return at, row + 6


def pack_small(at, pk, beg, vec2, sgrad, vec1, gew, giw, gow, gfw, gsm):
    width = vec1.shape[1]
    hidden = giw.shape[0]
    per = width // PACK

    def put(row, value):
        for h in range(per):
            pk[row + h:row + h + 1, :] = value[:, h * PACK:(h + 1) * PACK]

    for k in range(beg.shape[1] // width):
        put(at["ebias"] + k * per, beg[:, k * width:(k + 1) * width])
    for k in range(4):
        put(at["vec2"] + k * per, vec2[k:k + 1, :])
    for i in range(3):
        for k in range(5):
            put(at["sgrad"] + (i * 5 + k) * per, sgrad[i, k:k + 1, :])
    put(at["skip"], sgrad[0, 5:6, :])
    for k in range(2):
        put(at["vec1"] + k * per, vec1[k:k + 1, :])
    for lane, ref in ((0, gew), (128, giw), (256, gow)):
        high = min(ref.shape[0], hidden)
        pk[at["square"]:at["square"] + high, lane:lane + hidden] = ref[0:high, :]
    for h in range(per):
        pk[at["filter"] + h * hidden:at["filter"] + (h + 1) * hidden, :] = gfw[:, h * PACK:(h + 1) * PACK]
    for k in range(6):
        pk[at["small"] + k:at["small"] + k + 1, 0:hidden] = gsm[k, 0:1, :]


def exchange_kernel(sizes, at, plan, count, *refs):
    rows_n, pos_n = sizes
    n = rows_n * pos_n
    small = refs[:9]
    grads = refs[9:9 + count]
    pos = 9 + count
    packed_out = refs[pos]
    outs = refs[pos + 1:pos + 1 + len(plan)]
    scratch = list(refs[pos + 1 + len(plan):])
    pk, rbuf, red, gath, ss1, rs1, ss2, rs2 = scratch[:8]
    rest = scratch[8:]
    jobs = []
    for (src, blocks, alive, order), out in zip(plan, outs):
        m = len(order)
        jobs.append(Halving(grads[src], blocks, alive, order, rest[:2 * m - 1] + [out] + rest[2 * m - 1:2 * m + 1]))
        rest = rest[2 * m + 1:]
    me = lax.axis_index("rows") * pos_n + lax.axis_index("pos")
    chunk = pk.shape[0] // n

    def ident(t):
        return {"rows": t // pos_n, "pos": t % pos_n}

    def each(f):
        def body(k, carry):
            f(lax.rem(me + k, n))
            return carry

        lax.fori_loop(1, n, body, 0)

    def part(t):
        return pl.ds(pl.multiple_of(t * chunk, chunk), chunk)

    barrier = pltpu.get_barrier_semaphore()
    each(lambda t: pl.semaphore_signal(barrier, inc=1, device_id=ident(t), device_id_type=MESH))
    pk[...] = jnp.zeros_like(pk)
    pack_small(at, pk, *small)
    pl.semaphore_wait(barrier, n - 1)

    def scatter(t, slot):
        return pltpu.make_async_remote_copy(
            src_ref=pk.at[part(t), :], dst_ref=rbuf.at[slot], send_sem=ss1.at[t], recv_sem=rs1.at[slot], device_id=ident(t),
            device_id_type=MESH)

    def publish(t, slot):
        return pltpu.make_async_remote_copy(
            src_ref=red, dst_ref=gath.at[part(slot), :], send_sem=ss2.at[t], recv_sem=rs2.at[slot], device_id=ident(t),
            device_id_type=MESH)

    for job in jobs:
        job.start(0)
    each(lambda t: scatter(t, me).start())
    rbuf[me] = pk[part(me), :]
    stages = max(len(job.order) for job in jobs)
    for stage in range(stages):
        for job in jobs:
            if stage < len(job.order):
                job.finish(stage)
                if stage + 1 < len(job.order):
                    job.start(stage + 1)
        if stage == 0:
            each(lambda t: scatter(t, t).wait())
            total = rbuf[0]
            for s in range(1, n):
                total = total + rbuf[s]
            red[...] = total
            gath[part(me), :] = total
            each(lambda t: publish(t, me).start())
    each(lambda t: publish(t, t).wait())
    packed_out[...] = gath[...]


def exchange(sizes, at, used, small, grads, plan):
    rows_n, pos_n = sizes
    n = rows_n * pos_n
    total = -(-used // (8 * n)) * 8 * n
    chunk = total // n
    vm = pl.BlockSpec(memory_space=pltpu.VMEM)
    scratch = [pltpu.VMEM((total, PACK), f32), pltpu.VMEM((n, chunk, PACK), f32), pltpu.VMEM((chunk, PACK), f32),
        pltpu.VMEM((total, PACK), f32)] + [pltpu.SemaphoreType.DMA((n,))] * 4
    shapes = [jax.ShapeDtypeStruct((total, PACK), f32)]
    for src, (start, blocks), alive, order in plan:
        left = job_shapes(grads[src].shape, blocks, alive, order)
        shapes.append(jax.ShapeDtypeStruct(left[-1], bf))
        scratch += job_scratch(left, False)
    return pl.pallas_call(
        functools.partial(exchange_kernel, sizes, at, plan, len(grads)), out_shape=shapes,
        in_specs=[vm] * (9 + len(grads)), out_specs=[vm] * len(shapes), scratch_shapes=scratch,
        compiler_params=pltpu.CompilerParams(collective_id=0, has_side_effects=True, vmem_limit_bytes=VMEM_BYTES),
        name="exchange")(*small, *grads)


def unpack(at, packed, blocks, width, hidden, emb, ff):
    per = width // PACK
    counts = [len(parts) for parts in blocks]
    flat = [p for parts in blocks for p in parts]

    def kernel(pk, *refs):
        ins = list(refs[:len(flat)])
        fg, fs, mb, sw, sb, ew, eb, eo, iw, ib, io, ow, ob, oo, fw, sk, obias, sg, ss, eb2, rb = refs[len(flat):len(flat) + 21]
        outs = refs[len(flat) + 21:]

        def get(ref, lane, row):
            for h in range(per):
                ref[lane + h * PACK:lane + (h + 1) * PACK] = pk[row + h, :]

        get(fg, 0, at["vec1"])
        get(fs, 0, at["vec1"] + per)
        for i in range(3):
            base = at["sgrad"] + i * 5 * per
            for k in range(3):
                for h in range(per):
                    lane = i * width + h * PACK
                    sw[k:k + 1, lane:lane + PACK] = pk[base + k * per + h:base + k * per + h + 1, :]
            get(sb, i * width, base + 3 * per)
            get(mb, i * width, base + 4 * per)
        q = at["square"]
        ew[...] = pk[q:q + emb, 0:hidden]
        iw[...] = pk[q:q + hidden, 128:128 + hidden]
        ow[...] = pk[q:q + hidden, 256:256 + hidden]
        for k, ref in enumerate((oo, ob, io, ib, eo, eb)):
            ref[...] = pk[at["small"] + k, 0:hidden]
        for h in range(per):
            fw[:, h * PACK:(h + 1) * PACK] = pk[at["filter"] + h * hidden:at["filter"] + (h + 1) * hidden, :]
        get(sk, 0, at["skip"])
        for k, ref in enumerate((sg, ss, obias, rb)):
            get(ref, 0, at["vec2"] + k * per)
        for k in range(ff // width):
            get(eb2, k * width, at["ebias"] + k * per)
        for parts, out in zip(counts, outs):
            lane = 0
            for _ in range(parts):
                src = ins.pop(0)
                for b in range(src.shape[0]):
                    out[:, lane:lane + src.shape[2]] = src[b].astype(f32)
                    lane += src.shape[2]

    s = lambda *d: jax.ShapeDtypeStruct(d, f32)
    shapes = [s(width), s(width), s(3 * width), s(3, 3 * width), s(3 * width), s(emb, hidden), s(hidden), s(hidden),
        s(hidden, hidden), s(hidden), s(hidden), s(hidden, hidden), s(hidden), s(hidden), s(hidden, width), s(width), s(width),
        s(width), s(width), s(ff), s(width)]
    shapes += [s(parts[0].shape[1], sum(p.shape[0] for p in parts) * parts[0].shape[2]) for parts in blocks]
    vm = pl.BlockSpec(memory_space=pltpu.VMEM)
    return pl.pallas_call(
        kernel, out_shape=shapes, in_specs=[vm] * (1 + len(flat)), out_specs=[vm] * len(shapes), name="unpack")(packed, *flat)


def on_device(sizes, tokens, segments, cotangent, first_gain, first_shift, mixer_weight, mixer_bias, short_weight, short_bias,
        embed_weight, embed_bias, embed_omega, inner_weight, inner_bias, inner_omega, outer_weight, outer_bias, outer_omega,
        filter_weight, skip_gain, output_weight, output_bias, second_gain, second_shift, expand_weight, expand_bias,
        reduce_weight, reduce_bias):
    rows_n, pos_n = sizes
    length, width = tokens.shape[1:]
    emb, hidden = embed_weight.shape
    ff = expand_weight.shape[1]
    tok = tokens.reshape(-1, width)
    cot = cotangent.reshape(-1, width)
    filt = [embed_weight, embed_bias, embed_omega, inner_weight, inner_bias, inner_omega, outer_weight, outer_bias, outer_omega,
        filter_weight]
    tabs, tabst = radix_tables(length)
    zt, rates = filter_inputs(length, emb, width)
    proj, mixed, longc, mix, trans, spec, state, ntr = forward_mixer(
        tok, segments, first_gain, first_shift, mixer_weight, mixer_bias, short_weight, short_bias, skip_gain, filt, zt, rates,
        tabs, tabst)
    direct = rows_n * pos_n <= 32 and width % (16 * rows_n) == 0 and width // LANES % pos_n == 0 and ff // rows_n * 4 == width
    links = sizes if direct else None
    out, dat, wog, weg, wrg, beg, vec2 = mlp(
        links, mix, tok, cot, output_weight, output_bias, second_gain, second_shift, expand_weight, expand_bias, reduce_weight,
        reduce_bias)
    tgrad, wmg, sgrad, vec1, gew, giw, gow, gfw, gsm, *early = backward_mixer(
        links, weg, wrg, dat, tok, segments, first_gain, output_weight, longc, mixed, proj, trans, spec, ntr, mixer_weight,
        short_weight, skip_gain, state, filt, zt, rates, tabs, tabst)
    small = (beg, vec2, sgrad, vec1, gew, giw, gow, gfw, gsm)
    at, used = pack_places(width, hidden, emb, ff)
    blocks_m, blocks_o = 3 * width // LANES, width // LANES
    if direct:
        alive = alive_dims(rows_n, pos_n)
        core = [("rows", 0)]
        paired = [d for d in alive if d not in core]
        by_pos, by_rows = order_of(rows_n, pos_n, "pos"), order_of(rows_n, pos_n, "rows")
        half_m = blocks_m // pos_n
        cut = (half_m + 1) // 2
        grads = [wmg.reshape(grad_shape(blocks_m, width, rows_n, pos_n, False)),
            wog.reshape(grad_shape(blocks_o, width, rows_n, pos_n, True)), *early]
        left = [d for d in alive if d is None or d in by_pos[-1:]]
        plan = [(0, (0, cut), paired, by_pos[1:]), (0, (cut, half_m - cut), paired, by_rows[1:]),
            (1, (0, blocks_o // pos_n), alive, by_rows), (2, (0, early[0].shape[0]), left, by_pos[-1:]),
            (3, (0, early[1].shape[0]), left, by_pos[-1:])]
        packed, m_a, m_b, o_part, e_part, r_part = exchange(sizes, at, used, small, grads, plan)
        blocks = [[m_a, m_b], [o_part], [e_part], [r_part]]
    else:
        packed = lax.psum(pack_only(at, used, small), ("rows", "pos"))
        grads = [wmg.reshape(blocks_m, width, LANES), wog, weg, wrg]
        blocks = [[scatter_blocks(g, rows_n, pos_n, f)] for g, f in zip(grads, ("pos", "rows", "pos", "rows"))]
    (fg, fs, mb, sw, sb, ew, eb, eo, iw, ib, io, ow, ob, oo, fw, sk, obias, sg, ss, eb2, rb, m_grad, o_grad, e_grad, r_grad) = unpack(
        at, packed, blocks, width, hidden, emb, ff)
    return (out.reshape(tokens.shape), tgrad.reshape(tokens.shape), fg, fs, m_grad, mb, sw, sb, ew, eb, eo, iw, ib, io, ow, ob,
        oo, fw, sk, o_grad, obias, sg, ss, e_grad, eb2, r_grad, rb)


def pack_only(at, used, small):
    def kernel(*refs):
        refs[-1][...] = jnp.zeros_like(refs[-1])
        pack_small(at, refs[-1], *refs[:-1])

    vm = pl.BlockSpec(memory_space=pltpu.VMEM)
    return pl.pallas_call(
        kernel, out_shape=jax.ShapeDtypeStruct((used, PACK), f32), in_specs=[vm] * len(small), out_specs=vm, name="pack")(*small)


def solution(mesh):
    both = ("rows", "pos")
    split = P(both, None, None)
    grid = P("rows", "pos")
    in_specs = (split, P(both, None), split) + (P(),) * 25
    out_specs = (split, split, P(), P(), grid) + (P(),) * 14 + (grid, P(), P(), P(), grid, P(), grid, P())
    sizes = (mesh.shape["rows"], mesh.shape["pos"])
    return jax.shard_map(
        functools.partial(on_device, sizes), mesh=mesh, in_specs=in_specs, out_specs=out_specs, check_vma=False)
```

```python
import functools
import math

import jax
import jax.numpy as jnp
import numpy as np
from jax import lax
from jax.experimental import pallas as pl
from jax.experimental.pallas import tpu as pltpu
from jax.sharding import PartitionSpec as P

f32 = jnp.float32
bf = jnp.bfloat16
HI = lax.Precision.HIGHEST
MESH = pl.DeviceIdType.MESH
DOCS = 2
EPSILON = 1e-5
ROOT3 = math.sqrt(3.0) / 2
LANES = 128
CHUNK = 256
PACK = 384
VMEM_BYTES = 63 * 2**20


def nt(a, b, precision=None):
    return lax.dot_general(a, b, (((1,), (1,)), ((), ())), precision=precision, preferred_element_type=f32)


def nn(a, b, precision=None):
    return lax.dot_general(a, b, (((1,), (0,)), ((), ())), precision=precision, preferred_element_type=f32)


def tn(a, b, precision=None):
    return lax.dot_general(a, b, (((0,), (0,)), ((), ())), precision=precision, preferred_element_type=f32)


def three_pass(dot, a, b):
    ah, bh = a.astype(bf), b.astype(bf)
    al, bl = (a - ah.astype(f32)).astype(bf), (b - bh.astype(f32)).astype(bf)
    return dot(ah, bh) + dot(ah, bl) + dot(al, bh)


def norm_stats(x):
    mean = jnp.mean(x, axis=-1, keepdims=True)
    centered = x - mean
    variance = jnp.mean(centered * centered, axis=-1, keepdims=True)
    scale = lax.rsqrt(variance + EPSILON)
    return centered * scale, scale


def sum0(v):
    return jnp.sum(v, axis=0, keepdims=True)


def as_row(ref):
    return ref[...].reshape(1, -1)


def radix_tables(length):
    n = length // 3
    m = 2 * length
    place = np.arange(n)

    def angle(freqs):
        return 2 * np.pi * ((freqs[:, None] * place[None, :]) % m) / m

    even = angle(6 * np.arange(n // 2))
    sine = np.sin(even)
    sine[0] = np.cos(np.pi * place)
    odd = angle(6 * np.arange(n // 2) + 3)
    out = [np.concatenate([np.cos(even), sine], 0), np.concatenate([np.cos(odd), np.sin(odd)], 0)]
    for k in (1, 2):
        turn = angle(6 * np.arange(n) + k)
        c, s = np.cos(turn), np.sin(turn)
        out.append(np.block([[c, -s], [s, c]]))
    low = lambda v: jnp.asarray(v.astype(np.float32)).astype(bf)
    return [low(t) for t in out], [low(t.T) for t in out]


def spread(x0, x1, x2):
    s = x1 + x2
    d = x1 - x2
    y0 = (x0 + s).astype(bf)
    y3 = (x0 - d).astype(bf)
    y1 = jnp.concatenate([(x0 + 0.5 * d).astype(bf), (ROOT3 * s).astype(bf)], 0)
    y2 = jnp.concatenate([(x0 - 0.5 * s).astype(bf), (ROOT3 * d).astype(bf)], 0)
    return y0, y3, y1, y2


def gather(v0, v3, v1, v2):
    n = v0.shape[0]
    v1r, v1i, v2r, v2i = v1[:n], v1[n:], v2[:n], v2[n:]
    even = v0 + v3
    a = 0.5 * (v1r - v2r)
    b = ROOT3 * (v1i + v2i)
    x0 = even + v1r + v2r
    x1 = (v0 - v3) + a + b
    x2 = even - 0.5 * (v1r + v2r) + ROOT3 * (v1i - v2i)
    return x0, x1, x2


def filter_inputs(length, emb, width):
    bands_count = (emb - 1) // 2
    places = np.arange(length, dtype=np.float32)
    tnorm = places / np.float32(length - 1)
    wave = places * np.float32(2.0 * math.pi / length)
    bands = np.linspace(0.0001, bands_count - 1, bands_count).astype(np.float32)
    phase = (wave[:, None] * bands[None, :]).astype(np.float32)
    z = np.concatenate([tnorm[:, None], np.cos(phase), -np.sin(phase)], 1).astype(np.float32)
    zt = np.concatenate([z.T, np.zeros(((-emb) % 8, length), np.float32)], 0)
    rates = np.abs(np.linspace(math.log(0.01) / 1.5, math.log(0.01) / 0.3, width)).astype(np.float32)[None, :]
    return jnp.asarray(zt), jnp.asarray(rates)


def window(length, rate):
    tnorm = lax.broadcasted_iota(jnp.int32, (length, rate.shape[1]), 0).astype(f32) * (1.0 / (length - 1))
    return jnp.exp(-tnorm * rate)


def sin_cos(x):
    k = jnp.floor(x * (1.0 / math.pi) + 0.5)
    r = x - k * 3.140625
    r = r - k * 0.0009670257568359375
    r = r - k * 6.2771141529083251953e-07
    sign = 1.0 - 2.0 * (k - 2.0 * jnp.floor(k * 0.5))
    q = r * r
    s = 1.0 + q * (-1 / 6 + q * (1 / 120 + q * (-1 / 5040 + q * (1 / 362880 + q * (-1 / 39916800 + q * (1 / 6227020800))))))
    c = 1.0 + q * (-1 / 2 + q * (1 / 24 + q * (-1 / 720 + q * (1 / 40320 + q * (-1 / 3628800 + q * (1 / 479001600 - q * (1 / 87178291200)))))))
    return r * s * sign, c * sign


def column(ref):
    v = as_row(ref)
    n = v.shape[1]
    i = lax.broadcasted_iota(jnp.int32, (n, n), 0)
    j = lax.broadcasted_iota(jnp.int32, (n, n), 1)
    return jnp.sum(jnp.where(i == j, v, 0.0), axis=1, keepdims=True)


def token_masks(seg, length, wide):
    edge = jnp.sum((seg == 0).astype(jnp.int32), axis=1, keepdims=True)
    t = lax.broadcasted_iota(jnp.int32, (length, wide), 0)
    one = jnp.logical_and(t != 0, t != edge)
    two = jnp.logical_and(jnp.logical_and(one, t != 1), t != edge + 1)
    return t < edge, one, two


def interleave(streams, lag=1):
    streams = list(streams)
    waiting = [lag * k for k in range(len(streams))]
    while streams:
        for k in range(len(streams)):
            if waiting[k] > 0:
                waiting[k] -= 1
            elif next(streams[k], streams) is streams:
                waiting[k] = None
        streams, waiting = [s for s, w in zip(streams, waiting) if w is not None], [w for w in waiting if w is not None]


def specs_of(length, n):
    return ((0, 0, n // 2), (1, n, n // 2), (2, 2 * n, n), (3, 4 * n, n))


def bits_of(n):
    return n.bit_length() - 1


def order_of(rows_n, pos_n, first):
    rows = [("rows", b) for b in range(1, bits_of(rows_n))]
    pos = [("pos", b) for b in range(bits_of(pos_n))]
    return [("rows", 0)] + (pos + rows if first == "pos" else rows[:1] + pos + rows[1:])


def three_orders(rows_n, pos_n):
    pos = [("pos", b) for b in range(bits_of(pos_n))]
    near = [("rows", b) for b in range(1, bits_of(rows_n) - 1)]
    far = [("rows", bits_of(rows_n) - 1)]
    ring = pos + near
    turn = lambda k: ring[k:] + ring[:k]
    return turn(0) + far, turn(len(pos)) + far, turn(len(ring) - 1) + far


def alive_dims(rows_n, pos_n):
    pos = [("pos", b) for b in reversed(range(bits_of(pos_n)))]
    return pos + [None] + [("rows", b) for b in reversed(range(bits_of(rows_n)))]


def partner(step):
    axis, bit = step
    place = lax.axis_index(axis)
    mine = (place // (1 << bit)) % 2
    return mine, {axis: place + (1 - 2 * mine) * (1 << bit)}


def meet(steps):
    barrier = pltpu.get_barrier_semaphore()
    for step in steps:
        pl.semaphore_signal(barrier, inc=1, device_id=partner(step)[1], device_id_type=MESH)
    pl.semaphore_wait(barrier, len(steps))


class Halving:
    def __init__(self, ref, blocks, alive, order, refs, near=None):
        m = len(order)
        self.near = near
        got, sums, self.send_sem, self.recv_sem = refs[:m], refs[m:2 * m], refs[2 * m], refs[2 * m + 1]
        self.order, self.got, self.sums = order, got, sums
        self.stages = []
        alive = list(alive)
        for k, step in enumerate(order):
            self.stages.append((ref, blocks, tuple(alive), alive.index(step)))
            alive.remove(step)
            ref, blocks = sums[k], (0, blocks[1])

    def pick(self, stage, which):
        ref, (start, count), alive, dim = self.stages[stage]
        index = [slice(None)] * len(alive)
        index[alive.index(None)] = pl.ds(start, count)
        index[dim] = which
        return ref.at[tuple(index)]

    def copy(self, stage):
        mine, there = partner(self.order[stage])
        return pltpu.make_async_remote_copy(
            src_ref=self.pick(stage, 1 - mine), dst_ref=self.got[stage], send_sem=self.send_sem.at[stage],
            recv_sem=self.recv_sem.at[stage], device_id=there, device_id_type=MESH)

    def fetch(self):
        return pltpu.make_async_copy(self.pick(0, partner(self.order[0])[0]), self.sums[0], self.near)

    def start(self, stage):
        self.copy(stage).start()
        if stage == 0 and self.near is not None:
            self.fetch().start()

    def finish(self, stage):
        self.copy(stage).wait()
        if stage == 0 and self.near is not None:
            self.fetch().wait()
        _, (_, count), alive, dim = self.stages[stage]
        kept, got, out = self.pick(stage, partner(self.order[stage])[0]), self.got[stage], self.sums[stage]
        if stage == 0 and self.near is not None:
            kept = out
        split = [d for k, d in enumerate(alive) if k != dim].index(None)

        def add(lead):
            def body(b, carry):
                at = lead + (b,)
                out[at] = (kept[at].astype(f32) + got[at].astype(f32)).astype(bf)
                return carry

            lax.fori_loop(0, count, body, 0)

        leads = [()]
        for _ in range(split):
            leads = [lead + (k,) for lead in leads for k in range(2)]
        for lead in leads:
            add(lead)


def job_shapes(shape, blocks, alive, order):
    dims = list(alive)
    now = [blocks if d is None else 2 for d in dims] + list(shape[-2:])
    out = []
    for step in order:
        k = dims.index(step)
        dims.pop(k)
        now.pop(k)
        out.append(tuple(now))
    return out


def job_scratch(left, last):
    sums = left if last else left[:-1]
    return [pltpu.VMEM(s, bf) for s in left] + [pltpu.VMEM(s, bf) for s in sums] + [pltpu.SemaphoreType.DMA((len(left),))] * 2


def grad_shape(blocks, rows, rows_n, pos_n, cores):
    rbits, pbits = bits_of(rows_n), bits_of(pos_n)
    return (2,) * pbits + (blocks // pos_n,) + (2,) * (rbits - (0 if cores else 1)) + (rows // rows_n, LANES)


def forward_kernel(tok_ref, seg_ref, g1_ref, s1_ref, wg_ref, wi_ref, wv_ref, mb_ref, swg_ref, swi_ref, swv_ref, sb_ref,
        skip_ref, zt_ref, ew_ref, eb_ref, eo_ref, iw_ref, ib_ref, io_ref, ow_ref, ob_ref, oo_ref, fw_ref, rate_ref,
        t0, t3, t1, t2, u0, u3, u1, u2,
        proj_ref, mixed_ref, long_ref, mix_ref, trans_ref, low_ref, state_ref, nt_ref, normed, padded, spec_ref):
    c = pl.program_id(0)
    rows_here, length = seg_ref.shape
    width = tok_ref.shape[1]
    n = length // 3
    half = n // 2
    wide = fw_ref.shape[1]
    tables = ((t0, u0), (t3, u3), (t1, u1), (t2, u2))

    @pl.when(c == 0)
    def _():
        step = 256
        for i in range(tok_ref.shape[0] // step):
            part = slice(i * step, (i + 1) * step)
            xhat, _ = norm_stats(tok_ref[part, :].astype(f32))
            low = (xhat * as_row(g1_ref) + as_row(s1_ref)).astype(bf)
            normed[part, :] = low
            nt_ref[:, part] = low.T

    @pl.when(c == 0)
    def _():
        padded[...] = jnp.zeros_like(padded)
        padded[0:ew_ref.shape[0], :] = ew_ref[...]
        pre = tn(padded[...], zt_ref[...], HI) + column(eb_ref)
        e1, c1 = sin_cos(column(eo_ref) * pre)
        state_ref[0] = e1
        state_ref[1] = c1
        state_ref[2] = pre
        pre = tn(iw_ref[...], e1, HI) + column(ib_ref)
        e2, c2 = sin_cos(column(io_ref) * pre)
        state_ref[3] = e2
        state_ref[4] = c2
        state_ref[5] = pre
        pre = tn(ow_ref[...], e2, HI) + column(ob_ref)
        e3, c3 = sin_cos(column(oo_ref) * pre)
        state_ref[6] = e3
        state_ref[7] = c3
        state_ref[8] = pre

    def spectrum():
        kernel = three_pass(tn, state_ref[6], fw_ref[...]) * window(length, rate_ref[...])
        k = kernel.astype(bf).astype(f32)
        y0, y3, y1, y2 = spread(k[0:n], k[n:2 * n], k[2 * n:])
        yield
        first = lax.broadcasted_iota(jnp.int32, (half, wide), 0) == 0
        q0 = nn(t0[...], y0)
        spec_ref[0:half] = q0[0:half] * jnp.where(first, 0.5, 1.0)
        spec_ref[half:n] = jnp.where(first, 0.0, q0[half:])
        spec_ref[6 * n:6 * n + half] = jnp.where(first, 0.5 * q0[half:], q0[0:half])
        spec_ref[n:2 * n] = nn(t3[...], y3)
        yield
        spec_ref[2 * n:4 * n] = nn(t1[...], y1)
        spec_ref[4 * n:6 * n] = nn(t2[...], y2)
        yield
        low_ref[...] = spec_ref[...].astype(bf)

    mixed = [[None] * 3 for _ in range(rows_here)]
    inner = [None] * rows_here
    masks = [token_masks(seg_ref[r:r + 1, :], length, wide) for r in range(rows_here)]

    def project(r):
        rows = slice(r * length, (r + 1) * length)
        edge, one, two = masks[r]
        for i, (w, sw) in enumerate(((wg_ref, swg_ref), (wi_ref, swi_ref), (wv_ref, swv_ref))):
            at = pl.ds(pl.multiple_of(i * width + c * wide, wide), wide)
            p = nn(normed[rows, :], w[...]) + mb_ref[at].reshape(1, wide)
            yield
            proj_ref[i, rows, :] = p.astype(bf)
            m = (sb_ref[at].reshape(1, wide) + sw[0:1, :] * p + sw[1:2, :] * jnp.where(one, pltpu.roll(p, 1, 0), 0.0)
                + sw[2:3, :] * jnp.where(two, pltpu.roll(p, 2, 0), 0.0))
            mixed_ref[i, rows, :] = m.astype(bf)
            mixed[r][i] = m
        inner[r] = mixed[r][2] * mixed[r][1]

    def convolve(r):
        rows = slice(r * length, (r + 1) * length)
        edge = masks[r][0]
        inner_low = inner[r].astype(bf).astype(f32)
        xs = [jnp.where(edge, inner_low, 0.0), jnp.where(edge, 0.0, inner_low)]
        ys = [jnp.concatenate(pair_of, 1) for pair_of in zip(*(spread(x[0:n], x[n:2 * n], x[2 * n:]) for x in xs))]
        parts = {}
        for s, off, m in specs_of(length, n)[::-1]:
            t, u = tables[s]
            p = nn(t[...], ys[s])
            yield
            qa, qb = spec_ref[off:off + m], spec_ref[off + m:off + 2 * m]
            qc = spec_ref[6 * n:6 * n + m] if s == 0 else qa
            prod = []
            for d in range(DOCS):
                mine = p[:, d * wide:(d + 1) * wide]
                trans_ref[r, d, off:off + 2 * m, :] = mine.astype(bf)
                pa, pb = mine[:m], mine[m:]
                prod.append(jnp.concatenate([(pa * qa - pb * qb).astype(bf), (pa * qb + pb * qc).astype(bf)], 0))
            parts[s] = nn(u[...], jnp.concatenate(prod, 1))
            yield
        y = jnp.concatenate(gather(*(parts[s] for s in range(4))), 0)
        conv = jnp.where(edge, y[:, :wide], y[:, wide:])
        longconv = conv * (1.0 / length) + skip_ref[pl.ds(pl.multiple_of(c * wide, wide), wide)].reshape(1, wide) * inner[r]
        long_ref[rows, :] = longconv.astype(bf)
        mix_ref[rows, :] = (mixed[r][0] * longconv).astype(bf)

    def row_stream(r):
        yield from project(r)
        yield from convolve(r)

    interleave([spectrum()] + [row_stream(r) for r in range(rows_here)], LAG)


LAG = 2


def whole_spec(a):
    return pl.BlockSpec(a.shape, lambda *_: (0,) * a.ndim, pipeline_mode=pl.Buffered(1))


def fixed_spec(*shape):
    return pl.BlockSpec(shape, lambda *_: (0,) * len(shape))


def column_spec(rows, k, count):
    return pl.BlockSpec((rows, CHUNK), lambda c, r=0: (0, k * count + c))


def part_spec(length):
    return pl.BlockSpec((length, CHUNK), lambda c, r=0: (r, c))


def stack_spec(count, length):
    return pl.BlockSpec((count, length, CHUNK), lambda c, r=0: (0, r, c))


def vector_chunk():
    return pl.BlockSpec((CHUNK,), lambda c, r: (c,))


def forward_mixer(tok, segments, g1, s1, wm, mb, sw, sb, skip, filt, zt, rates, tabs, tabst):
    rows_here, length = segments.shape
    total, width = tok.shape
    n = length // 3
    count = width // CHUNK
    fw = filt[-1]
    hidden = fw.shape[0]
    sds = jax.ShapeDtypeStruct
    ins = [tok, segments, g1, s1, wm, wm, wm, mb, sw, sw, sw, sb, skip, zt, *filt, rates, *tabs, *tabst]
    specs = [whole_spec(a) for a in (tok, segments, g1, s1)]
    specs += [column_spec(width, k, count) for k in range(3)] + [whole_spec(mb)] + [column_spec(3, k, count) for k in range(3)]
    specs += [whole_spec(sb), whole_spec(skip), whole_spec(zt)] + [whole_spec(a) for a in filt[:-1]]
    specs += [column_spec(hidden, 0, count), column_spec(1, 0, count)] + [whole_spec(a) for a in (*tabs, *tabst)]
    return pl.pallas_call(
        forward_kernel, grid=(count,), in_specs=specs,
        out_specs=[stack_spec(3, total), stack_spec(3, total), part_spec(total), part_spec(total),
            pl.BlockSpec((rows_here, DOCS, 2 * length, CHUNK), lambda c: (0, 0, 0, c)), column_spec(2 * length + n // 2, 0, count),
            fixed_spec(9, hidden, length), fixed_spec(width, total)],
        out_shape=[sds((3, total, width), bf), sds((3, total, width), bf), sds((total, width), bf), sds((total, width), bf),
            sds((rows_here, DOCS, 2 * length, width), bf), sds((2 * length + n // 2, width), bf),
            sds((9, hidden, length), f32), sds((width, total), bf)],
        scratch_shapes=[pltpu.VMEM((total, width), bf), pltpu.VMEM((zt.shape[0], hidden), f32),
            pltpu.VMEM((2 * length + n // 2, CHUNK), f32)],
        compiler_params=pltpu.CompilerParams(vmem_limit_bytes=VMEM_BYTES),
        cost_estimate=pl.CostEstimate(
            flops=total * width * (6 * width + 4 * 2 * 5 * n), bytes_accessed=40 * total * width, transcendentals=0),
        name="mixer_forward")(*ins)


def gelu_parts(e):
    d = 1.0 + (0.3275911 / math.sqrt(2)) * jnp.abs(e)
    t = pl.reciprocal(d, approx=True)
    t = t * (2.0 - d * t)
    bell = jnp.exp(e * e * (-0.5))
    poly = t * (0.5 * 0.254829592 + t * (0.5 * -0.284496736 + t * (0.5 * 1.421413741 + t * (0.5 * -1.453152027 + t * (0.5 * 1.061405429)))))
    tail = poly * bell
    phi = jnp.where(e >= 0, 1.0 - tail, tail)
    return phi, phi + e * bell * (1 / math.sqrt(2 * math.pi))


def mlp_kernel(links, mix_ref, tok_ref, cot_ref, wo_ref, bo_ref, g2_ref, s2_ref, we_ref, be_ref, wr_ref, br_ref,
        out_ref, dat_ref, wog_ref, weg_ref, wrg_ref, beg_ref, vec_ref, hid, acc, dn2, n2, n2t, cott, act, de, *pair):
    j = pl.program_id(0)
    last = pl.num_programs(0) - 1
    total, width = tok_ref.shape
    part_ff = we_ref.shape[1]
    step = 512
    steps = total // step

    def at(i, size=step):
        return pl.ds(pl.multiple_of(i * size, size), size)

    core = ("rows", 0)
    if links:
        ahead_s, back_s, ahead_got, back_got, send_sem, recv_sem = pair

        def copies(k):
            mine, there = partner(core)
            slot = lax.rem(k, 2)
            return [
                pltpu.make_async_remote_copy(
                    src_ref=src.at[1 - mine], dst_ref=dst.at[slot], send_sem=send_sem.at[w], recv_sem=recv_sem.at[w, slot],
                    device_id=there, device_id_type=MESH)
                for w, (src, dst) in enumerate(((ahead_s, ahead_got), (back_s, back_got)))]

        def finish(k):
            for copy in copies(k):
                copy.wait()
            mine, _ = partner(core)
            slot = lax.rem(k, 2)
            count = ahead_s.shape[1]

            def add(b, carry):
                weg_ref[k * count + b] = (ahead_s[mine, b].astype(f32) + ahead_got[slot, b].astype(f32)).astype(bf)
                wrg_ref[b, k] = (back_s[mine, b].astype(f32) + back_got[slot, b].astype(f32)).astype(bf)
                return carry

            lax.fori_loop(0, count, add, 0)

    @pl.when(j == 0)
    def _():
        if links:
            meet([core])

        def body(i, carry):
            rows = at(i)
            h = tok_ref[rows, :].astype(f32) + nn(mix_ref[rows, :], wo_ref[...]) + as_row(bo_ref)
            hid[rows, :] = h
            xhat, _ = norm_stats(h)
            n2[rows, :] = (xhat * as_row(g2_ref) + as_row(s2_ref)).astype(bf)
            acc[rows, :] = h + as_row(br_ref)
            dn2[rows, :] = jnp.zeros((step, width), f32)
            return carry

        lax.fori_loop(0, steps, body, 0)
        for i in range(steps):
            rows = slice(i * step, (i + 1) * step)
            n2t[:, rows] = n2[rows, :].T
            cott[:, rows] = cot_ref[rows, :].T

    def tile(i, carry):
        rows = at(i)
        e = nn(n2[rows, :], we_ref[...]) + be_ref[pl.ds(pl.multiple_of(j * part_ff, part_ff), part_ff)].reshape(1, part_ff)
        da = nt(cot_ref[rows, :], wr_ref[...])
        phi, slope = gelu_parts(e)
        a = (e * phi).astype(bf)
        d = (da * slope).astype(bf)
        act[rows, :] = a
        de[rows, :] = d
        acc[rows, :] += nn(a, wr_ref[...])
        dn2[rows, :] += nt(d, we_ref[...])
        return carry + sum0(d.astype(f32))

    beg_ref[...] = lax.fori_loop(0, steps, tile, jnp.zeros((1, part_ff), f32))

    def grads(i, carry):
        rows = at(i, 384)
        back = nn(cott[rows, :], act[...]).astype(bf).T
        ahead = nn(n2t[rows, :], de[...]).astype(bf)
        blocks = 384 // LANES
        if links:
            tall = back_s.shape[3]
            for h in range(blocks):
                for y in range(back_s.shape[2]):
                    for k in range(2):
                        top = (2 * y + k) * tall
                        back_s[k, i * blocks + h, y] = back[top:top + tall, h * LANES:(h + 1) * LANES]
            tall = ahead_s.shape[3]
            groups = 384 // (2 * tall)
            for h in range(part_ff // LANES):
                for g in range(groups):
                    for k in range(2):
                        top = (2 * g + k) * tall
                        ahead_s[k, h, i * groups + g] = ahead[top:top + tall, h * LANES:(h + 1) * LANES]
        else:
            for h in range(blocks):
                wrg_ref[i * blocks + h, pl.ds(pl.multiple_of(j * part_ff, part_ff), part_ff), :] = back[:, h * LANES:(h + 1) * LANES]
            for h in range(part_ff // LANES):
                weg_ref[j * (part_ff // LANES) + h, rows, :] = ahead[:, h * LANES:(h + 1) * LANES]
        return carry

    if links:
        @pl.when(j > 0)
        def _():
            finish(j - 1)

    lax.fori_loop(0, width // 384, grads, 0)
    if links:
        for copy in copies(j):
            copy.start()

    @pl.when(j == last)
    def _():
        def body(i, carry):
            rows = at(i)
            out_ref[rows, :] = acc[rows, :].astype(bf)
            xhat, scale = norm_stats(hid[rows, :])
            dn = dn2[rows, :]
            gd = dn * as_row(g2_ref)
            m1 = jnp.mean(gd, axis=-1, keepdims=True)
            m2 = jnp.mean(gd * xhat, axis=-1, keepdims=True)
            cot = cot_ref[rows, :].astype(f32)
            low = (cot + scale * (gd - m1 - xhat * m2)).astype(bf)
            dat_ref[rows, :] = low
            return (carry[0] + sum0(dn * xhat), carry[1] + sum0(dn), carry[2] + sum0(low.astype(f32)), carry[3] + sum0(cot))

        zero = jnp.zeros((1, width), f32)
        sums = lax.fori_loop(0, steps, body, (zero,) * 4)
        for k in range(4):
            vec_ref[k:k + 1, :] = sums[k]
        for i in range(steps):
            rows = slice(i * step, (i + 1) * step)
            n2t[:, rows] = mix_ref[rows, :].T

        def weights(i, carry):
            rows = at(i, 256)
            part = nn(n2t[rows, :], dat_ref[...]).astype(bf)
            for h in range(width // LANES):
                wog_ref[h, rows, :] = part[:, h * LANES:(h + 1) * LANES]
            return carry

        lax.fori_loop(0, width // 256, weights, 0)
        if links:
            finish(j)


def single(*shape):
    return pl.BlockSpec(shape, lambda *_: (0,) * len(shape), pipeline_mode=pl.Buffered(1))


def mlp(links, mix, tok, cot, wo, bo, g2, s2, we, be, wr, br, part_ff=768):
    total, width = tok.shape
    ff = we.shape[1]
    sds = jax.ShapeDtypeStruct
    blocks = width // LANES
    parts = ff // part_ff
    scratch = [pltpu.VMEM((total, width), f32)] * 3 + [pltpu.VMEM((total, width), bf)]
    scratch += [pltpu.VMEM((width, total), bf)] * 2 + [pltpu.VMEM((total, part_ff), bf)] * 2
    if links:
        rows_n = links[0]
        pairs = rows_n // 2
        ahead = (ff // LANES, pairs, width // rows_n, LANES)
        back = (blocks, parts, pairs // parts, ff // rows_n, LANES)
        for shape in ((part_ff // LANES, *ahead[1:]), (blocks, *back[2:])):
            scratch.append(pltpu.VMEM((2, *shape), bf))
        for shape in ((part_ff // LANES, *ahead[1:]), (blocks, *back[2:])):
            scratch.append(pltpu.VMEM((2, *shape), bf))
        scratch += [pltpu.SemaphoreType.DMA((2,)), pltpu.SemaphoreType.DMA((2, 2))]
    else:
        ahead, back = (ff // LANES, width, LANES), (blocks, ff, LANES)
    side = dict(collective_id=1, has_side_effects=True) if links else {}
    return pl.pallas_call(
        functools.partial(mlp_kernel, links), grid=(parts,),
        in_specs=[whole_spec(a) for a in (mix, tok, cot, wo, bo, g2, s2)]
            + [pl.BlockSpec((width, part_ff), lambda j: (0, j)), whole_spec(be), pl.BlockSpec((part_ff, width), lambda j: (j, 0)),
                whole_spec(br)],
        out_specs=[single(total, width), single(total, width), single(blocks, width, LANES), single(*ahead), single(*back),
            pl.BlockSpec((1, part_ff), lambda j: (0, j)), single(8, width)],
        out_shape=[sds((total, width), bf), sds((total, width), bf), sds((blocks, width, LANES), bf), sds(ahead, bf),
            sds(back, bf), sds((1, ff), f32), sds((8, width), f32)],
        scratch_shapes=scratch,
        compiler_params=pltpu.CompilerParams(vmem_limit_bytes=VMEM_BYTES, **side),
        cost_estimate=pl.CostEstimate(
            flops=12 * total * width * ff + 4 * total * width * width, bytes_accessed=30 * total * width,
            transcendentals=total * ff),
        name="mlp")(mix, tok, cot, wo, bo, g2, s2, we, be, wr, br)


def backward_kernel(links, plan, sources, *refs):
    moved = len(plan)
    grads, refs = refs[:sources], refs[sources:]
    (dat_ref, tok_ref, seg_ref, g1_ref, wo_ref, long_ref, mixed_ref, proj_ref, trans_ref, spec_ref, nt_ref,
        wg_ref, wi_ref, wv_ref, swg_ref, swi_ref, swv_ref, skip_ref, state_ref, zt_ref, iw_ref, ow_ref, eo_ref, io_ref,
        oo_ref, fw_ref, rate_ref, t0, t3, t1, t2, u0, u3, u1, u2,
        tg_ref, wgrad_ref, sg_ref, vec_ref, gew_ref, giw_ref, gow_ref, gfw_ref, gsm_ref) = refs[:44]
    outs, (dn, de3, dp_s, ds_s, *pair) = refs[44:44 + moved], refs[44 + moved:]
    c = pl.program_id(0)
    r = pl.program_id(1)
    chunks = pl.num_programs(0)
    last_row = pl.num_programs(1) - 1
    length, wide = long_ref.shape
    n = length // 3
    half = n // 2
    rows = pl.ds(pl.multiple_of(r * length, length), length)
    tables = ((t0, u0), (t3, u3), (t1, u1), (t2, u2))

    @pl.when(r == 0)
    def _():
        ds_s[...] = jnp.zeros_like(ds_s)
        sg_ref[...] = jnp.zeros_like(sg_ref)

    @pl.when(jnp.logical_and(c == 0, r == 0))
    def _():
        dn[...] = jnp.zeros_like(dn)
        de3[...] = jnp.zeros_like(de3)
        vec_ref[...] = jnp.zeros_like(vec_ref)

    core = ("rows", 0)
    jobs = []
    if links:
        pair_s, pair_got, pair_send, pair_recv = pair[:4]
        rest = list(pair[4:])
        for (src, blocks, alive, order, _), out in zip(plan, outs):
            m = len(order)
            jobs.append(Halving(grads[src], blocks, alive, order, rest[:2 * m - 1] + [out] + rest[2 * m - 1:2 * m + 1],
                rest[2 * m + 1]))
            rest = rest[2 * m + 2:]

        def pair_copy(k):
            mine, there = partner(core)
            slot = lax.rem(k, 2)
            return pltpu.make_async_remote_copy(
                src_ref=pair_s.at[1 - mine], dst_ref=pair_got.at[slot], send_sem=pair_send, recv_sem=pair_recv.at[slot],
                device_id=there, device_id_type=MESH)

        def pair_finish(k):
            pair_copy(k).wait()
            mine, _ = partner(core)
            slot = lax.rem(k, 2)
            for i in range(3):
                for h in range(wide // LANES):
                    wgrad_ref[i, k * (wide // LANES) + h] = (
                        pair_s[mine, i, h].astype(f32) + pair_got[slot, i, h].astype(f32)).astype(bf)

        step = c * pl.num_programs(1) + r

        @pl.when(step == 0)
        def _():
            meet([core] + list(dict.fromkeys(s for job in plan for s in job[3] if s != core)))

        def advance(job, stage):
            if stage > 0:
                job.finish(stage - 1)
            if stage < len(job.order):
                job.start(stage)

        for now in range(MOMENTS):
            due = [(job, entry[4].index(now)) for job, entry in zip(jobs, plan) if now in entry[4]]
            if due:
                @pl.when(step == now)
                def _(due=due):
                    for job, stage in due:
                        advance(job, stage)

    def add(off, v):
        ds_s[off:off + v.shape[0], :] += v

    edge, one, two = token_masks(seg_ref[pl.ds(r, 1), :], length, wide)
    dm = nt(dat_ref[rows, :], wo_ref[...])
    gate_out = mixed_ref[0].astype(f32)
    gate_in = mixed_ref[1].astype(f32)
    value = mixed_ref[2].astype(f32)
    d_gate = dm * long_ref[...].astype(f32)
    d_long = dm * gate_out
    sg_ref[0, 5:6, :] += sum0(d_long * (value * gate_in))
    d_conv = None
    for d in range(DOCS):
        x = jnp.where(edge, d_long, 0.0) if d == 0 else jnp.where(edge, 0.0, d_long)
        ys = spread(x[0:n], x[n:2 * n], x[2 * n:])
        parts = []
        for s, off, m in specs_of(length, n):
            t, u = tables[s]
            g = nn(t[...], ys[s])
            ga, gb = g[:m], g[m:]
            qa, qb = spec_ref[off:off + m].astype(f32), spec_ref[off + m:off + 2 * m].astype(f32)
            qc = spec_ref[6 * n:6 * n + m].astype(f32) if s == 0 else qa
            pa, pb = trans_ref[0, d, off:off + m, :].astype(f32), trans_ref[0, d, off + m:off + 2 * m, :].astype(f32)
            back = jnp.concatenate([(ga * qa + gb * qb).astype(bf), (gb * qc - ga * qb).astype(bf)], 0)
            if s == 0:
                add(0, ga * pa)
                add(6 * n, gb * pb)
            else:
                add(off, ga * pa + gb * pb)
            add(off + m, gb * pa - ga * pb)
            parts.append(nn(u[...], back))
        y = jnp.concatenate(gather(*parts), 0)
        d_conv = y if d == 0 else jnp.where(edge, d_conv, y)
    d_inner = skip_ref[pl.ds(pl.multiple_of(c * wide, wide), wide)].reshape(1, wide) * d_long + d_conv * (1.0 / length)
    grads = (d_gate, d_inner * value, d_inner * gate_in)
    for i, (dmx, w, sw) in enumerate(zip(grads, (wg_ref, wi_ref, wv_ref), (swg_ref, swi_ref, swv_ref))):
        a1 = pltpu.roll(jnp.where(one, dmx, 0.0), length - 1, 0)
        a2 = pltpu.roll(jnp.where(two, dmx, 0.0), length - 2, 0)
        dp = (sw[0:1, :] * dmx + sw[1:2, :] * a1 + sw[2:3, :] * a2).astype(bf)
        p = proj_ref[i].astype(f32)
        for k, v in enumerate((p * dmx, p * a1, p * a2, dmx, dp.astype(f32))):
            sg_ref[i, k:k + 1, :] += sum0(v)
        dp_s[i, rows, :] = dp
        dn[rows, :] += nt(dp, w[...])

    @pl.when(r == last_row)
    def _():
        if links:
            @pl.when(c > 0)
            def _():
                pair_finish(c - 1)

        for i in range(3):
            part = nn(nt_ref[...], dp_s[i]).astype(bf)
            for h in range(wide // LANES):
                if links:
                    tall = pair_s.shape[4]
                    for g in range(pair_s.shape[3]):
                        for k in range(2):
                            top = (2 * g + k) * tall
                            pair_s[k, i, h, g] = part[top:top + tall, h * LANES:(h + 1) * LANES]
                else:
                    wgrad_ref[i, c * (wide // LANES) + h] = part[:, h * LANES:(h + 1) * LANES]
        if links:
            pair_copy(c).start()
        first = lax.broadcasted_iota(jnp.int32, (half, wide), 0) == 0
        extra = ds_s[6 * n:6 * n + half]
        ds_s[0:half] = jnp.where(first, 0.5, 1.0) * (ds_s[0:half] + jnp.where(first, 0.0, extra))
        ds_s[half:n] = jnp.where(first, 0.5 * extra, ds_s[half:n])
        parts = [nn(tables[s][1][...], (ds_s[off:off + 2 * m] * (1.0 / length)).astype(bf)) for s, off, m in specs_of(length, n)]
        gk = jnp.concatenate(gather(*parts), 0) * window(length, rate_ref[...])
        gfw_ref[...] = nn(state_ref[6], gk, HI)
        de3[...] += nt(fw_ref[...], gk, HI)

    @pl.when(c == chunks - 1)
    def _():
        step = 256
        g1 = as_row(g1_ref)
        for i in range(length // step):
            part = slice(i * step, (i + 1) * step)
            there = pl.ds(pl.multiple_of(r * length + i * step, step), step)
            xhat, scale = norm_stats(tok_ref[part, :].astype(f32))
            d = dn[there, :]
            gd = d * g1
            a = jnp.mean(gd, axis=-1, keepdims=True)
            b = jnp.mean(gd * xhat, axis=-1, keepdims=True)
            tg_ref[part, :] = (dat_ref[there, :].astype(f32) + scale * (gd - a - xhat * b)).astype(bf)
            vec_ref[0:1, :] += sum0(d * xhat)
            vec_ref[1:2, :] += sum0(d)

    @pl.when(jnp.logical_and(c == chunks - 1, r == last_row))
    def _():
        ones = jnp.ones((8, length), f32)
        flat = lambda v: nt(ones, v, HI)
        g = de3[...] * state_ref[7]
        gsm_ref[0] = flat(g * state_ref[8])
        g = g * column(oo_ref)
        gsm_ref[1] = flat(g)
        gow_ref[...] = nt(state_ref[3], g, HI)
        g = nn(ow_ref[...], g, HI) * state_ref[4]
        gsm_ref[2] = flat(g * state_ref[5])
        g = g * column(io_ref)
        gsm_ref[3] = flat(g)
        giw_ref[...] = nt(state_ref[0], g, HI)
        g = nn(iw_ref[...], g, HI) * state_ref[1]
        gsm_ref[4] = flat(g * state_ref[2])
        g = g * column(eo_ref)
        gsm_ref[5] = flat(g)
        gew_ref[...] = nt(zt_ref[...], g, HI)
        if links:
            pair_finish(c)
            for job in jobs:
                job.finish(len(job.order) - 1)


MOMENTS = 6


def backward_mixer(links, weg, wrg, wog, dat, tok, segments, g1, wo, longc, mixed, proj, trans, spec, ntr, wm, sw, skip, state, filt, zt, rates,
        tabs, tabst):
    rows_here, length = segments.shape
    total, width = tok.shape
    n = length // 3
    count = width // CHUNK
    ew, eb, eo, iw, ib, io, ow, ob, oo, fw = filt
    hidden = fw.shape[0]
    sds = jax.ShapeDtypeStruct
    plan, grads, moved, scratch = [], [], [], []
    wide_blocks = width // LANES
    wm_shape = (3, wide_blocks, width, LANES)
    if links:
        rows_n, pos_n = links
        alive = [d for d in alive_dims(rows_n, pos_n) if d != ("rows", 0)]
        pair = (3, CHUNK // LANES, rows_n // 2, width // rows_n, LANES)
        wm_shape = (3, wide_blocks, *pair[2:])
        scratch = [pltpu.VMEM((2, *pair), bf), pltpu.VMEM((2, *pair), bf), pltpu.SemaphoreType.DMA, pltpu.SemaphoreType.DMA((2,))]
        full = alive_dims(rows_n, pos_n)
        rows_of = wrg.shape[1] * wrg.shape[2] * wrg.shape[3] * 2
        grads = [weg.reshape(grad_shape(weg.shape[0], width, rows_n, pos_n, False)),
            wrg.reshape(grad_shape(wrg.shape[0], rows_of, rows_n, pos_n, False)),
            wog.reshape(grad_shape(wog.shape[0], width, rows_n, pos_n, True))]
        e_blocks, r_blocks, o_blocks = (g.shape[bits_of(pos_n)] for g in grads)
        first, second, third = three_orders(rows_n, pos_n)
        cut_e, cut_r = 2 * e_blocks // 3, 2 * r_blocks // 3
        plan = [(0, (0, cut_e), alive, first, (0, 3, 4, 5)), (1, (0, cut_r), alive, second, (0, 3, 4, 5)),
            (0, (cut_e, e_blocks - cut_e), alive, third, (0, 3, 4, 5)), (1, (cut_r, r_blocks - cut_r), alive, third, (0, 3, 4, 5)),
            (2, (0, o_blocks), full, [("rows", 0)] + first, (0, 1, 3, 4, 5))]
        for src, (_, blocks), dims, order, _ in plan:
            left = job_shapes(grads[src].shape, blocks, dims, order)
            moved.append(left[-1])
            scratch += job_scratch(left, False) + [pltpu.SemaphoreType.DMA]
    side = dict(collective_id=2, has_side_effects=True) if links else {}
    late = lambda c, r: (jnp.where(c == count - 1, r, 0), 0)
    ins = [*grads, dat, tok, segments, g1, wo, longc, mixed, proj, trans, spec, ntr, wm, wm, wm, sw, sw, sw, skip, state, zt,
        iw, ow, eo, io, oo, fw, rates, *tabs, *tabst]
    specs = [pl.BlockSpec(memory_space=pl.ANY) for g in grads] + [whole_spec(dat), pl.BlockSpec((length, width), late, pipeline_mode=pl.Buffered(1)), whole_spec(segments), whole_spec(g1),
        pl.BlockSpec((CHUNK, width), lambda c, r: (c, 0)), part_spec(length), stack_spec(3, length), stack_spec(3, length),
        pl.BlockSpec((1, DOCS, 2 * length, CHUNK), lambda c, r: (r, 0, 0, c)), column_spec(2 * length + n // 2, 0, count),
        whole_spec(ntr)]
    specs += [column_spec(width, k, count) for k in range(3)] + [column_spec(3, k, count) for k in range(3)]
    specs += [whole_spec(a) for a in (skip, state, zt, iw, ow, eo, io, oo)]
    specs += [column_spec(hidden, 0, count), column_spec(1, 0, count)] + [whole_spec(a) for a in (*tabs, *tabst)]
    return pl.pallas_call(
        functools.partial(backward_kernel, links, plan, len(grads)), grid=(count, rows_here), in_specs=specs,
        out_specs=[pl.BlockSpec((length, width), late, pipeline_mode=pl.Buffered(1)),
            single(*wm_shape),
            pl.BlockSpec((3, 8, CHUNK), lambda c, r: (0, 0, c)), fixed_spec(8, width), fixed_spec(zt.shape[0], hidden),
            fixed_spec(hidden, hidden), fixed_spec(hidden, hidden), column_spec(hidden, 0, count), fixed_spec(6, 8, hidden)]
            + [single(*s) for s in moved],
        out_shape=[sds((total, width), bf), sds(wm_shape, bf), sds((3, 8, width), f32),
            sds((8, width), f32), sds((zt.shape[0], hidden), f32), sds((hidden, hidden), f32), sds((hidden, hidden), f32),
            sds((hidden, width), f32), sds((6, 8, hidden), f32)]
            + [sds(s, bf) for s in moved],
        scratch_shapes=[pltpu.VMEM((total, width), f32), pltpu.VMEM((hidden, length), f32), pltpu.VMEM((3, total, CHUNK), bf),
            pltpu.VMEM((6 * n + n // 2, CHUNK), f32)] + scratch,
        compiler_params=pltpu.CompilerParams(vmem_limit_bytes=VMEM_BYTES, **side),
        cost_estimate=pl.CostEstimate(
            flops=total * width * (14 * width + 4 * 2 * 5 * n), bytes_accessed=50 * total * width, transcendentals=0),
        name="mixer_backward")(*ins)


def scatter_blocks(grad, rows_n, pos_n, first):
    blocks, height, wide = grad.shape
    if blocks % pos_n:
        flat = grad.transpose(1, 0, 2).reshape(height, blocks * wide)
        wide = blocks * wide // pos_n
        blocks = pos_n
        grad = flat.reshape(height, blocks, wide).transpose(1, 0, 2)
    high = height // rows_n
    rbits, pbits = bits_of(rows_n), bits_of(pos_n)
    acc = grad.reshape((2,) * pbits + (blocks // pos_n,) + (2,) * rbits + (high, wide))
    alive = alive_dims(rows_n, pos_n)
    for axis, bit in order_of(rows_n, pos_n, first):
        dim = alive.index((axis, bit))
        mine = (lax.axis_index(axis) >> bit) & 1
        size = rows_n if axis == "rows" else pos_n
        send = lax.dynamic_index_in_dim(acc, 1 - mine, dim, keepdims=False)
        keep = lax.dynamic_index_in_dim(acc, mine, dim, keepdims=False)
        got = lax.ppermute(send, axis, [(i, i ^ (1 << bit)) for i in range(size)])
        acc = (keep.astype(f32) + got.astype(f32)).astype(bf)
        alive.pop(dim)
    return acc


def pack_places(width, hidden, emb, ff):
    per = width // PACK
    at = {"filter": 0, "square": hidden * per}
    row = at["square"] + hidden
    for name, vectors in (("vec1", 2), ("vec2", 4), ("sgrad", 15), ("skip", 1), ("ebias", ff // width)):
        at[name] = row
        row += vectors * per
    at["small"] = row
    return at, row + 6


def pack_small(at, pk, beg, vec2, sgrad, vec1, gew, giw, gow, gfw, gsm):
    width = vec1.shape[1]
    hidden = giw.shape[0]
    per = width // PACK

    def put(row, value):
        for h in range(per):
            pk[row + h:row + h + 1, :] = value[:, h * PACK:(h + 1) * PACK]

    for k in range(beg.shape[1] // width):
        put(at["ebias"] + k * per, beg[:, k * width:(k + 1) * width])
    for k in range(4):
        put(at["vec2"] + k * per, vec2[k:k + 1, :])
    for i in range(3):
        for k in range(5):
            put(at["sgrad"] + (i * 5 + k) * per, sgrad[i, k:k + 1, :])
    put(at["skip"], sgrad[0, 5:6, :])
    for k in range(2):
        put(at["vec1"] + k * per, vec1[k:k + 1, :])
    for lane, ref in ((0, gew), (128, giw), (256, gow)):
        high = min(ref.shape[0], hidden)
        pk[at["square"]:at["square"] + high, lane:lane + hidden] = ref[0:high, :]
    for h in range(per):
        pk[at["filter"] + h * hidden:at["filter"] + (h + 1) * hidden, :] = gfw[:, h * PACK:(h + 1) * PACK]
    for k in range(6):
        pk[at["small"] + k:at["small"] + k + 1, 0:hidden] = gsm[k, 0:1, :]


def exchange_kernel(sizes, at, plan, count, *refs):
    rows_n, pos_n = sizes
    small = refs[:9]
    grads = refs[9:9 + count]
    pos = 9 + count
    packed_out = refs[pos]
    outs = refs[pos + 1:pos + 1 + len(plan)]
    scratch = list(refs[pos + 1 + len(plan):])
    pk, from_twin, half, rbuf, red, gath, ss1, rs1, ss2, rs2, pair_sems = scratch[:11]
    rest = scratch[11:]
    jobs = []
    for (src, blocks, alive, order), out in zip(plan, outs):
        m = len(order)
        jobs.append(Halving(grads[src], blocks, alive, order, rest[:2 * m - 1] + [out] + rest[2 * m - 1:2 * m + 1]))
        rest = rest[2 * m + 1:]
    n = rows_n * pos_n // 2
    side = pk.shape[0] // 2
    chunk = side // n
    place = lax.axis_index("rows")
    core = lax.rem(place, 2)
    me = (place // 2) * pos_n + lax.axis_index("pos")
    twin = {"rows": place + 1 - 2 * core}

    def ident(t):
        return {"rows": (t // pos_n) * 2 + core, "pos": t % pos_n}

    def each(f):
        def body(k, carry):
            f(lax.rem(me + k, n))
            return carry

        lax.fori_loop(1, n, body, 0)

    def own(t):
        return pl.ds(pl.multiple_of(t * chunk, chunk), chunk)

    def at_side(which, t=None):
        if t is None:
            return pl.ds(pl.multiple_of(which * side, side), side)
        return pl.ds(pl.multiple_of(which * side + t * chunk, chunk), chunk)

    barrier = pltpu.get_barrier_semaphore()
    pl.semaphore_signal(barrier, inc=1, device_id=twin, device_id_type=MESH)
    each(lambda t: pl.semaphore_signal(barrier, inc=1, device_id=ident(t), device_id_type=MESH))
    pk[...] = jnp.zeros_like(pk)
    pack_small(at, pk, *small)
    pl.semaphore_wait(barrier, n)

    to_twin = pltpu.make_async_remote_copy(
        src_ref=pk.at[at_side(1 - core), :], dst_ref=from_twin, send_sem=pair_sems.at[0], recv_sem=pair_sems.at[1],
        device_id=twin, device_id_type=MESH)
    back_twin = pltpu.make_async_remote_copy(
        src_ref=gath.at[at_side(core), :], dst_ref=gath.at[at_side(core), :], send_sem=pair_sems.at[2],
        recv_sem=pair_sems.at[3], device_id=twin, device_id_type=MESH)

    def scatter(t, slot):
        return pltpu.make_async_remote_copy(
            src_ref=half.at[own(t), :], dst_ref=rbuf.at[slot], send_sem=ss1.at[t], recv_sem=rs1.at[slot], device_id=ident(t),
            device_id_type=MESH)

    def publish(t, slot):
        return pltpu.make_async_remote_copy(
            src_ref=red, dst_ref=gath.at[at_side(core, slot), :], send_sem=ss2.at[t], recv_sem=rs2.at[slot],
            device_id=ident(t), device_id_type=MESH)

    def advance(stage):
        for job in jobs:
            if stage < len(job.order):
                job.finish(stage)
                if stage + 1 < len(job.order):
                    job.start(stage + 1)

    to_twin.start()
    for job in jobs:
        job.start(0)
    to_twin.wait()
    half[...] = pk[at_side(core), :] + from_twin[...]
    each(lambda t: scatter(t, me).start())
    rbuf[me] = half[own(me), :]
    advance(0)
    each(lambda t: scatter(t, t).wait())
    total = rbuf[0]
    for s in range(1, n):
        total = total + rbuf[s]
    red[...] = total
    gath[at_side(core, me), :] = total
    each(lambda t: publish(t, me).start())
    stages = max(len(job.order) for job in jobs)
    for stage in range(1, stages - 1):
        advance(stage)
    each(lambda t: publish(t, t).wait())
    back_twin.start()
    advance(stages - 1)
    back_twin.wait()
    packed_out[...] = gath[...]


def exchange(sizes, at, used, small, grads, plan):
    rows_n, pos_n = sizes
    n = rows_n * pos_n
    total = -(-used // (8 * n)) * 8 * n
    chunk = total // n
    vm = pl.BlockSpec(memory_space=pltpu.VMEM)
    tall = lambda rows: pltpu.VMEM((rows, PACK), f32)
    scratch = [tall(total), tall(total // 2), tall(total // 2), pltpu.VMEM((n // 2, chunk, PACK), f32), tall(chunk), tall(total)]
    scratch += [pltpu.SemaphoreType.DMA((n // 2,))] * 4 + [pltpu.SemaphoreType.DMA((4,))]
    shapes = [jax.ShapeDtypeStruct((total, PACK), f32)]
    for src, (start, blocks), alive, order in plan:
        left = job_shapes(grads[src].shape, blocks, alive, order)
        shapes.append(jax.ShapeDtypeStruct(left[-1], bf))
        scratch += job_scratch(left, False)
    return pl.pallas_call(
        functools.partial(exchange_kernel, sizes, at, plan, len(grads)), out_shape=shapes,
        in_specs=[vm] * (9 + len(grads)), out_specs=[vm] * len(shapes), scratch_shapes=scratch,
        compiler_params=pltpu.CompilerParams(collective_id=0, has_side_effects=True, vmem_limit_bytes=VMEM_BYTES),
        name="exchange")(*small, *grads)


def unpack(at, packed, results, blocks, width, hidden, emb, ff):
    per = width // PACK
    counts = [len(parts) for parts in blocks]
    flat = [p for parts in blocks for p in parts]

    def kernel(pk, *refs):
        copies = []
        if results:
            sems, refs = refs[-1], refs[:-1]
            m = len(results)
            copies = [pltpu.make_async_copy(a, b, sems.at[k]) for k, (a, b) in enumerate(zip(refs[:m], refs[-m:]))]
            refs = refs[m:-m]
        for copy in copies:
            copy.start()
        ins = list(refs[:len(flat)])
        fg, fs, mb, sw, sb, ew, eb, eo, iw, ib, io, ow, ob, oo, fw, sk, obias, sg, ss, eb2, rb = refs[len(flat):len(flat) + 21]
        outs = refs[len(flat) + 21:]

        def get(ref, lane, row):
            for h in range(per):
                ref[lane + h * PACK:lane + (h + 1) * PACK] = pk[row + h, :]

        get(fg, 0, at["vec1"])
        get(fs, 0, at["vec1"] + per)
        for i in range(3):
            base = at["sgrad"] + i * 5 * per
            for k in range(3):
                for h in range(per):
                    lane = i * width + h * PACK
                    sw[k:k + 1, lane:lane + PACK] = pk[base + k * per + h:base + k * per + h + 1, :]
            get(sb, i * width, base + 3 * per)
            get(mb, i * width, base + 4 * per)
        q = at["square"]
        ew[...] = pk[q:q + emb, 0:hidden]
        iw[...] = pk[q:q + hidden, 128:128 + hidden]
        ow[...] = pk[q:q + hidden, 256:256 + hidden]
        for k, ref in enumerate((oo, ob, io, ib, eo, eb)):
            ref[...] = pk[at["small"] + k, 0:hidden]
        for h in range(per):
            fw[:, h * PACK:(h + 1) * PACK] = pk[at["filter"] + h * hidden:at["filter"] + (h + 1) * hidden, :]
        get(sk, 0, at["skip"])
        for k, ref in enumerate((sg, ss, obias, rb)):
            get(ref, 0, at["vec2"] + k * per)
        for k in range(ff // width):
            get(eb2, k * width, at["ebias"] + k * per)
        for parts, out in zip(counts, outs):
            lane = 0
            for _ in range(parts):
                src = ins.pop(0)
                for b in range(src.shape[0]):
                    out[:, lane:lane + src.shape[2]] = src[b].astype(f32)
                    lane += src.shape[2]
        for copy in copies:
            copy.wait()

    s = lambda *d: jax.ShapeDtypeStruct(d, f32)
    shapes = [s(width), s(width), s(3 * width), s(3, 3 * width), s(3 * width), s(emb, hidden), s(hidden), s(hidden),
        s(hidden, hidden), s(hidden), s(hidden), s(hidden, hidden), s(hidden), s(hidden), s(hidden, width), s(width), s(width),
        s(width), s(width), s(ff), s(width)]
    shapes += [s(parts[0].shape[1], sum(p.shape[0] for p in parts) * parts[0].shape[2]) for parts in blocks]
    shapes += [jax.ShapeDtypeStruct(a.shape, a.dtype) for a in results]
    vm = pl.BlockSpec(memory_space=pltpu.VMEM)
    far = [pl.BlockSpec(memory_space=pl.ANY)] * len(results)
    return pl.pallas_call(
        kernel, out_shape=shapes, in_specs=[vm] + far + [vm] * len(flat), out_specs=[vm] * (len(shapes) - len(results)) + far,
        scratch_shapes=[pltpu.SemaphoreType.DMA((len(results),))] if results else [],
        compiler_params=pltpu.CompilerParams(vmem_limit_bytes=VMEM_BYTES), name="unpack")(packed, *results, *flat)


def on_device(sizes, tokens, segments, cotangent, first_gain, first_shift, mixer_weight, mixer_bias, short_weight, short_bias,
        embed_weight, embed_bias, embed_omega, inner_weight, inner_bias, inner_omega, outer_weight, outer_bias, outer_omega,
        filter_weight, skip_gain, output_weight, output_bias, second_gain, second_shift, expand_weight, expand_bias,
        reduce_weight, reduce_bias):
    rows_n, pos_n = sizes
    length, width = tokens.shape[1:]
    emb, hidden = embed_weight.shape
    ff = expand_weight.shape[1]
    tok = tokens.reshape(-1, width)
    cot = cotangent.reshape(-1, width)
    filt = [embed_weight, embed_bias, embed_omega, inner_weight, inner_bias, inner_omega, outer_weight, outer_bias, outer_omega,
        filter_weight]
    tabs, tabst = radix_tables(length)
    zt, rates = filter_inputs(length, emb, width)
    proj, mixed, longc, mix, trans, spec, state, ntr = forward_mixer(
        tok, segments, first_gain, first_shift, mixer_weight, mixer_bias, short_weight, short_bias, skip_gain, filt, zt, rates,
        tabs, tabst)
    direct = rows_n * pos_n == 32 and pos_n == 2 and width % (16 * rows_n) == 0 and width // LANES % pos_n == 0 and ff // rows_n * 4 == width
    links = sizes if direct else None
    out, dat, wog, weg, wrg, beg, vec2 = mlp(
        links, mix, tok, cot, output_weight, output_bias, second_gain, second_shift, expand_weight, expand_bias, reduce_weight,
        reduce_bias)
    tgrad, wmg, sgrad, vec1, gew, giw, gow, gfw, gsm, *early = backward_mixer(
        links, weg, wrg, wog, dat, tok, segments, first_gain, output_weight, longc, mixed, proj, trans, spec, ntr, mixer_weight,
        short_weight, skip_gain, state, filt, zt, rates, tabs, tabst)
    small = (beg, vec2, sgrad, vec1, gew, giw, gow, gfw, gsm)
    at, used = pack_places(width, hidden, emb, ff)
    blocks_m, blocks_o = 3 * width // LANES, width // LANES
    if direct:
        paired = [d for d in alive_dims(rows_n, pos_n) if d != ("rows", 0)]
        third = blocks_m // pos_n // 3
        grads = [wmg.reshape(grad_shape(blocks_m, width, rows_n, pos_n, False))]
        plan = [(0, (k * third, third), paired, order) for k, order in enumerate(three_orders(rows_n, pos_n))]
        packed, *m_parts = exchange(sizes, at, used, small, grads, plan)
        e_a, r_a, e_b, r_b, o_part = early
        blocks = [m_parts, [o_part], [e_a, e_b], [r_a, r_b]]
    else:
        packed = lax.psum(pack_only(at, used, small), ("rows", "pos"))
        grads = [wmg.reshape(blocks_m, width, LANES), wog, weg, wrg]
        blocks = [[scatter_blocks(g, rows_n, pos_n, f)] for g, f in zip(grads, ("pos", "rows", "pos", "rows"))]
    (fg, fs, mb, sw, sb, ew, eb, eo, iw, ib, io, ow, ob, oo, fw, sk, obias, sg, ss, eb2, rb, m_grad, o_grad, e_grad, r_grad, *results) = unpack(
        at, packed, [], blocks, width, hidden, emb, ff)
    if results:
        out, tgrad = results
    return (out.reshape(tokens.shape), tgrad.reshape(tokens.shape), fg, fs, m_grad, mb, sw, sb, ew, eb, eo, iw, ib, io, ow, ob,
        oo, fw, sk, o_grad, obias, sg, ss, e_grad, eb2, r_grad, rb)


def pack_only(at, used, small):
    def kernel(*refs):
        refs[-1][...] = jnp.zeros_like(refs[-1])
        pack_small(at, refs[-1], *refs[:-1])

    vm = pl.BlockSpec(memory_space=pltpu.VMEM)
    return pl.pallas_call(
        kernel, out_shape=jax.ShapeDtypeStruct((used, PACK), f32), in_specs=[vm] * len(small), out_specs=vm, name="pack")(*small)


def solution(mesh):
    both = ("rows", "pos")
    split = P(both, None, None)
    grid = P("rows", "pos")
    in_specs = (split, P(both, None), split) + (P(),) * 25
    out_specs = (split, split, P(), P(), grid) + (P(),) * 14 + (grid, P(), P(), P(), grid, P(), grid, P())
    sizes = (mesh.shape["rows"], mesh.shape["pos"])
    return jax.shard_map(
        functools.partial(on_device, sizes), mesh=mesh, in_specs=in_specs, out_specs=out_specs, check_vma=False)
```

```python
import functools
import math

import jax
import jax.numpy as jnp
import numpy as np
from jax import lax
from jax.experimental import pallas as pl
from jax.experimental.pallas import tpu as pltpu
from jax.sharding import PartitionSpec as P

f32 = jnp.float32
bf = jnp.bfloat16
HI = lax.Precision.HIGHEST
MESH = pl.DeviceIdType.MESH
DOCS = 2
EPSILON = 1e-5
ROOT3 = math.sqrt(3.0) / 2
LANES = 128
CHUNK = 256
PACK = 384
VMEM_BYTES = 63 * 2**20


def nt(a, b, precision=None):
    return lax.dot_general(a, b, (((1,), (1,)), ((), ())), precision=precision, preferred_element_type=f32)


def nn(a, b, precision=None):
    return lax.dot_general(a, b, (((1,), (0,)), ((), ())), precision=precision, preferred_element_type=f32)


def tn(a, b, precision=None):
    return lax.dot_general(a, b, (((0,), (0,)), ((), ())), precision=precision, preferred_element_type=f32)


def three_pass(dot, a, b):
    ah, bh = a.astype(bf), b.astype(bf)
    al, bl = (a - ah.astype(f32)).astype(bf), (b - bh.astype(f32)).astype(bf)
    return dot(ah, bh) + dot(ah, bl) + dot(al, bh)


def norm_stats(x):
    mean = jnp.mean(x, axis=-1, keepdims=True)
    centered = x - mean
    variance = jnp.mean(centered * centered, axis=-1, keepdims=True)
    scale = lax.rsqrt(variance + EPSILON)
    return centered * scale, scale


def sum0(v):
    return jnp.sum(v, axis=0, keepdims=True)


def as_row(ref):
    return ref[...].reshape(1, -1)


def radix_tables(length):
    n = length // 3
    m = 2 * length
    place = np.arange(n)

    def angle(freqs):
        return 2 * np.pi * ((freqs[:, None] * place[None, :]) % m) / m

    even = angle(6 * np.arange(n // 2))
    sine = np.sin(even)
    sine[0] = np.cos(np.pi * place)
    odd = angle(6 * np.arange(n // 2) + 3)
    out = [np.concatenate([np.cos(even), sine], 0), np.concatenate([np.cos(odd), np.sin(odd)], 0)]
    for k in (1, 2):
        turn = angle(6 * np.arange(n) + k)
        c, s = np.cos(turn), np.sin(turn)
        out.append(np.block([[c, -s], [s, c]]))
    low = lambda v: jnp.asarray(v.astype(np.float32)).astype(bf)
    return [low(t) for t in out], [low(t.T) for t in out]


def spread(x0, x1, x2):
    s = x1 + x2
    d = x1 - x2
    y0 = (x0 + s).astype(bf)
    y3 = (x0 - d).astype(bf)
    y1 = jnp.concatenate([(x0 + 0.5 * d).astype(bf), (ROOT3 * s).astype(bf)], 0)
    y2 = jnp.concatenate([(x0 - 0.5 * s).astype(bf), (ROOT3 * d).astype(bf)], 0)
    return y0, y3, y1, y2


def gather(v0, v3, v1, v2):
    n = v0.shape[0]
    v1r, v1i, v2r, v2i = v1[:n], v1[n:], v2[:n], v2[n:]
    even = v0 + v3
    a = 0.5 * (v1r - v2r)
    b = ROOT3 * (v1i + v2i)
    x0 = even + v1r + v2r
    x1 = (v0 - v3) + a + b
    x2 = even - 0.5 * (v1r + v2r) + ROOT3 * (v1i - v2i)
    return x0, x1, x2


def filter_inputs(length, emb, width):
    bands_count = (emb - 1) // 2
    places = np.arange(length, dtype=np.float32)
    tnorm = places / np.float32(length - 1)
    wave = places * np.float32(2.0 * math.pi / length)
    bands = np.linspace(0.0001, bands_count - 1, bands_count).astype(np.float32)
    phase = (wave[:, None] * bands[None, :]).astype(np.float32)
    z = np.concatenate([tnorm[:, None], np.cos(phase), -np.sin(phase)], 1).astype(np.float32)
    zt = np.concatenate([z.T, np.zeros(((-emb) % 8, length), np.float32)], 0)
    rates = np.abs(np.linspace(math.log(0.01) / 1.5, math.log(0.01) / 0.3, width)).astype(np.float32)[None, :]
    return jnp.asarray(zt), jnp.asarray(rates)


def window(length, rate):
    tnorm = lax.broadcasted_iota(jnp.int32, (length, rate.shape[1]), 0).astype(f32) * (1.0 / (length - 1))
    return jnp.exp(-tnorm * rate)


def sin_cos(x):
    k = jnp.floor(x * (1.0 / math.pi) + 0.5)
    r = x - k * 3.140625
    r = r - k * 0.0009670257568359375
    r = r - k * 6.2771141529083251953e-07
    sign = 1.0 - 2.0 * (k - 2.0 * jnp.floor(k * 0.5))
    q = r * r
    s = 1.0 + q * (-1 / 6 + q * (1 / 120 + q * (-1 / 5040 + q * (1 / 362880 + q * (-1 / 39916800 + q * (1 / 6227020800))))))
    c = 1.0 + q * (-1 / 2 + q * (1 / 24 + q * (-1 / 720 + q * (1 / 40320 + q * (-1 / 3628800 + q * (1 / 479001600 - q * (1 / 87178291200)))))))
    return r * s * sign, c * sign


def column(ref):
    v = as_row(ref)
    n = v.shape[1]
    i = lax.broadcasted_iota(jnp.int32, (n, n), 0)
    j = lax.broadcasted_iota(jnp.int32, (n, n), 1)
    return jnp.sum(jnp.where(i == j, v, 0.0), axis=1, keepdims=True)


def token_masks(seg, length, wide):
    edge = jnp.sum((seg == 0).astype(jnp.int32), axis=1, keepdims=True)
    t = lax.broadcasted_iota(jnp.int32, (length, wide), 0)
    one = jnp.logical_and(t != 0, t != edge)
    two = jnp.logical_and(jnp.logical_and(one, t != 1), t != edge + 1)
    return t < edge, one, two


def interleave(streams, lag=1):
    streams = list(streams)
    waiting = [lag * k for k in range(len(streams))]
    while streams:
        for k in range(len(streams)):
            if waiting[k] > 0:
                waiting[k] -= 1
            elif next(streams[k], streams) is streams:
                waiting[k] = None
        streams, waiting = [s for s, w in zip(streams, waiting) if w is not None], [w for w in waiting if w is not None]


def specs_of(length, n):
    return ((0, 0, n // 2), (1, n, n // 2), (2, 2 * n, n), (3, 4 * n, n))


def bits_of(n):
    return n.bit_length() - 1


def order_of(rows_n, pos_n, first):
    rows = [("rows", b) for b in range(1, bits_of(rows_n))]
    pos = [("pos", b) for b in range(bits_of(pos_n))]
    return [("rows", 0)] + (pos + rows if first == "pos" else rows[:1] + pos + rows[1:])


def three_orders(rows_n, pos_n):
    pos = [("pos", b) for b in range(bits_of(pos_n))]
    near = [("rows", b) for b in range(1, bits_of(rows_n) - 1)]
    far = [("rows", bits_of(rows_n) - 1)]
    ring = pos + near
    turn = lambda k: ring[k:] + ring[:k]
    return turn(0) + far, turn(len(pos)) + far, turn(len(ring) - 1) + far


def alive_dims(rows_n, pos_n):
    pos = [("pos", b) for b in reversed(range(bits_of(pos_n)))]
    return pos + [None] + [("rows", b) for b in reversed(range(bits_of(rows_n)))]


def partner(step):
    axis, bit = step
    place = lax.axis_index(axis)
    mine = (place // (1 << bit)) % 2
    return mine, {axis: place + (1 - 2 * mine) * (1 << bit)}


def greet(steps):
    barrier = pltpu.get_barrier_semaphore()
    for step in steps:
        pl.semaphore_signal(barrier, inc=1, device_id=partner(step)[1], device_id_type=MESH)


def meet(steps):
    pl.semaphore_wait(pltpu.get_barrier_semaphore(), len(steps))


class Halving:
    def __init__(self, ref, blocks, alive, order, refs, near=None):
        m = len(order)
        self.near = near
        got, sums, self.send_sem, self.recv_sem = refs[:m], refs[m:2 * m], refs[2 * m], refs[2 * m + 1]
        self.order, self.got, self.sums = order, got, sums
        self.stages = []
        alive = list(alive)
        for k, step in enumerate(order):
            self.stages.append((ref, blocks, tuple(alive), alive.index(step)))
            alive.remove(step)
            ref, blocks = sums[k], (0, blocks[1])

    def pick(self, stage, which):
        ref, (start, count), alive, dim = self.stages[stage]
        index = [slice(None)] * len(alive)
        index[alive.index(None)] = pl.ds(start, count)
        index[dim] = which
        return ref.at[tuple(index)]

    def copy(self, stage):
        mine, there = partner(self.order[stage])
        return pltpu.make_async_remote_copy(
            src_ref=self.pick(stage, 1 - mine), dst_ref=self.got[stage], send_sem=self.send_sem.at[stage],
            recv_sem=self.recv_sem.at[stage], device_id=there, device_id_type=MESH)

    def fetch(self):
        return pltpu.make_async_copy(self.pick(0, partner(self.order[0])[0]), self.sums[0], self.near)

    def start(self, stage):
        self.copy(stage).start()
        if stage == 0 and self.near is not None:
            self.fetch().start()

    def finish(self, stage):
        self.copy(stage).wait()
        if stage == 0 and self.near is not None:
            self.fetch().wait()
        _, (_, count), alive, dim = self.stages[stage]
        kept, got, out = self.pick(stage, partner(self.order[stage])[0]), self.got[stage], self.sums[stage]
        if stage == 0 and self.near is not None:
            kept = out
        split = [d for k, d in enumerate(alive) if k != dim].index(None)

        def add(lead):
            def body(b, carry):
                at = lead + (b,)
                out[at] = (kept[at].astype(f32) + got[at].astype(f32)).astype(bf)
                return carry

            lax.fori_loop(0, count, body, 0)

        leads = [()]
        for _ in range(split):
            leads = [lead + (k,) for lead in leads for k in range(2)]
        for lead in leads:
            add(lead)


def job_shapes(shape, blocks, alive, order):
    dims = list(alive)
    now = [blocks if d is None else 2 for d in dims] + list(shape[-2:])
    out = []
    for step in order:
        k = dims.index(step)
        dims.pop(k)
        now.pop(k)
        out.append(tuple(now))
    return out


def job_scratch(left, last):
    sums = left if last else left[:-1]
    return [pltpu.VMEM(s, bf) for s in left] + [pltpu.VMEM(s, bf) for s in sums] + [pltpu.SemaphoreType.DMA((len(left),))] * 2


def grad_shape(blocks, rows, rows_n, pos_n, cores):
    rbits, pbits = bits_of(rows_n), bits_of(pos_n)
    return (2,) * pbits + (blocks // pos_n,) + (2,) * (rbits - (0 if cores else 1)) + (rows // rows_n, LANES)


def forward_kernel(tok_ref, seg_ref, g1_ref, s1_ref, wg_ref, wi_ref, wv_ref, mb_ref, swg_ref, swi_ref, swv_ref, sb_ref,
        skip_ref, zt_ref, ew_ref, eb_ref, eo_ref, iw_ref, ib_ref, io_ref, ow_ref, ob_ref, oo_ref, fw_ref, rate_ref,
        t0, t3, t1, t2, u0, u3, u1, u2,
        proj_ref, mixed_ref, long_ref, mix_ref, trans_ref, low_ref, state_ref, nt_ref, normed, padded, spec_ref):
    c = pl.program_id(0)
    rows_here, length = seg_ref.shape
    width = tok_ref.shape[1]
    n = length // 3
    half = n // 2
    wide = fw_ref.shape[1]
    tables = ((t0, u0), (t3, u3), (t1, u1), (t2, u2))

    @pl.when(c == 0)
    def _():
        step = 256
        for i in range(tok_ref.shape[0] // step):
            part = slice(i * step, (i + 1) * step)
            xhat, _ = norm_stats(tok_ref[part, :].astype(f32))
            low = (xhat * as_row(g1_ref) + as_row(s1_ref)).astype(bf)
            normed[part, :] = low
            nt_ref[:, part] = low.T

    @pl.when(c == 0)
    def _():
        padded[...] = jnp.zeros_like(padded)
        padded[0:ew_ref.shape[0], :] = ew_ref[...]
        pre = tn(padded[...], zt_ref[...], HI) + column(eb_ref)
        e1, c1 = sin_cos(column(eo_ref) * pre)
        state_ref[0] = e1
        state_ref[1] = c1
        state_ref[2] = pre
        pre = tn(iw_ref[...], e1, HI) + column(ib_ref)
        e2, c2 = sin_cos(column(io_ref) * pre)
        state_ref[3] = e2
        state_ref[4] = c2
        state_ref[5] = pre
        pre = tn(ow_ref[...], e2, HI) + column(ob_ref)
        e3, c3 = sin_cos(column(oo_ref) * pre)
        state_ref[6] = e3
        state_ref[7] = c3
        state_ref[8] = pre

    def spectrum():
        kernel = three_pass(tn, state_ref[6], fw_ref[...]) * window(length, rate_ref[...])
        k = kernel.astype(bf).astype(f32)
        y0, y3, y1, y2 = spread(k[0:n], k[n:2 * n], k[2 * n:])
        yield
        first = lax.broadcasted_iota(jnp.int32, (half, wide), 0) == 0
        q0 = nn(t0[...], y0)
        spec_ref[0:half] = q0[0:half] * jnp.where(first, 0.5, 1.0)
        spec_ref[half:n] = jnp.where(first, 0.0, q0[half:])
        spec_ref[6 * n:6 * n + half] = jnp.where(first, 0.5 * q0[half:], q0[0:half])
        spec_ref[n:2 * n] = nn(t3[...], y3)
        yield
        spec_ref[2 * n:4 * n] = nn(t1[...], y1)
        spec_ref[4 * n:6 * n] = nn(t2[...], y2)
        yield
        low_ref[...] = spec_ref[...].astype(bf)

    mixed = [[None] * 3 for _ in range(rows_here)]
    inner = [None] * rows_here
    masks = [token_masks(seg_ref[r:r + 1, :], length, wide) for r in range(rows_here)]

    def project(r):
        rows = slice(r * length, (r + 1) * length)
        edge, one, two = masks[r]
        for i, (w, sw) in enumerate(((wg_ref, swg_ref), (wi_ref, swi_ref), (wv_ref, swv_ref))):
            at = pl.ds(pl.multiple_of(i * width + c * wide, wide), wide)
            p = nn(normed[rows, :], w[...]) + mb_ref[at].reshape(1, wide)
            yield
            proj_ref[i, rows, :] = p.astype(bf)
            m = (sb_ref[at].reshape(1, wide) + sw[0:1, :] * p + sw[1:2, :] * jnp.where(one, pltpu.roll(p, 1, 0), 0.0)
                + sw[2:3, :] * jnp.where(two, pltpu.roll(p, 2, 0), 0.0))
            mixed_ref[i, rows, :] = m.astype(bf)
            mixed[r][i] = m
        inner[r] = mixed[r][2] * mixed[r][1]

    def convolve(r):
        rows = slice(r * length, (r + 1) * length)
        edge = masks[r][0]
        inner_low = inner[r].astype(bf).astype(f32)
        xs = [jnp.where(edge, inner_low, 0.0), jnp.where(edge, 0.0, inner_low)]
        ys = [jnp.concatenate(pair_of, 1) for pair_of in zip(*(spread(x[0:n], x[n:2 * n], x[2 * n:]) for x in xs))]
        parts = {}
        for s, off, m in specs_of(length, n)[::-1]:
            t, u = tables[s]
            p = nn(t[...], ys[s])
            yield
            qa, qb = spec_ref[off:off + m], spec_ref[off + m:off + 2 * m]
            qc = spec_ref[6 * n:6 * n + m] if s == 0 else qa
            prod = []
            for d in range(DOCS):
                mine = p[:, d * wide:(d + 1) * wide]
                trans_ref[r, d, off:off + 2 * m, :] = mine.astype(bf)
                pa, pb = mine[:m], mine[m:]
                prod.append(jnp.concatenate([(pa * qa - pb * qb).astype(bf), (pa * qb + pb * qc).astype(bf)], 0))
            parts[s] = nn(u[...], jnp.concatenate(prod, 1))
            yield
        y = jnp.concatenate(gather(*(parts[s] for s in range(4))), 0)
        conv = jnp.where(edge, y[:, :wide], y[:, wide:])
        longconv = conv * (1.0 / length) + skip_ref[pl.ds(pl.multiple_of(c * wide, wide), wide)].reshape(1, wide) * inner[r]
        long_ref[rows, :] = longconv.astype(bf)
        mix_ref[rows, :] = (mixed[r][0] * longconv).astype(bf)

    def row_stream(r):
        yield from project(r)
        yield from convolve(r)

    interleave([spectrum()] + [row_stream(r) for r in range(rows_here)], LAG)


LAG = 2


def whole_spec(a):
    return pl.BlockSpec(a.shape, lambda *_: (0,) * a.ndim, pipeline_mode=pl.Buffered(1))


def fixed_spec(*shape):
    return pl.BlockSpec(shape, lambda *_: (0,) * len(shape))


def column_spec(rows, k, count):
    return pl.BlockSpec((rows, CHUNK), lambda c, r=0: (0, k * count + c))


def part_spec(length):
    return pl.BlockSpec((length, CHUNK), lambda c, r=0: (r, c))


def stack_spec(count, length):
    return pl.BlockSpec((count, length, CHUNK), lambda c, r=0: (0, r, c))


def vector_chunk():
    return pl.BlockSpec((CHUNK,), lambda c, r: (c,))


def forward_mixer(tok, segments, g1, s1, wm, mb, sw, sb, skip, filt, zt, rates, tabs, tabst):
    rows_here, length = segments.shape
    total, width = tok.shape
    n = length // 3
    count = width // CHUNK
    fw = filt[-1]
    hidden = fw.shape[0]
    sds = jax.ShapeDtypeStruct
    ins = [tok, segments, g1, s1, wm, wm, wm, mb, sw, sw, sw, sb, skip, zt, *filt, rates, *tabs, *tabst]
    specs = [whole_spec(a) for a in (tok, segments, g1, s1)]
    specs += [column_spec(width, k, count) for k in range(3)] + [whole_spec(mb)] + [column_spec(3, k, count) for k in range(3)]
    specs += [whole_spec(sb), whole_spec(skip), whole_spec(zt)] + [whole_spec(a) for a in filt[:-1]]
    specs += [column_spec(hidden, 0, count), column_spec(1, 0, count)] + [whole_spec(a) for a in (*tabs, *tabst)]
    return pl.pallas_call(
        forward_kernel, grid=(count,), in_specs=specs,
        out_specs=[stack_spec(3, total), stack_spec(3, total), part_spec(total), part_spec(total),
            pl.BlockSpec((rows_here, DOCS, 2 * length, CHUNK), lambda c: (0, 0, 0, c)), column_spec(2 * length + n // 2, 0, count),
            fixed_spec(9, hidden, length), fixed_spec(width, total)],
        out_shape=[sds((3, total, width), bf), sds((3, total, width), bf), sds((total, width), bf), sds((total, width), bf),
            sds((rows_here, DOCS, 2 * length, width), bf), sds((2 * length + n // 2, width), bf),
            sds((9, hidden, length), f32), sds((width, total), bf)],
        scratch_shapes=[pltpu.VMEM((total, width), bf), pltpu.VMEM((zt.shape[0], hidden), f32),
            pltpu.VMEM((2 * length + n // 2, CHUNK), f32)],
        compiler_params=pltpu.CompilerParams(vmem_limit_bytes=VMEM_BYTES),
        cost_estimate=pl.CostEstimate(
            flops=total * width * (6 * width + 4 * 2 * 5 * n), bytes_accessed=40 * total * width, transcendentals=0),
        name="mixer_forward")(*ins)


def gelu_parts(e):
    d = 1.0 + (0.3275911 / math.sqrt(2)) * jnp.abs(e)
    t = pl.reciprocal(d, approx=True)
    t = t * (2.0 - d * t)
    bell = jnp.exp(e * e * (-0.5))
    poly = t * (0.5 * 0.254829592 + t * (0.5 * -0.284496736 + t * (0.5 * 1.421413741 + t * (0.5 * -1.453152027 + t * (0.5 * 1.061405429)))))
    tail = poly * bell
    phi = jnp.where(e >= 0, 1.0 - tail, tail)
    return phi, phi + e * bell * (1 / math.sqrt(2 * math.pi))


def mlp_kernel(links, mix_ref, tok_ref, cot_ref, wo_ref, bo_ref, g2_ref, s2_ref, we_ref, be_ref, wr_ref, br_ref,
        out_ref, dat_ref, wog_ref, weg_ref, wrg_ref, beg_ref, vec_ref, hid, acc, dn2, n2, n2t, cott, act, de, *pair):
    j = pl.program_id(0)
    last = pl.num_programs(0) - 1
    total, width = tok_ref.shape
    part_ff = we_ref.shape[1]
    step = 512
    steps = total // step

    def at(i, size=step):
        return pl.ds(pl.multiple_of(i * size, size), size)

    core = ("rows", 0)
    if links:
        ahead_s, back_s, ahead_got, back_got, send_sem, recv_sem = pair

        def copies(k):
            mine, there = partner(core)
            slot = lax.rem(k, 2)
            return [
                pltpu.make_async_remote_copy(
                    src_ref=src.at[1 - mine], dst_ref=dst.at[slot], send_sem=send_sem.at[w], recv_sem=recv_sem.at[w, slot],
                    device_id=there, device_id_type=MESH)
                for w, (src, dst) in enumerate(((ahead_s, ahead_got), (back_s, back_got)))]

        def finish(k):
            for copy in copies(k):
                copy.wait()
            mine, _ = partner(core)
            slot = lax.rem(k, 2)
            count = ahead_s.shape[1]

            def add(b, carry):
                weg_ref[k * count + b] = (ahead_s[mine, b].astype(f32) + ahead_got[slot, b].astype(f32)).astype(bf)
                wrg_ref[b, k] = (back_s[mine, b].astype(f32) + back_got[slot, b].astype(f32)).astype(bf)
                return carry

            lax.fori_loop(0, count, add, 0)

    @pl.when(j == 0)
    def _():
        if links:
            greet([core])

        def body(i, carry):
            rows = at(i)
            h = tok_ref[rows, :].astype(f32) + nn(mix_ref[rows, :], wo_ref[...]) + as_row(bo_ref)
            hid[rows, :] = h
            xhat, _ = norm_stats(h)
            n2[rows, :] = (xhat * as_row(g2_ref) + as_row(s2_ref)).astype(bf)
            acc[rows, :] = h + as_row(br_ref)
            dn2[rows, :] = jnp.zeros((step, width), f32)
            return carry

        lax.fori_loop(0, steps, body, 0)
        for i in range(steps):
            rows = slice(i * step, (i + 1) * step)
            n2t[:, rows] = n2[rows, :].T
            cott[:, rows] = cot_ref[rows, :].T

    def tile(i, carry):
        rows = at(i)
        e = nn(n2[rows, :], we_ref[...]) + be_ref[pl.ds(pl.multiple_of(j * part_ff, part_ff), part_ff)].reshape(1, part_ff)
        da = nt(cot_ref[rows, :], wr_ref[...])
        phi, slope = gelu_parts(e)
        a = (e * phi).astype(bf)
        d = (da * slope).astype(bf)
        act[rows, :] = a
        de[rows, :] = d
        acc[rows, :] += nn(a, wr_ref[...])
        dn2[rows, :] += nt(d, we_ref[...])
        return carry + sum0(d.astype(f32))

    beg_ref[...] = lax.fori_loop(0, steps, tile, jnp.zeros((1, part_ff), f32))

    def grads(i, carry):
        rows = at(i, 384)
        back = nn(cott[rows, :], act[...]).astype(bf).T
        ahead = nn(n2t[rows, :], de[...]).astype(bf)
        blocks = 384 // LANES
        if links:
            tall = back_s.shape[3]
            for h in range(blocks):
                for y in range(back_s.shape[2]):
                    for k in range(2):
                        top = (2 * y + k) * tall
                        back_s[k, i * blocks + h, y] = back[top:top + tall, h * LANES:(h + 1) * LANES]
            tall = ahead_s.shape[3]
            groups = 384 // (2 * tall)
            for h in range(part_ff // LANES):
                for g in range(groups):
                    for k in range(2):
                        top = (2 * g + k) * tall
                        ahead_s[k, h, i * groups + g] = ahead[top:top + tall, h * LANES:(h + 1) * LANES]
        else:
            for h in range(blocks):
                wrg_ref[i * blocks + h, pl.ds(pl.multiple_of(j * part_ff, part_ff), part_ff), :] = back[:, h * LANES:(h + 1) * LANES]
            for h in range(part_ff // LANES):
                weg_ref[j * (part_ff // LANES) + h, rows, :] = ahead[:, h * LANES:(h + 1) * LANES]
        return carry

    if links:
        @pl.when(j > 0)
        def _():
            finish(j - 1)

    lax.fori_loop(0, width // 384, grads, 0)
    if links:
        @pl.when(j == 0)
        def _():
            meet([core])

        for copy in copies(j):
            copy.start()

    @pl.when(j == last)
    def _():
        def body(i, carry):
            rows = at(i)
            out_ref[rows, :] = acc[rows, :].astype(bf)
            xhat, scale = norm_stats(hid[rows, :])
            dn = dn2[rows, :]
            gd = dn * as_row(g2_ref)
            m1 = jnp.mean(gd, axis=-1, keepdims=True)
            m2 = jnp.mean(gd * xhat, axis=-1, keepdims=True)
            cot = cot_ref[rows, :].astype(f32)
            low = (cot + scale * (gd - m1 - xhat * m2)).astype(bf)
            dat_ref[rows, :] = low
            return (carry[0] + sum0(dn * xhat), carry[1] + sum0(dn), carry[2] + sum0(low.astype(f32)), carry[3] + sum0(cot))

        zero = jnp.zeros((1, width), f32)
        sums = lax.fori_loop(0, steps, body, (zero,) * 4)
        for k in range(4):
            vec_ref[k:k + 1, :] = sums[k]
        for i in range(steps):
            rows = slice(i * step, (i + 1) * step)
            n2t[:, rows] = mix_ref[rows, :].T

        def weights(i, carry):
            rows = at(i, 256)
            part = nn(n2t[rows, :], dat_ref[...]).astype(bf)
            for h in range(width // LANES):
                wog_ref[h, rows, :] = part[:, h * LANES:(h + 1) * LANES]
            return carry

        lax.fori_loop(0, width // 256, weights, 0)
        if links:
            finish(j)


def single(*shape):
    return pl.BlockSpec(shape, lambda *_: (0,) * len(shape), pipeline_mode=pl.Buffered(1))


def mlp(links, mix, tok, cot, wo, bo, g2, s2, we, be, wr, br, part_ff=768):
    total, width = tok.shape
    ff = we.shape[1]
    sds = jax.ShapeDtypeStruct
    blocks = width // LANES
    parts = ff // part_ff
    scratch = [pltpu.VMEM((total, width), f32)] * 3 + [pltpu.VMEM((total, width), bf)]
    scratch += [pltpu.VMEM((width, total), bf)] * 2 + [pltpu.VMEM((total, part_ff), bf)] * 2
    if links:
        rows_n = links[0]
        pairs = rows_n // 2
        ahead = (ff // LANES, pairs, width // rows_n, LANES)
        back = (blocks, parts, pairs // parts, ff // rows_n, LANES)
        for shape in ((part_ff // LANES, *ahead[1:]), (blocks, *back[2:])):
            scratch.append(pltpu.VMEM((2, *shape), bf))
        for shape in ((part_ff // LANES, *ahead[1:]), (blocks, *back[2:])):
            scratch.append(pltpu.VMEM((2, *shape), bf))
        scratch += [pltpu.SemaphoreType.DMA((2,)), pltpu.SemaphoreType.DMA((2, 2))]
    else:
        ahead, back = (ff // LANES, width, LANES), (blocks, ff, LANES)
    side = dict(collective_id=1, has_side_effects=True) if links else {}
    return pl.pallas_call(
        functools.partial(mlp_kernel, links), grid=(parts,),
        in_specs=[whole_spec(a) for a in (mix, tok, cot, wo, bo, g2, s2)]
            + [pl.BlockSpec((width, part_ff), lambda j: (0, j)), whole_spec(be), pl.BlockSpec((part_ff, width), lambda j: (j, 0)),
                whole_spec(br)],
        out_specs=[single(total, width), single(total, width), single(blocks, width, LANES), single(*ahead), single(*back),
            pl.BlockSpec((1, part_ff), lambda j: (0, j)), single(8, width)],
        out_shape=[sds((total, width), bf), sds((total, width), bf), sds((blocks, width, LANES), bf), sds(ahead, bf),
            sds(back, bf), sds((1, ff), f32), sds((8, width), f32)],
        scratch_shapes=scratch,
        compiler_params=pltpu.CompilerParams(vmem_limit_bytes=VMEM_BYTES, **side),
        cost_estimate=pl.CostEstimate(
            flops=12 * total * width * ff + 4 * total * width * width, bytes_accessed=30 * total * width,
            transcendentals=total * ff),
        name="mlp")(mix, tok, cot, wo, bo, g2, s2, we, be, wr, br)


def backward_kernel(links, plan, sources, *refs):
    moved = len(plan)
    grads, refs = refs[:sources], refs[sources:]
    (dat_ref, tok_ref, seg_ref, g1_ref, wo_ref, long_ref, mixed_ref, proj_ref, trans_ref, spec_ref, nt_far,
        wg_ref, wi_ref, wv_ref, swg_ref, swi_ref, swv_ref, skip_ref, state_far, zt_ref, iw_ref, ow_ref, eo_ref, io_ref,
        oo_ref, fw_ref, rate_ref, t0, t3, t1, t2, u0, u3, u1, u2,
        tg_ref, wgrad_ref, sg_ref, vec_ref, gew_ref, giw_ref, gow_ref, gfw_ref, gsm_ref) = refs[:44]
    outs, (dn, de3, dp_s, ds_s, nt_ref, state_ref, late_sems, *pair) = refs[44:44 + moved], refs[44 + moved:]
    c = pl.program_id(0)
    r = pl.program_id(1)
    chunks = pl.num_programs(0)
    last_row = pl.num_programs(1) - 1
    length, wide = long_ref.shape
    n = length // 3
    half = n // 2
    rows = pl.ds(pl.multiple_of(r * length, length), length)
    tables = ((t0, u0), (t3, u3), (t1, u1), (t2, u2))

    late_copies = [pltpu.make_async_copy(a, b, late_sems.at[k]) for k, (a, b) in enumerate(((nt_far, nt_ref), (state_far, state_ref)))]

    @pl.when(jnp.logical_and(c == 0, r == 0))
    def _():
        for copy in late_copies:
            copy.start()

    @pl.when(r == 0)
    def _():
        ds_s[...] = jnp.zeros_like(ds_s)
        sg_ref[...] = jnp.zeros_like(sg_ref)

    @pl.when(jnp.logical_and(c == 0, r == 0))
    def _():
        dn[...] = jnp.zeros_like(dn)
        de3[...] = jnp.zeros_like(de3)
        vec_ref[...] = jnp.zeros_like(vec_ref)

    core = ("rows", 0)
    jobs = []
    if links:
        pair_s, pair_got, pair_send, pair_recv = pair[:4]
        rest = list(pair[4:])
        for (src, blocks, alive, order, _), out in zip(plan, outs):
            m = len(order)
            jobs.append(Halving(grads[src], blocks, alive, order, rest[:2 * m - 1] + [out] + rest[2 * m - 1:2 * m + 1],
                rest[2 * m + 1]))
            rest = rest[2 * m + 2:]

        def pair_copy(k):
            mine, there = partner(core)
            slot = lax.rem(k, 2)
            return pltpu.make_async_remote_copy(
                src_ref=pair_s.at[1 - mine], dst_ref=pair_got.at[slot], send_sem=pair_send, recv_sem=pair_recv.at[slot],
                device_id=there, device_id_type=MESH)

        def pair_finish(k):
            pair_copy(k).wait()
            mine, _ = partner(core)
            slot = lax.rem(k, 2)
            for i in range(3):
                for h in range(wide // LANES):
                    wgrad_ref[i, k * (wide // LANES) + h] = (
                        pair_s[mine, i, h].astype(f32) + pair_got[slot, i, h].astype(f32)).astype(bf)

        step = c * pl.num_programs(1) + r

        partners = [core] + list(dict.fromkeys(s for job in plan for s in job[3] if s != core))

        @pl.when(step == 0)
        def _():
            greet(partners)

        @pl.when(step == 0)
        def _():
            meet(partners)

        def advance(job, stage):
            if stage > 0:
                job.finish(stage - 1)
            if stage < len(job.order):
                job.start(stage)

        for now in range(MOMENTS):
            due = [(job, entry[4].index(now)) for job, entry in zip(jobs, plan) if now in entry[4]]
            if due:
                @pl.when(step == now)
                def _(due=due):
                    for job, stage in due:
                        advance(job, stage)

    def add(off, v):
        ds_s[off:off + v.shape[0], :] += v

    edge, one, two = token_masks(seg_ref[pl.ds(r, 1), :], length, wide)
    dm = nt(dat_ref[rows, :], wo_ref[...])
    gate_out = mixed_ref[0].astype(f32)
    gate_in = mixed_ref[1].astype(f32)
    value = mixed_ref[2].astype(f32)
    d_gate = dm * long_ref[...].astype(f32)
    d_long = dm * gate_out
    sg_ref[0, 5:6, :] += sum0(d_long * (value * gate_in))
    d_conv = None
    for d in range(DOCS):
        x = jnp.where(edge, d_long, 0.0) if d == 0 else jnp.where(edge, 0.0, d_long)
        ys = spread(x[0:n], x[n:2 * n], x[2 * n:])
        parts = []
        for s, off, m in specs_of(length, n):
            t, u = tables[s]
            g = nn(t[...], ys[s])
            ga, gb = g[:m], g[m:]
            qa, qb = spec_ref[off:off + m].astype(f32), spec_ref[off + m:off + 2 * m].astype(f32)
            qc = spec_ref[6 * n:6 * n + m].astype(f32) if s == 0 else qa
            pa, pb = trans_ref[0, d, off:off + m, :].astype(f32), trans_ref[0, d, off + m:off + 2 * m, :].astype(f32)
            back = jnp.concatenate([(ga * qa + gb * qb).astype(bf), (gb * qc - ga * qb).astype(bf)], 0)
            if s == 0:
                add(0, ga * pa)
                add(6 * n, gb * pb)
            else:
                add(off, ga * pa + gb * pb)
            add(off + m, gb * pa - ga * pb)
            parts.append(nn(u[...], back))
        y = jnp.concatenate(gather(*parts), 0)
        d_conv = y if d == 0 else jnp.where(edge, d_conv, y)
    d_inner = skip_ref[pl.ds(pl.multiple_of(c * wide, wide), wide)].reshape(1, wide) * d_long + d_conv * (1.0 / length)
    grads = (d_gate, d_inner * value, d_inner * gate_in)
    for i, (dmx, w, sw) in enumerate(zip(grads, (wg_ref, wi_ref, wv_ref), (swg_ref, swi_ref, swv_ref))):
        a1 = pltpu.roll(jnp.where(one, dmx, 0.0), length - 1, 0)
        a2 = pltpu.roll(jnp.where(two, dmx, 0.0), length - 2, 0)
        dp = (sw[0:1, :] * dmx + sw[1:2, :] * a1 + sw[2:3, :] * a2).astype(bf)
        p = proj_ref[i].astype(f32)
        for k, v in enumerate((p * dmx, p * a1, p * a2, dmx, dp.astype(f32))):
            sg_ref[i, k:k + 1, :] += sum0(v)
        dp_s[i, rows, :] = dp
        dn[rows, :] += nt(dp, w[...])

    @pl.when(jnp.logical_and(c == 0, r == last_row))
    def _():
        for copy in late_copies:
            copy.wait()

    @pl.when(r == last_row)
    def _():
        if links:
            @pl.when(c > 0)
            def _():
                pair_finish(c - 1)

        for i in range(3):
            part = nn(nt_ref[...], dp_s[i]).astype(bf)
            for h in range(wide // LANES):
                if links:
                    tall = pair_s.shape[4]
                    for g in range(pair_s.shape[3]):
                        for k in range(2):
                            top = (2 * g + k) * tall
                            pair_s[k, i, h, g] = part[top:top + tall, h * LANES:(h + 1) * LANES]
                else:
                    wgrad_ref[i, c * (wide // LANES) + h] = part[:, h * LANES:(h + 1) * LANES]
        if links:
            pair_copy(c).start()
        first = lax.broadcasted_iota(jnp.int32, (half, wide), 0) == 0
        extra = ds_s[6 * n:6 * n + half]
        ds_s[0:half] = jnp.where(first, 0.5, 1.0) * (ds_s[0:half] + jnp.where(first, 0.0, extra))
        ds_s[half:n] = jnp.where(first, 0.5 * extra, ds_s[half:n])
        parts = [nn(tables[s][1][...], (ds_s[off:off + 2 * m] * (1.0 / length)).astype(bf)) for s, off, m in specs_of(length, n)]
        gk = jnp.concatenate(gather(*parts), 0) * window(length, rate_ref[...])
        gfw_ref[...] = nn(state_ref[6], gk, HI)
        de3[...] += nt(fw_ref[...], gk, HI)

    @pl.when(c == chunks - 1)
    def _():
        step = 256
        g1 = as_row(g1_ref)
        for i in range(length // step):
            part = slice(i * step, (i + 1) * step)
            there = pl.ds(pl.multiple_of(r * length + i * step, step), step)
            xhat, scale = norm_stats(tok_ref[part, :].astype(f32))
            d = dn[there, :]
            gd = d * g1
            a = jnp.mean(gd, axis=-1, keepdims=True)
            b = jnp.mean(gd * xhat, axis=-1, keepdims=True)
            tg_ref[part, :] = (dat_ref[there, :].astype(f32) + scale * (gd - a - xhat * b)).astype(bf)
            vec_ref[0:1, :] += sum0(d * xhat)
            vec_ref[1:2, :] += sum0(d)

    @pl.when(jnp.logical_and(c == chunks - 1, r == last_row))
    def _():
        ones = jnp.ones((8, length), f32)
        flat = lambda v: nt(ones, v, HI)
        g = de3[...] * state_ref[7]
        gsm_ref[0] = flat(g * state_ref[8])
        g = g * column(oo_ref)
        gsm_ref[1] = flat(g)
        gow_ref[...] = nt(state_ref[3], g, HI)
        g = nn(ow_ref[...], g, HI) * state_ref[4]
        gsm_ref[2] = flat(g * state_ref[5])
        g = g * column(io_ref)
        gsm_ref[3] = flat(g)
        giw_ref[...] = nt(state_ref[0], g, HI)
        g = nn(iw_ref[...], g, HI) * state_ref[1]
        gsm_ref[4] = flat(g * state_ref[2])
        g = g * column(eo_ref)
        gsm_ref[5] = flat(g)
        gew_ref[...] = nt(zt_ref[...], g, HI)
        if links:
            pair_finish(c)
            for job in jobs:
                job.finish(len(job.order) - 1)


MOMENTS = 6


def backward_mixer(links, weg, wrg, wog, dat, tok, segments, g1, wo, longc, mixed, proj, trans, spec, ntr, wm, sw, skip, state, filt, zt, rates,
        tabs, tabst):
    rows_here, length = segments.shape
    total, width = tok.shape
    n = length // 3
    count = width // CHUNK
    ew, eb, eo, iw, ib, io, ow, ob, oo, fw = filt
    hidden = fw.shape[0]
    sds = jax.ShapeDtypeStruct
    plan, grads, moved, scratch = [], [], [], []
    wide_blocks = width // LANES
    wm_shape = (3, wide_blocks, width, LANES)
    if links:
        rows_n, pos_n = links
        alive = [d for d in alive_dims(rows_n, pos_n) if d != ("rows", 0)]
        pair = (3, CHUNK // LANES, rows_n // 2, width // rows_n, LANES)
        wm_shape = (3, wide_blocks, *pair[2:])
        scratch = [pltpu.VMEM((2, *pair), bf), pltpu.VMEM((2, *pair), bf), pltpu.SemaphoreType.DMA, pltpu.SemaphoreType.DMA((2,))]
        full = alive_dims(rows_n, pos_n)
        rows_of = wrg.shape[1] * wrg.shape[2] * wrg.shape[3] * 2
        grads = [weg.reshape(grad_shape(weg.shape[0], width, rows_n, pos_n, False)),
            wrg.reshape(grad_shape(wrg.shape[0], rows_of, rows_n, pos_n, False)),
            wog.reshape(grad_shape(wog.shape[0], width, rows_n, pos_n, True))]
        e_blocks, r_blocks, o_blocks = (g.shape[bits_of(pos_n)] for g in grads)
        first, second, third = three_orders(rows_n, pos_n)
        cut_e, cut_r = 2 * e_blocks // 3, 2 * r_blocks // 3
        plan = [(0, (0, cut_e), alive, first, (0, 3, 4, 5)), (1, (0, cut_r), alive, second, (0, 3, 4, 5)),
            (0, (cut_e, e_blocks - cut_e), alive, third, (0, 3, 4, 5)), (1, (cut_r, r_blocks - cut_r), alive, third, (0, 3, 4, 5)),
            (2, (0, o_blocks), full, [("rows", 0)] + first, (0, 1, 3, 4, 5))]
        for src, (_, blocks), dims, order, _ in plan:
            left = job_shapes(grads[src].shape, blocks, dims, order)
            moved.append(left[-1])
            scratch += job_scratch(left, False) + [pltpu.SemaphoreType.DMA]
    side = dict(collective_id=2, has_side_effects=True) if links else {}
    late = lambda c, r: (jnp.where(c == count - 1, r, 0), 0)
    ins = [*grads, dat, tok, segments, g1, wo, longc, mixed, proj, trans, spec, ntr, wm, wm, wm, sw, sw, sw, skip, state, zt,
        iw, ow, eo, io, oo, fw, rates, *tabs, *tabst]
    specs = [pl.BlockSpec(memory_space=pl.ANY) for g in grads] + [whole_spec(dat), pl.BlockSpec((length, width), late, pipeline_mode=pl.Buffered(1)), whole_spec(segments), whole_spec(g1),
        pl.BlockSpec((CHUNK, width), lambda c, r: (c, 0)), part_spec(length), stack_spec(3, length), stack_spec(3, length),
        pl.BlockSpec((1, DOCS, 2 * length, CHUNK), lambda c, r: (r, 0, 0, c)), column_spec(2 * length + n // 2, 0, count),
        pl.BlockSpec(memory_space=pl.ANY)]
    specs += [column_spec(width, k, count) for k in range(3)] + [column_spec(3, k, count) for k in range(3)]
    specs += [whole_spec(skip), pl.BlockSpec(memory_space=pl.ANY)] + [whole_spec(a) for a in (zt, iw, ow, eo, io, oo)]
    specs += [column_spec(hidden, 0, count), column_spec(1, 0, count)] + [whole_spec(a) for a in (*tabs, *tabst)]
    return pl.pallas_call(
        functools.partial(backward_kernel, links, plan, len(grads)), grid=(count, rows_here), in_specs=specs,
        out_specs=[pl.BlockSpec((length, width), late),
            single(*wm_shape),
            pl.BlockSpec((3, 8, CHUNK), lambda c, r: (0, 0, c)), fixed_spec(8, width), fixed_spec(zt.shape[0], hidden),
            fixed_spec(hidden, hidden), fixed_spec(hidden, hidden), column_spec(hidden, 0, count), fixed_spec(6, 8, hidden)]
            + [single(*s) for s in moved],
        out_shape=[sds((total, width), bf), sds(wm_shape, bf), sds((3, 8, width), f32),
            sds((8, width), f32), sds((zt.shape[0], hidden), f32), sds((hidden, hidden), f32), sds((hidden, hidden), f32),
            sds((hidden, width), f32), sds((6, 8, hidden), f32)]
            + [sds(s, bf) for s in moved],
        scratch_shapes=[pltpu.VMEM((total, width), f32), pltpu.VMEM((hidden, length), f32), pltpu.VMEM((3, total, CHUNK), bf),
            pltpu.VMEM((6 * n + n // 2, CHUNK), f32), pltpu.VMEM(ntr.shape, bf), pltpu.VMEM(state.shape, f32),
            pltpu.SemaphoreType.DMA((2,))] + scratch,
        compiler_params=pltpu.CompilerParams(vmem_limit_bytes=VMEM_BYTES, **side),
        cost_estimate=pl.CostEstimate(
            flops=total * width * (14 * width + 4 * 2 * 5 * n), bytes_accessed=50 * total * width, transcendentals=0),
        name="mixer_backward")(*ins)


def scatter_blocks(grad, rows_n, pos_n, first):
    blocks, height, wide = grad.shape
    if blocks % pos_n:
        flat = grad.transpose(1, 0, 2).reshape(height, blocks * wide)
        wide = blocks * wide // pos_n
        blocks = pos_n
        grad = flat.reshape(height, blocks, wide).transpose(1, 0, 2)
    high = height // rows_n
    rbits, pbits = bits_of(rows_n), bits_of(pos_n)
    acc = grad.reshape((2,) * pbits + (blocks // pos_n,) + (2,) * rbits + (high, wide))
    alive = alive_dims(rows_n, pos_n)
    for axis, bit in order_of(rows_n, pos_n, first):
        dim = alive.index((axis, bit))
        mine = (lax.axis_index(axis) >> bit) & 1
        size = rows_n if axis == "rows" else pos_n
        send = lax.dynamic_index_in_dim(acc, 1 - mine, dim, keepdims=False)
        keep = lax.dynamic_index_in_dim(acc, mine, dim, keepdims=False)
        got = lax.ppermute(send, axis, [(i, i ^ (1 << bit)) for i in range(size)])
        acc = (keep.astype(f32) + got.astype(f32)).astype(bf)
        alive.pop(dim)
    return acc


def pack_places(width, hidden, emb, ff):
    per = width // PACK
    at = {"filter": 0, "square": hidden * per}
    row = at["square"] + hidden
    for name, vectors in (("vec1", 2), ("vec2", 4), ("sgrad", 15), ("skip", 1), ("ebias", ff // width)):
        at[name] = row
        row += vectors * per
    at["small"] = row
    return at, row + 6


def pack_small(at, pk, beg, vec2, sgrad, vec1, gew, giw, gow, gfw, gsm):
    width = vec1.shape[1]
    hidden = giw.shape[0]
    per = width // PACK

    def put(row, value):
        for h in range(per):
            pk[row + h:row + h + 1, :] = value[:, h * PACK:(h + 1) * PACK]

    for k in range(beg.shape[1] // width):
        put(at["ebias"] + k * per, beg[:, k * width:(k + 1) * width])
    for k in range(4):
        put(at["vec2"] + k * per, vec2[k:k + 1, :])
    for i in range(3):
        for k in range(5):
            put(at["sgrad"] + (i * 5 + k) * per, sgrad[i, k:k + 1, :])
    put(at["skip"], sgrad[0, 5:6, :])
    for k in range(2):
        put(at["vec1"] + k * per, vec1[k:k + 1, :])
    for lane, ref in ((0, gew), (128, giw), (256, gow)):
        high = min(ref.shape[0], hidden)
        pk[at["square"]:at["square"] + high, lane:lane + hidden] = ref[0:high, :]
    for h in range(per):
        pk[at["filter"] + h * hidden:at["filter"] + (h + 1) * hidden, :] = gfw[:, h * PACK:(h + 1) * PACK]
    for k in range(6):
        pk[at["small"] + k:at["small"] + k + 1, 0:hidden] = gsm[k, 0:1, :]


def exchange_kernel(sizes, at, plan, count, *refs):
    rows_n, pos_n = sizes
    small = refs[:9]
    grads = refs[9:9 + count]
    pos = 9 + count
    packed_out = refs[pos]
    outs = refs[pos + 1:pos + 1 + len(plan)]
    scratch = list(refs[pos + 1 + len(plan):])
    pk, from_twin, half, rbuf, red, gath, ss1, rs1, ss2, rs2, pair_sems = scratch[:11]
    rest = scratch[11:]
    jobs = []
    for (src, blocks, alive, order), out in zip(plan, outs):
        m = len(order)
        jobs.append(Halving(grads[src], blocks, alive, order, rest[:2 * m - 1] + [out] + rest[2 * m - 1:2 * m + 1]))
        rest = rest[2 * m + 1:]
    n = rows_n * pos_n // 2
    side = pk.shape[0] // 2
    chunk = side // n
    place = lax.axis_index("rows")
    core = lax.rem(place, 2)
    me = (place // 2) * pos_n + lax.axis_index("pos")
    twin = {"rows": place + 1 - 2 * core}

    def ident(t):
        return {"rows": (t // pos_n) * 2 + core, "pos": t % pos_n}

    def each(f):
        def body(k, carry):
            f(lax.rem(me + k, n))
            return carry

        lax.fori_loop(1, n, body, 0)

    def own(t):
        return pl.ds(pl.multiple_of(t * chunk, chunk), chunk)

    def at_side(which, t=None):
        if t is None:
            return pl.ds(pl.multiple_of(which * side, side), side)
        return pl.ds(pl.multiple_of(which * side + t * chunk, chunk), chunk)

    barrier = pltpu.get_barrier_semaphore()
    pl.semaphore_signal(barrier, inc=1, device_id=twin, device_id_type=MESH)
    each(lambda t: pl.semaphore_signal(barrier, inc=1, device_id=ident(t), device_id_type=MESH))
    pk[...] = jnp.zeros_like(pk)
    pack_small(at, pk, *small)
    pl.semaphore_wait(barrier, n)

    to_twin = pltpu.make_async_remote_copy(
        src_ref=pk.at[at_side(1 - core), :], dst_ref=from_twin, send_sem=pair_sems.at[0], recv_sem=pair_sems.at[1],
        device_id=twin, device_id_type=MESH)
    back_twin = pltpu.make_async_remote_copy(
        src_ref=gath.at[at_side(core), :], dst_ref=gath.at[at_side(core), :], send_sem=pair_sems.at[2],
        recv_sem=pair_sems.at[3], device_id=twin, device_id_type=MESH)

    def scatter(t, slot):
        return pltpu.make_async_remote_copy(
            src_ref=half.at[own(t), :], dst_ref=rbuf.at[slot], send_sem=ss1.at[t], recv_sem=rs1.at[slot], device_id=ident(t),
            device_id_type=MESH)

    def publish(t, slot):
        return pltpu.make_async_remote_copy(
            src_ref=red, dst_ref=gath.at[at_side(core, slot), :], send_sem=ss2.at[t], recv_sem=rs2.at[slot],
            device_id=ident(t), device_id_type=MESH)

    def advance(stage):
        for job in jobs:
            if stage < len(job.order):
                job.finish(stage)
                if stage + 1 < len(job.order):
                    job.start(stage + 1)

    to_twin.start()
    for job in jobs:
        job.start(0)
    to_twin.wait()
    half[...] = pk[at_side(core), :] + from_twin[...]
    each(lambda t: scatter(t, me).start())
    rbuf[me] = half[own(me), :]
    advance(0)
    each(lambda t: scatter(t, t).wait())
    total = rbuf[0]
    for s in range(1, n):
        total = total + rbuf[s]
    red[...] = total
    gath[at_side(core, me), :] = total
    each(lambda t: publish(t, me).start())
    stages = max(len(job.order) for job in jobs)
    for stage in range(1, stages - 1):
        advance(stage)
    each(lambda t: publish(t, t).wait())
    back_twin.start()
    advance(stages - 1)
    back_twin.wait()
    packed_out[...] = gath[...]


def exchange(sizes, at, used, small, grads, plan):
    rows_n, pos_n = sizes
    n = rows_n * pos_n
    total = -(-used // (8 * n)) * 8 * n
    chunk = total // n
    vm = pl.BlockSpec(memory_space=pltpu.VMEM)
    tall = lambda rows: pltpu.VMEM((rows, PACK), f32)
    scratch = [tall(total), tall(total // 2), tall(total // 2), pltpu.VMEM((n // 2, chunk, PACK), f32), tall(chunk), tall(total)]
    scratch += [pltpu.SemaphoreType.DMA((n // 2,))] * 4 + [pltpu.SemaphoreType.DMA((4,))]
    shapes = [jax.ShapeDtypeStruct((total, PACK), f32)]
    for src, (start, blocks), alive, order in plan:
        left = job_shapes(grads[src].shape, blocks, alive, order)
        shapes.append(jax.ShapeDtypeStruct(left[-1], bf))
        scratch += job_scratch(left, False)
    return pl.pallas_call(
        functools.partial(exchange_kernel, sizes, at, plan, len(grads)), out_shape=shapes,
        in_specs=[vm] * (9 + len(grads)), out_specs=[vm] * len(shapes), scratch_shapes=scratch,
        compiler_params=pltpu.CompilerParams(collective_id=0, has_side_effects=True, vmem_limit_bytes=VMEM_BYTES),
        name="exchange")(*small, *grads)


def unpack(at, packed, results, blocks, width, hidden, emb, ff):
    per = width // PACK
    counts = [len(parts) for parts in blocks]
    flat = [p for parts in blocks for p in parts]

    def kernel(pk, *refs):
        m = len(results)
        for a, b in zip(refs[:m], refs[len(refs) - m:]):
            b[...] = a[...]

        @pl.when(pl.program_id(0) == 0)
        def _():
            small(pk, *refs[m:len(refs) - m])

    def small(pk, *refs):
        ins = list(refs[:len(flat)])
        fg, fs, mb, sw, sb, ew, eb, eo, iw, ib, io, ow, ob, oo, fw, sk, obias, sg, ss, eb2, rb = refs[len(flat):len(flat) + 21]
        outs = refs[len(flat) + 21:]

        def get(ref, lane, row):
            for h in range(per):
                ref[lane + h * PACK:lane + (h + 1) * PACK] = pk[row + h, :]

        get(fg, 0, at["vec1"])
        get(fs, 0, at["vec1"] + per)
        for i in range(3):
            base = at["sgrad"] + i * 5 * per
            for k in range(3):
                for h in range(per):
                    lane = i * width + h * PACK
                    sw[k:k + 1, lane:lane + PACK] = pk[base + k * per + h:base + k * per + h + 1, :]
            get(sb, i * width, base + 3 * per)
            get(mb, i * width, base + 4 * per)
        q = at["square"]
        ew[...] = pk[q:q + emb, 0:hidden]
        iw[...] = pk[q:q + hidden, 128:128 + hidden]
        ow[...] = pk[q:q + hidden, 256:256 + hidden]
        for k, ref in enumerate((oo, ob, io, ib, eo, eb)):
            ref[...] = pk[at["small"] + k, 0:hidden]
        for h in range(per):
            fw[:, h * PACK:(h + 1) * PACK] = pk[at["filter"] + h * hidden:at["filter"] + (h + 1) * hidden, :]
        get(sk, 0, at["skip"])
        for k, ref in enumerate((sg, ss, obias, rb)):
            get(ref, 0, at["vec2"] + k * per)
        for k in range(ff // width):
            get(eb2, k * width, at["ebias"] + k * per)
        for parts, out in zip(counts, outs):
            lane = 0
            for _ in range(parts):
                src = ins.pop(0)
                for b in range(src.shape[0]):
                    out[:, lane:lane + src.shape[2]] = src[b].astype(f32)
                    lane += src.shape[2]

    s = lambda *d: jax.ShapeDtypeStruct(d, f32)
    shapes = [s(width), s(width), s(3 * width), s(3, 3 * width), s(3 * width), s(emb, hidden), s(hidden), s(hidden),
        s(hidden, hidden), s(hidden), s(hidden), s(hidden, hidden), s(hidden), s(hidden), s(hidden, width), s(width), s(width),
        s(width), s(width), s(ff), s(width)]
    shapes += [s(parts[0].shape[1], sum(p.shape[0] for p in parts) * parts[0].shape[2]) for parts in blocks]
    steps = 6 if results else 1
    whole = lambda a: pl.BlockSpec(a.shape, lambda i: (0,) * len(a.shape))
    part = [pl.BlockSpec((a.shape[0] // steps, a.shape[1]), lambda i: (i, 0)) for a in results]
    return pl.pallas_call(
        kernel, grid=(steps,), out_shape=shapes + [jax.ShapeDtypeStruct(a.shape, a.dtype) for a in results],
        in_specs=[whole(packed)] + part + [whole(a) for a in flat], out_specs=[whole(a) for a in shapes] + part,
        compiler_params=pltpu.CompilerParams(vmem_limit_bytes=VMEM_BYTES), name="unpack")(packed, *results, *flat)


def on_device(sizes, tokens, segments, cotangent, first_gain, first_shift, mixer_weight, mixer_bias, short_weight, short_bias,
        embed_weight, embed_bias, embed_omega, inner_weight, inner_bias, inner_omega, outer_weight, outer_bias, outer_omega,
        filter_weight, skip_gain, output_weight, output_bias, second_gain, second_shift, expand_weight, expand_bias,
        reduce_weight, reduce_bias):
    rows_n, pos_n = sizes
    length, width = tokens.shape[1:]
    emb, hidden = embed_weight.shape
    ff = expand_weight.shape[1]
    tok = tokens.reshape(-1, width)
    cot = cotangent.reshape(-1, width)
    filt = [embed_weight, embed_bias, embed_omega, inner_weight, inner_bias, inner_omega, outer_weight, outer_bias, outer_omega,
        filter_weight]
    tabs, tabst = radix_tables(length)
    zt, rates = filter_inputs(length, emb, width)
    proj, mixed, longc, mix, trans, spec, state, ntr = forward_mixer(
        tok, segments, first_gain, first_shift, mixer_weight, mixer_bias, short_weight, short_bias, skip_gain, filt, zt, rates,
        tabs, tabst)
    direct = rows_n * pos_n == 32 and pos_n == 2 and width % (16 * rows_n) == 0 and width // LANES % pos_n == 0 and ff // rows_n * 4 == width
    links = sizes if direct else None
    out, dat, wog, weg, wrg, beg, vec2 = mlp(
        links, mix, tok, cot, output_weight, output_bias, second_gain, second_shift, expand_weight, expand_bias, reduce_weight,
        reduce_bias)
    tgrad, wmg, sgrad, vec1, gew, giw, gow, gfw, gsm, *early = backward_mixer(
        links, weg, wrg, wog, dat, tok, segments, first_gain, output_weight, longc, mixed, proj, trans, spec, ntr, mixer_weight,
        short_weight, skip_gain, state, filt, zt, rates, tabs, tabst)
    small = (beg, vec2, sgrad, vec1, gew, giw, gow, gfw, gsm)
    at, used = pack_places(width, hidden, emb, ff)
    blocks_m, blocks_o = 3 * width // LANES, width // LANES
    if direct:
        paired = [d for d in alive_dims(rows_n, pos_n) if d != ("rows", 0)]
        third = blocks_m // pos_n // 3
        grads = [wmg.reshape(grad_shape(blocks_m, width, rows_n, pos_n, False))]
        plan = [(0, (k * third, third), paired, order) for k, order in enumerate(three_orders(rows_n, pos_n))]
        packed, *m_parts = exchange(sizes, at, used, small, grads, plan)
        e_a, r_a, e_b, r_b, o_part = early
        blocks = [m_parts, [o_part], [e_a, e_b], [r_a, r_b]]
    else:
        packed = lax.psum(pack_only(at, used, small), ("rows", "pos"))
        grads = [wmg.reshape(blocks_m, width, LANES), wog, weg, wrg]
        blocks = [[scatter_blocks(g, rows_n, pos_n, f)] for g, f in zip(grads, ("pos", "rows", "pos", "rows"))]
    (fg, fs, mb, sw, sb, ew, eb, eo, iw, ib, io, ow, ob, oo, fw, sk, obias, sg, ss, eb2, rb, m_grad, o_grad, e_grad, r_grad, *results) = unpack(
        at, packed, [out, tgrad] if direct else [], blocks, width, hidden, emb, ff)
    if results:
        out, tgrad = results
    return (out.reshape(tokens.shape), tgrad.reshape(tokens.shape), fg, fs, m_grad, mb, sw, sb, ew, eb, eo, iw, ib, io, ow, ob,
        oo, fw, sk, o_grad, obias, sg, ss, e_grad, eb2, r_grad, rb)


def pack_only(at, used, small):
    def kernel(*refs):
        refs[-1][...] = jnp.zeros_like(refs[-1])
        pack_small(at, refs[-1], *refs[:-1])

    vm = pl.BlockSpec(memory_space=pltpu.VMEM)
    return pl.pallas_call(
        kernel, out_shape=jax.ShapeDtypeStruct((used, PACK), f32), in_specs=[vm] * len(small), out_specs=vm, name="pack")(*small)


def solution(mesh):
    both = ("rows", "pos")
    split = P(both, None, None)
    grid = P("rows", "pos")
    in_specs = (split, P(both, None), split) + (P(),) * 25
    out_specs = (split, split, P(), P(), grid) + (P(),) * 14 + (grid, P(), P(), P(), grid, P(), grid, P())
    sizes = (mesh.shape["rows"], mesh.shape["pos"])
    return jax.shard_map(
        functools.partial(on_device, sizes), mesh=mesh, in_specs=in_specs, out_specs=out_specs, check_vma=False)
```

```python
import functools
import math

import jax
import jax.numpy as jnp
import numpy as np
from jax import lax
from jax.experimental import pallas as pl
from jax.experimental.pallas import tpu as pltpu
from jax.sharding import PartitionSpec as P

f32 = jnp.float32
bf = jnp.bfloat16
HI = lax.Precision.HIGHEST
MESH = pl.DeviceIdType.MESH
DOCS = 2
EPSILON = 1e-5
ROOT3 = math.sqrt(3.0) / 2
LANES = 128
CHUNK = 256
PACK = 384
VMEM_BYTES = 63 * 2**20


def nt(a, b, precision=None):
    return lax.dot_general(a, b, (((1,), (1,)), ((), ())), precision=precision, preferred_element_type=f32)


def nn(a, b, precision=None):
    return lax.dot_general(a, b, (((1,), (0,)), ((), ())), precision=precision, preferred_element_type=f32)


def tn(a, b, precision=None):
    return lax.dot_general(a, b, (((0,), (0,)), ((), ())), precision=precision, preferred_element_type=f32)


def three_pass(dot, a, b):
    ah, bh = a.astype(bf), b.astype(bf)
    al, bl = (a - ah.astype(f32)).astype(bf), (b - bh.astype(f32)).astype(bf)
    return dot(ah, bh) + dot(ah, bl) + dot(al, bh)


def norm_stats(x):
    mean = jnp.mean(x, axis=-1, keepdims=True)
    centered = x - mean
    variance = jnp.mean(centered * centered, axis=-1, keepdims=True)
    scale = lax.rsqrt(variance + EPSILON)
    return centered * scale, scale


def sum0(v):
    return jnp.sum(v, axis=0, keepdims=True)


def as_row(ref):
    return ref[...].reshape(1, -1)


def radix_tables(length):
    n = length // 3
    m = 2 * length
    place = np.arange(n)

    def angle(freqs):
        return 2 * np.pi * ((freqs[:, None] * place[None, :]) % m) / m

    even = angle(6 * np.arange(n // 2))
    sine = np.sin(even)
    sine[0] = np.cos(np.pi * place)
    odd = angle(6 * np.arange(n // 2) + 3)
    out = [np.concatenate([np.cos(even), sine], 0), np.concatenate([np.cos(odd), np.sin(odd)], 0)]
    for k in (1, 2):
        turn = angle(6 * np.arange(n) + k)
        c, s = np.cos(turn), np.sin(turn)
        out.append(np.block([[c, -s], [s, c]]))
    low = lambda v: jnp.asarray(v.astype(np.float32)).astype(bf)
    return [low(t) for t in out], [low(t.T) for t in out]


def spread(x0, x1, x2):
    s = x1 + x2
    d = x1 - x2
    y0 = (x0 + s).astype(bf)
    y3 = (x0 - d).astype(bf)
    y1 = jnp.concatenate([(x0 + 0.5 * d).astype(bf), (ROOT3 * s).astype(bf)], 0)
    y2 = jnp.concatenate([(x0 - 0.5 * s).astype(bf), (ROOT3 * d).astype(bf)], 0)
    return y0, y3, y1, y2


def gather(v0, v3, v1, v2):
    n = v0.shape[0]
    v1r, v1i, v2r, v2i = v1[:n], v1[n:], v2[:n], v2[n:]
    even = v0 + v3
    a = 0.5 * (v1r - v2r)
    b = ROOT3 * (v1i + v2i)
    x0 = even + v1r + v2r
    x1 = (v0 - v3) + a + b
    x2 = even - 0.5 * (v1r + v2r) + ROOT3 * (v1i - v2i)
    return x0, x1, x2


def filter_inputs(length, emb, width):
    bands_count = (emb - 1) // 2
    places = np.arange(length, dtype=np.float32)
    tnorm = places / np.float32(length - 1)
    wave = places * np.float32(2.0 * math.pi / length)
    bands = np.linspace(0.0001, bands_count - 1, bands_count).astype(np.float32)
    phase = (wave[:, None] * bands[None, :]).astype(np.float32)
    z = np.concatenate([tnorm[:, None], np.cos(phase), -np.sin(phase)], 1).astype(np.float32)
    zt = np.concatenate([z.T, np.zeros(((-emb) % 8, length), np.float32)], 0)
    rates = np.abs(np.linspace(math.log(0.01) / 1.5, math.log(0.01) / 0.3, width)).astype(np.float32)[None, :]
    return jnp.asarray(zt), jnp.asarray(rates)


def window(length, rate):
    tnorm = lax.broadcasted_iota(jnp.int32, (length, rate.shape[1]), 0).astype(f32) * (1.0 / (length - 1))
    return jnp.exp(-tnorm * rate)


def sin_cos(x):
    k = jnp.floor(x * (1.0 / math.pi) + 0.5)
    r = x - k * 3.140625
    r = r - k * 0.0009670257568359375
    r = r - k * 6.2771141529083251953e-07
    sign = 1.0 - 2.0 * (k - 2.0 * jnp.floor(k * 0.5))
    q = r * r
    s = 1.0 + q * (-1 / 6 + q * (1 / 120 + q * (-1 / 5040 + q * (1 / 362880 + q * (-1 / 39916800 + q * (1 / 6227020800))))))
    c = 1.0 + q * (-1 / 2 + q * (1 / 24 + q * (-1 / 720 + q * (1 / 40320 + q * (-1 / 3628800 + q * (1 / 479001600 - q * (1 / 87178291200)))))))
    return r * s * sign, c * sign


def column(ref):
    v = as_row(ref)
    n = v.shape[1]
    i = lax.broadcasted_iota(jnp.int32, (n, n), 0)
    j = lax.broadcasted_iota(jnp.int32, (n, n), 1)
    return jnp.sum(jnp.where(i == j, v, 0.0), axis=1, keepdims=True)


def token_masks(seg, length, wide):
    edge = jnp.sum((seg == 0).astype(jnp.int32), axis=1, keepdims=True)
    t = lax.broadcasted_iota(jnp.int32, (length, wide), 0)
    one = jnp.logical_and(t != 0, t != edge)
    two = jnp.logical_and(jnp.logical_and(one, t != 1), t != edge + 1)
    return t < edge, one, two


def interleave(streams, lag=1):
    streams = list(streams)
    waiting = [lag * k for k in range(len(streams))]
    while streams:
        for k in range(len(streams)):
            if waiting[k] > 0:
                waiting[k] -= 1
            elif next(streams[k], streams) is streams:
                waiting[k] = None
        streams, waiting = [s for s, w in zip(streams, waiting) if w is not None], [w for w in waiting if w is not None]


def specs_of(length, n):
    return ((0, 0, n // 2), (1, n, n // 2), (2, 2 * n, n), (3, 4 * n, n))


def bits_of(n):
    return n.bit_length() - 1


def order_of(rows_n, pos_n, first):
    rows = [("rows", b) for b in range(1, bits_of(rows_n))]
    pos = [("pos", b) for b in range(bits_of(pos_n))]
    return [("rows", 0)] + (pos + rows if first == "pos" else rows[:1] + pos + rows[1:])


def three_orders(rows_n, pos_n):
    pos = [("pos", b) for b in range(bits_of(pos_n))]
    near = [("rows", b) for b in range(1, bits_of(rows_n) - 1)]
    far = [("rows", bits_of(rows_n) - 1)]
    ring = pos + near
    turn = lambda k: ring[k:] + ring[:k]
    return turn(0) + far, turn(len(pos)) + far, turn(len(ring) - 1) + far


def alive_dims(rows_n, pos_n):
    pos = [("pos", b) for b in reversed(range(bits_of(pos_n)))]
    return pos + [None] + [("rows", b) for b in reversed(range(bits_of(rows_n)))]


def partner(step):
    axis, bit = step
    place = lax.axis_index(axis)
    mine = (place // (1 << bit)) % 2
    return mine, {axis: place + (1 - 2 * mine) * (1 << bit)}


def greet(steps):
    barrier = pltpu.get_barrier_semaphore()
    for step in steps:
        pl.semaphore_signal(barrier, inc=1, device_id=partner(step)[1], device_id_type=MESH)


def meet(steps):
    pl.semaphore_wait(pltpu.get_barrier_semaphore(), len(steps))


class Halving:
    def __init__(self, ref, blocks, alive, order, refs, near=None):
        m = len(order)
        self.near = near
        got, sums, self.send_sem, self.recv_sem = refs[:m], refs[m:2 * m], refs[2 * m], refs[2 * m + 1]
        self.order, self.got, self.sums = order, got, sums
        self.stages = []
        alive = list(alive)
        for k, step in enumerate(order):
            self.stages.append((ref, blocks, tuple(alive), alive.index(step)))
            alive.remove(step)
            ref, blocks = sums[k], (0, blocks[1])

    def pick(self, stage, which):
        ref, (start, count), alive, dim = self.stages[stage]
        index = [slice(None)] * len(alive)
        index[alive.index(None)] = pl.ds(start, count)
        index[dim] = which
        return ref.at[tuple(index)]

    def copy(self, stage):
        mine, there = partner(self.order[stage])
        return pltpu.make_async_remote_copy(
            src_ref=self.pick(stage, 1 - mine), dst_ref=self.got[stage], send_sem=self.send_sem.at[stage],
            recv_sem=self.recv_sem.at[stage], device_id=there, device_id_type=MESH)

    def fetch(self):
        return pltpu.make_async_copy(self.pick(0, partner(self.order[0])[0]), self.sums[0], self.near)

    def start(self, stage):
        self.copy(stage).start()
        if stage == 0 and self.near is not None:
            self.fetch().start()

    def finish(self, stage):
        self.copy(stage).wait()
        if stage == 0 and self.near is not None:
            self.fetch().wait()
        _, (_, count), alive, dim = self.stages[stage]
        kept, got, out = self.pick(stage, partner(self.order[stage])[0]), self.got[stage], self.sums[stage]
        if stage == 0 and self.near is not None:
            kept = out
        split = [d for k, d in enumerate(alive) if k != dim].index(None)

        def add(lead):
            def body(b, carry):
                at = lead + (b,)
                out[at] = (kept[at].astype(f32) + got[at].astype(f32)).astype(bf)
                return carry

            lax.fori_loop(0, count, body, 0)

        leads = [()]
        for _ in range(split):
            leads = [lead + (k,) for lead in leads for k in range(2)]
        for lead in leads:
            add(lead)


def job_shapes(shape, blocks, alive, order):
    dims = list(alive)
    now = [blocks if d is None else 2 for d in dims] + list(shape[-2:])
    out = []
    for step in order:
        k = dims.index(step)
        dims.pop(k)
        now.pop(k)
        out.append(tuple(now))
    return out


def job_scratch(left, last):
    sums = left if last else left[:-1]
    return [pltpu.VMEM(s, bf) for s in left] + [pltpu.VMEM(s, bf) for s in sums] + [pltpu.SemaphoreType.DMA((len(left),))] * 2


def grad_shape(blocks, rows, rows_n, pos_n, cores):
    rbits, pbits = bits_of(rows_n), bits_of(pos_n)
    return (2,) * pbits + (blocks // pos_n,) + (2,) * (rbits - (0 if cores else 1)) + (rows // rows_n, LANES)


def forward_kernel(tok_ref, seg_ref, g1_ref, s1_ref, wg_ref, wi_ref, wv_ref, mb_ref, swg_ref, swi_ref, swv_ref, sb_ref,
        skip_ref, zt_ref, ew_ref, eb_ref, eo_ref, iw_ref, ib_ref, io_ref, ow_ref, ob_ref, oo_ref, fw_ref, rate_ref,
        t0, t3, t1, t2, u0, u3, u1, u2,
        proj_ref, mixed_ref, long_ref, mix_ref, trans_ref, low_ref, state_ref, nt_ref, normed, padded, spec_ref):
    c = pl.program_id(0)
    rows_here, length = seg_ref.shape
    width = tok_ref.shape[1]
    n = length // 3
    half = n // 2
    wide = fw_ref.shape[1]
    tables = ((t0, u0), (t3, u3), (t1, u1), (t2, u2))

    @pl.when(c == 0)
    def _():
        step = 256
        for i in range(tok_ref.shape[0] // step):
            part = slice(i * step, (i + 1) * step)
            xhat, _ = norm_stats(tok_ref[part, :].astype(f32))
            low = (xhat * as_row(g1_ref) + as_row(s1_ref)).astype(bf)
            normed[part, :] = low
            nt_ref[:, part] = low.T

    @pl.when(c == 0)
    def _():
        padded[...] = jnp.zeros_like(padded)
        padded[0:ew_ref.shape[0], :] = ew_ref[...]
        pre = tn(padded[...], zt_ref[...], HI) + column(eb_ref)
        e1, c1 = sin_cos(column(eo_ref) * pre)
        state_ref[0] = e1
        state_ref[1] = c1
        state_ref[2] = pre
        pre = tn(iw_ref[...], e1, HI) + column(ib_ref)
        e2, c2 = sin_cos(column(io_ref) * pre)
        state_ref[3] = e2
        state_ref[4] = c2
        state_ref[5] = pre
        pre = tn(ow_ref[...], e2, HI) + column(ob_ref)
        e3, c3 = sin_cos(column(oo_ref) * pre)
        state_ref[6] = e3
        state_ref[7] = c3
        state_ref[8] = pre

    def spectrum():
        kernel = three_pass(tn, state_ref[6], fw_ref[...]) * window(length, rate_ref[...])
        k = kernel.astype(bf).astype(f32)
        y0, y3, y1, y2 = spread(k[0:n], k[n:2 * n], k[2 * n:])
        yield
        first = lax.broadcasted_iota(jnp.int32, (half, wide), 0) == 0
        q0 = nn(t0[...], y0)
        spec_ref[0:half] = q0[0:half] * jnp.where(first, 0.5, 1.0)
        spec_ref[half:n] = jnp.where(first, 0.0, q0[half:])
        spec_ref[6 * n:6 * n + half] = jnp.where(first, 0.5 * q0[half:], q0[0:half])
        spec_ref[n:2 * n] = nn(t3[...], y3)
        yield
        spec_ref[2 * n:4 * n] = nn(t1[...], y1)
        spec_ref[4 * n:6 * n] = nn(t2[...], y2)
        yield
        low_ref[...] = spec_ref[...].astype(bf)

    mixed = [[None] * 3 for _ in range(rows_here)]
    inner = [None] * rows_here
    masks = [token_masks(seg_ref[r:r + 1, :], length, wide) for r in range(rows_here)]

    def project(r):
        rows = slice(r * length, (r + 1) * length)
        edge, one, two = masks[r]
        for i, (w, sw) in enumerate(((wg_ref, swg_ref), (wi_ref, swi_ref), (wv_ref, swv_ref))):
            at = pl.ds(pl.multiple_of(i * width + c * wide, wide), wide)
            p = nn(normed[rows, :], w[...]) + mb_ref[at].reshape(1, wide)
            yield
            proj_ref[i, rows, :] = p.astype(bf)
            m = (sb_ref[at].reshape(1, wide) + sw[0:1, :] * p + sw[1:2, :] * jnp.where(one, pltpu.roll(p, 1, 0), 0.0)
                + sw[2:3, :] * jnp.where(two, pltpu.roll(p, 2, 0), 0.0))
            mixed_ref[i, rows, :] = m.astype(bf)
            mixed[r][i] = m
        inner[r] = mixed[r][2] * mixed[r][1]

    def convolve(r):
        rows = slice(r * length, (r + 1) * length)
        edge = masks[r][0]
        inner_low = inner[r].astype(bf).astype(f32)
        xs = [jnp.where(edge, inner_low, 0.0), jnp.where(edge, 0.0, inner_low)]
        ys = [jnp.concatenate(pair_of, 1) for pair_of in zip(*(spread(x[0:n], x[n:2 * n], x[2 * n:]) for x in xs))]
        parts = {}
        for s, off, m in specs_of(length, n)[::-1]:
            t, u = tables[s]
            p = nn(t[...], ys[s])
            yield
            qa, qb = spec_ref[off:off + m], spec_ref[off + m:off + 2 * m]
            qc = spec_ref[6 * n:6 * n + m] if s == 0 else qa
            prod = []
            for d in range(DOCS):
                mine = p[:, d * wide:(d + 1) * wide]
                trans_ref[r, d, off:off + 2 * m, :] = mine.astype(bf)
                pa, pb = mine[:m], mine[m:]
                prod.append(jnp.concatenate([(pa * qa - pb * qb).astype(bf), (pa * qb + pb * qc).astype(bf)], 0))
            parts[s] = nn(u[...], jnp.concatenate(prod, 1))
            yield
        y = jnp.concatenate(gather(*(parts[s] for s in range(4))), 0)
        conv = jnp.where(edge, y[:, :wide], y[:, wide:])
        longconv = conv * (1.0 / length) + skip_ref[pl.ds(pl.multiple_of(c * wide, wide), wide)].reshape(1, wide) * inner[r]
        long_ref[rows, :] = longconv.astype(bf)
        mix_ref[rows, :] = (mixed[r][0] * longconv).astype(bf)

    def row_stream(r):
        yield from project(r)
        yield from convolve(r)

    interleave([spectrum()] + [row_stream(r) for r in range(rows_here)], LAG)


LAG = 2


def whole_spec(a):
    return pl.BlockSpec(a.shape, lambda *_: (0,) * a.ndim, pipeline_mode=pl.Buffered(1))


def fixed_spec(*shape):
    return pl.BlockSpec(shape, lambda *_: (0,) * len(shape))


def column_spec(rows, k, count):
    return pl.BlockSpec((rows, CHUNK), lambda c, r=0: (0, k * count + c))


def part_spec(length):
    return pl.BlockSpec((length, CHUNK), lambda c, r=0: (r, c))


def stack_spec(count, length):
    return pl.BlockSpec((count, length, CHUNK), lambda c, r=0: (0, r, c))


def vector_chunk():
    return pl.BlockSpec((CHUNK,), lambda c, r: (c,))


def forward_mixer(tok, segments, g1, s1, wm, mb, sw, sb, skip, filt, zt, rates, tabs, tabst):
    rows_here, length = segments.shape
    total, width = tok.shape
    n = length // 3
    count = width // CHUNK
    fw = filt[-1]
    hidden = fw.shape[0]
    sds = jax.ShapeDtypeStruct
    ins = [tok, segments, g1, s1, wm, wm, wm, mb, sw, sw, sw, sb, skip, zt, *filt, rates, *tabs, *tabst]
    specs = [whole_spec(a) for a in (tok, segments, g1, s1)]
    specs += [column_spec(width, k, count) for k in range(3)] + [whole_spec(mb)] + [column_spec(3, k, count) for k in range(3)]
    specs += [whole_spec(sb), whole_spec(skip), whole_spec(zt)] + [whole_spec(a) for a in filt[:-1]]
    specs += [column_spec(hidden, 0, count), column_spec(1, 0, count)] + [whole_spec(a) for a in (*tabs, *tabst)]
    return pl.pallas_call(
        forward_kernel, grid=(count,), in_specs=specs,
        out_specs=[stack_spec(3, total), stack_spec(3, total), part_spec(total), part_spec(total),
            pl.BlockSpec((rows_here, DOCS, 2 * length, CHUNK), lambda c: (0, 0, 0, c)), column_spec(2 * length + n // 2, 0, count),
            fixed_spec(9, hidden, length), fixed_spec(width, total)],
        out_shape=[sds((3, total, width), bf), sds((3, total, width), bf), sds((total, width), bf), sds((total, width), bf),
            sds((rows_here, DOCS, 2 * length, width), bf), sds((2 * length + n // 2, width), bf),
            sds((9, hidden, length), f32), sds((width, total), bf)],
        scratch_shapes=[pltpu.VMEM((total, width), bf), pltpu.VMEM((zt.shape[0], hidden), f32),
            pltpu.VMEM((2 * length + n // 2, CHUNK), f32)],
        compiler_params=pltpu.CompilerParams(vmem_limit_bytes=VMEM_BYTES),
        cost_estimate=pl.CostEstimate(
            flops=total * width * (6 * width + 4 * 2 * 5 * n), bytes_accessed=40 * total * width, transcendentals=0),
        name="mixer_forward")(*ins)


def gelu_parts(e):
    d = 1.0 + (0.3275911 / math.sqrt(2)) * jnp.abs(e)
    t = pl.reciprocal(d, approx=True)
    t = t * (2.0 - d * t)
    bell = jnp.exp(e * e * (-0.5))
    poly = t * (0.5 * 0.254829592 + t * (0.5 * -0.284496736 + t * (0.5 * 1.421413741 + t * (0.5 * -1.453152027 + t * (0.5 * 1.061405429)))))
    tail = poly * bell
    phi = jnp.where(e >= 0, 1.0 - tail, tail)
    return phi, phi + e * bell * (1 / math.sqrt(2 * math.pi))


def mlp_kernel(links, mix_ref, tok_ref, cot_ref, wo_ref, bo_ref, g2_ref, s2_ref, we_ref, be_ref, wr_ref, br_ref,
        out_ref, dat_ref, wog_ref, weg_ref, wrg_ref, beg_ref, vec_ref, hid, acc, dn2, n2, n2t, cott, act, de, *pair):
    j = pl.program_id(0)
    last = pl.num_programs(0) - 1
    total, width = tok_ref.shape
    part_ff = we_ref.shape[1]
    step = 512
    steps = total // step

    def at(i, size=step):
        return pl.ds(pl.multiple_of(i * size, size), size)

    core = ("rows", 0)
    if links:
        ahead_s, back_s, ahead_got, back_got, send_sem, recv_sem = pair

        def copies(k):
            mine, there = partner(core)
            slot = lax.rem(k, 2)
            return [
                pltpu.make_async_remote_copy(
                    src_ref=src.at[1 - mine], dst_ref=dst.at[slot], send_sem=send_sem.at[w], recv_sem=recv_sem.at[w, slot],
                    device_id=there, device_id_type=MESH)
                for w, (src, dst) in enumerate(((ahead_s, ahead_got), (back_s, back_got)))]

        def finish(k):
            for copy in copies(k):
                copy.wait()
            mine, _ = partner(core)
            slot = lax.rem(k, 2)
            count = ahead_s.shape[1]

            def add(b, carry):
                weg_ref[k * count + b] = (ahead_s[mine, b].astype(f32) + ahead_got[slot, b].astype(f32)).astype(bf)
                wrg_ref[b, k] = (back_s[mine, b].astype(f32) + back_got[slot, b].astype(f32)).astype(bf)
                return carry

            lax.fori_loop(0, count, add, 0)

    @pl.when(j == 0)
    def _():
        if links:
            greet([core])

        def body(i, carry):
            rows = at(i)
            h = tok_ref[rows, :].astype(f32) + nn(mix_ref[rows, :], wo_ref[...]) + as_row(bo_ref)
            hid[rows, :] = h
            xhat, _ = norm_stats(h)
            n2[rows, :] = (xhat * as_row(g2_ref) + as_row(s2_ref)).astype(bf)
            acc[rows, :] = h + as_row(br_ref)
            dn2[rows, :] = jnp.zeros((step, width), f32)
            return carry

        lax.fori_loop(0, steps, body, 0)
        for i in range(steps):
            rows = slice(i * step, (i + 1) * step)
            n2t[:, rows] = n2[rows, :].T
            cott[:, rows] = cot_ref[rows, :].T

    def tile(i, carry):
        rows = at(i)
        e = nn(n2[rows, :], we_ref[...]) + be_ref[pl.ds(pl.multiple_of(j * part_ff, part_ff), part_ff)].reshape(1, part_ff)
        da = nt(cot_ref[rows, :], wr_ref[...])
        phi, slope = gelu_parts(e)
        a = (e * phi).astype(bf)
        d = (da * slope).astype(bf)
        act[rows, :] = a
        de[rows, :] = d
        acc[rows, :] += nn(a, wr_ref[...])
        dn2[rows, :] += nt(d, we_ref[...])
        return carry + sum0(d.astype(f32))

    beg_ref[...] = lax.fori_loop(0, steps, tile, jnp.zeros((1, part_ff), f32))

    def grads(i, carry):
        rows = at(i, 384)
        back = nn(cott[rows, :], act[...]).astype(bf).T
        ahead = nn(n2t[rows, :], de[...]).astype(bf)
        blocks = 384 // LANES
        if links:
            tall = back_s.shape[3]
            for h in range(blocks):
                for y in range(back_s.shape[2]):
                    for k in range(2):
                        top = (2 * y + k) * tall
                        back_s[k, i * blocks + h, y] = back[top:top + tall, h * LANES:(h + 1) * LANES]
            tall = ahead_s.shape[3]
            groups = 384 // (2 * tall)
            for h in range(part_ff // LANES):
                for g in range(groups):
                    for k in range(2):
                        top = (2 * g + k) * tall
                        ahead_s[k, h, i * groups + g] = ahead[top:top + tall, h * LANES:(h + 1) * LANES]
        else:
            for h in range(blocks):
                wrg_ref[i * blocks + h, pl.ds(pl.multiple_of(j * part_ff, part_ff), part_ff), :] = back[:, h * LANES:(h + 1) * LANES]
            for h in range(part_ff // LANES):
                weg_ref[j * (part_ff // LANES) + h, rows, :] = ahead[:, h * LANES:(h + 1) * LANES]
        return carry

    if links:
        @pl.when(j > 0)
        def _():
            finish(j - 1)

    lax.fori_loop(0, width // 384, grads, 0)
    if links:
        @pl.when(j == 0)
        def _():
            meet([core])

        for copy in copies(j):
            copy.start()

    @pl.when(j == last)
    def _():
        def body(i, carry):
            rows = at(i)
            out_ref[rows, :] = acc[rows, :].astype(bf)
            xhat, scale = norm_stats(hid[rows, :])
            dn = dn2[rows, :]
            gd = dn * as_row(g2_ref)
            m1 = jnp.mean(gd, axis=-1, keepdims=True)
            m2 = jnp.mean(gd * xhat, axis=-1, keepdims=True)
            cot = cot_ref[rows, :].astype(f32)
            low = (cot + scale * (gd - m1 - xhat * m2)).astype(bf)
            dat_ref[rows, :] = low
            return (carry[0] + sum0(dn * xhat), carry[1] + sum0(dn), carry[2] + sum0(low.astype(f32)), carry[3] + sum0(cot))

        zero = jnp.zeros((1, width), f32)
        sums = lax.fori_loop(0, steps, body, (zero,) * 4)
        for k in range(4):
            vec_ref[k:k + 1, :] = sums[k]
        for i in range(steps):
            rows = slice(i * step, (i + 1) * step)
            n2t[:, rows] = mix_ref[rows, :].T

        def weights(i, carry):
            rows = at(i, 256)
            part = nn(n2t[rows, :], dat_ref[...]).astype(bf)
            for h in range(width // LANES):
                wog_ref[h, rows, :] = part[:, h * LANES:(h + 1) * LANES]
            return carry

        lax.fori_loop(0, width // 256, weights, 0)
        if links:
            finish(j)


def single(*shape):
    return pl.BlockSpec(shape, lambda *_: (0,) * len(shape), pipeline_mode=pl.Buffered(1))


def mlp(links, mix, tok, cot, wo, bo, g2, s2, we, be, wr, br, part_ff=768):
    total, width = tok.shape
    ff = we.shape[1]
    sds = jax.ShapeDtypeStruct
    blocks = width // LANES
    parts = ff // part_ff
    scratch = [pltpu.VMEM((total, width), f32)] * 3 + [pltpu.VMEM((total, width), bf)]
    scratch += [pltpu.VMEM((width, total), bf)] * 2 + [pltpu.VMEM((total, part_ff), bf)] * 2
    if links:
        rows_n = links[0]
        pairs = rows_n // 2
        ahead = (ff // LANES, pairs, width // rows_n, LANES)
        back = (blocks, parts, pairs // parts, ff // rows_n, LANES)
        for shape in ((part_ff // LANES, *ahead[1:]), (blocks, *back[2:])):
            scratch.append(pltpu.VMEM((2, *shape), bf))
        for shape in ((part_ff // LANES, *ahead[1:]), (blocks, *back[2:])):
            scratch.append(pltpu.VMEM((2, *shape), bf))
        scratch += [pltpu.SemaphoreType.DMA((2,)), pltpu.SemaphoreType.DMA((2, 2))]
    else:
        ahead, back = (ff // LANES, width, LANES), (blocks, ff, LANES)
    side = dict(collective_id=1, has_side_effects=True) if links else {}
    return pl.pallas_call(
        functools.partial(mlp_kernel, links), grid=(parts,),
        in_specs=[whole_spec(a) for a in (mix, tok, cot, wo, bo, g2, s2)]
            + [pl.BlockSpec((width, part_ff), lambda j: (0, j)), whole_spec(be), pl.BlockSpec((part_ff, width), lambda j: (j, 0)),
                whole_spec(br)],
        out_specs=[single(total, width), single(total, width), single(blocks, width, LANES), single(*ahead), single(*back),
            pl.BlockSpec((1, part_ff), lambda j: (0, j)), single(8, width)],
        out_shape=[sds((total, width), bf), sds((total, width), bf), sds((blocks, width, LANES), bf), sds(ahead, bf),
            sds(back, bf), sds((1, ff), f32), sds((8, width), f32)],
        scratch_shapes=scratch,
        compiler_params=pltpu.CompilerParams(vmem_limit_bytes=VMEM_BYTES, **side),
        cost_estimate=pl.CostEstimate(
            flops=12 * total * width * ff + 4 * total * width * width, bytes_accessed=30 * total * width,
            transcendentals=total * ff),
        name="mlp")(mix, tok, cot, wo, bo, g2, s2, we, be, wr, br)


def backward_kernel(links, plan, sources, *refs):
    moved = len(plan)
    grads, refs = refs[:sources], refs[sources:]
    (dat_ref, tok_ref, seg_ref, g1_ref, wo_ref, long_ref, mixed_ref, proj_ref, trans_ref, spec_ref, nt_far,
        wg_ref, wi_ref, wv_ref, swg_ref, swi_ref, swv_ref, skip_ref, state_far, zt_ref, iw_ref, ow_ref, eo_ref, io_ref,
        oo_ref, fw_ref, rate_ref, t0, t3, t1, t2, u0, u3, u1, u2,
        tg_ref, wgrad_ref, sg_ref, vec_ref, gew_ref, giw_ref, gow_ref, gfw_ref, gsm_ref) = refs[:44]
    outs, (dn, de3, dp_s, ds_s, nt_ref, state_ref, late_sems, *pair) = refs[44:44 + moved], refs[44 + moved:]
    c = pl.program_id(0)
    r = pl.program_id(1)
    chunks = pl.num_programs(0)
    last_row = pl.num_programs(1) - 1
    length, wide = long_ref.shape
    n = length // 3
    half = n // 2
    rows = pl.ds(pl.multiple_of(r * length, length), length)
    tables = ((t0, u0), (t3, u3), (t1, u1), (t2, u2))

    late_copies = [pltpu.make_async_copy(a, b, late_sems.at[k]) for k, (a, b) in enumerate(((nt_far, nt_ref), (state_far, state_ref)))]

    @pl.when(jnp.logical_and(c == 0, r == 0))
    def _():
        for copy in late_copies:
            copy.start()

    @pl.when(r == 0)
    def _():
        ds_s[...] = jnp.zeros_like(ds_s)
        sg_ref[...] = jnp.zeros_like(sg_ref)

    @pl.when(jnp.logical_and(c == 0, r == 0))
    def _():
        dn[...] = jnp.zeros_like(dn)
        de3[...] = jnp.zeros_like(de3)
        vec_ref[...] = jnp.zeros_like(vec_ref)

    core = ("rows", 0)
    jobs = []
    if links:
        pair_s, pair_got, pair_send, pair_recv = pair[:4]
        rest = list(pair[4:])
        for (src, blocks, alive, order, _), out in zip(plan, outs):
            m = len(order)
            jobs.append(Halving(grads[src], blocks, alive, order, rest[:2 * m - 1] + [out] + rest[2 * m - 1:2 * m + 1],
                rest[2 * m + 1]))
            rest = rest[2 * m + 2:]

        def pair_copy(k):
            mine, there = partner(core)
            slot = lax.rem(k, 2)
            return pltpu.make_async_remote_copy(
                src_ref=pair_s.at[1 - mine], dst_ref=pair_got.at[slot], send_sem=pair_send, recv_sem=pair_recv.at[slot],
                device_id=there, device_id_type=MESH)

        def pair_finish(k):
            pair_copy(k).wait()
            mine, _ = partner(core)
            slot = lax.rem(k, 2)
            for i in range(3):
                for h in range(wide // LANES):
                    wgrad_ref[i, k * (wide // LANES) + h] = (
                        pair_s[mine, i, h].astype(f32) + pair_got[slot, i, h].astype(f32)).astype(bf)

        step = c * pl.num_programs(1) + r

        partners = [core] + list(dict.fromkeys(s for job in plan for s in job[3] if s != core))

        @pl.when(step == 0)
        def _():
            greet(partners)

        @pl.when(step == 0)
        def _():
            meet(partners)

        def advance(job, stage):
            if stage > 0:
                job.finish(stage - 1)
            if stage < len(job.order):
                job.start(stage)

        for now in range(MOMENTS):
            due = [(job, entry[4].index(now)) for job, entry in zip(jobs, plan) if now in entry[4]]
            if due:
                @pl.when(step == now)
                def _(due=due):
                    for job, stage in due:
                        advance(job, stage)

    def add(off, v):
        ds_s[off:off + v.shape[0], :] += v

    edge, one, two = token_masks(seg_ref[pl.ds(r, 1), :], length, wide)
    dm = nt(dat_ref[rows, :], wo_ref[...])
    gate_out = mixed_ref[0].astype(f32)
    gate_in = mixed_ref[1].astype(f32)
    value = mixed_ref[2].astype(f32)
    d_gate = dm * long_ref[...].astype(f32)
    d_long = dm * gate_out
    sg_ref[0, 5:6, :] += sum0(d_long * (value * gate_in))
    d_conv = None
    for d in range(DOCS):
        x = jnp.where(edge, d_long, 0.0) if d == 0 else jnp.where(edge, 0.0, d_long)
        ys = spread(x[0:n], x[n:2 * n], x[2 * n:])
        parts = []
        for s, off, m in specs_of(length, n):
            t, u = tables[s]
            g = nn(t[...], ys[s])
            ga, gb = g[:m], g[m:]
            qa, qb = spec_ref[off:off + m].astype(f32), spec_ref[off + m:off + 2 * m].astype(f32)
            qc = spec_ref[6 * n:6 * n + m].astype(f32) if s == 0 else qa
            pa, pb = trans_ref[0, d, off:off + m, :].astype(f32), trans_ref[0, d, off + m:off + 2 * m, :].astype(f32)
            back = jnp.concatenate([(ga * qa + gb * qb).astype(bf), (gb * qc - ga * qb).astype(bf)], 0)
            if s == 0:
                add(0, ga * pa)
                add(6 * n, gb * pb)
            else:
                add(off, ga * pa + gb * pb)
            add(off + m, gb * pa - ga * pb)
            parts.append(nn(u[...], back))
        y = jnp.concatenate(gather(*parts), 0)
        d_conv = y if d == 0 else jnp.where(edge, d_conv, y)
    d_inner = skip_ref[pl.ds(pl.multiple_of(c * wide, wide), wide)].reshape(1, wide) * d_long + d_conv * (1.0 / length)
    grads = (d_gate, d_inner * value, d_inner * gate_in)
    for i, (dmx, w, sw) in enumerate(zip(grads, (wg_ref, wi_ref, wv_ref), (swg_ref, swi_ref, swv_ref))):
        a1 = pltpu.roll(jnp.where(one, dmx, 0.0), length - 1, 0)
        a2 = pltpu.roll(jnp.where(two, dmx, 0.0), length - 2, 0)
        dp = (sw[0:1, :] * dmx + sw[1:2, :] * a1 + sw[2:3, :] * a2).astype(bf)
        p = proj_ref[i].astype(f32)
        for k, v in enumerate((p * dmx, p * a1, p * a2, dmx, dp.astype(f32))):
            sg_ref[i, k:k + 1, :] += sum0(v)
        dp_s[i, rows, :] = dp
        dn[rows, :] += nt(dp, w[...])

    @pl.when(jnp.logical_and(c == 0, r == last_row))
    def _():
        for copy in late_copies:
            copy.wait()

    @pl.when(r == last_row)
    def _():
        if links:
            @pl.when(c > 0)
            def _():
                pair_finish(c - 1)

        for i in range(3):
            part = nn(nt_ref[...], dp_s[i]).astype(bf)
            for h in range(wide // LANES):
                if links:
                    tall = pair_s.shape[4]
                    for g in range(pair_s.shape[3]):
                        for k in range(2):
                            top = (2 * g + k) * tall
                            pair_s[k, i, h, g] = part[top:top + tall, h * LANES:(h + 1) * LANES]
                else:
                    wgrad_ref[i, c * (wide // LANES) + h] = part[:, h * LANES:(h + 1) * LANES]
        if links:
            pair_copy(c).start()
        first = lax.broadcasted_iota(jnp.int32, (half, wide), 0) == 0
        extra = ds_s[6 * n:6 * n + half]
        ds_s[0:half] = jnp.where(first, 0.5, 1.0) * (ds_s[0:half] + jnp.where(first, 0.0, extra))
        ds_s[half:n] = jnp.where(first, 0.5 * extra, ds_s[half:n])
        parts = [nn(tables[s][1][...], (ds_s[off:off + 2 * m] * (1.0 / length)).astype(bf)) for s, off, m in specs_of(length, n)]
        gk = jnp.concatenate(gather(*parts), 0) * window(length, rate_ref[...])
        gfw_ref[...] = nn(state_ref[6], gk, HI)
        de3[...] += nt(fw_ref[...], gk, HI)

    @pl.when(c == chunks - 1)
    def _():
        step = 256
        g1 = as_row(g1_ref)
        for i in range(length // step):
            part = slice(i * step, (i + 1) * step)
            there = pl.ds(pl.multiple_of(r * length + i * step, step), step)
            xhat, scale = norm_stats(tok_ref[part, :].astype(f32))
            d = dn[there, :]
            gd = d * g1
            a = jnp.mean(gd, axis=-1, keepdims=True)
            b = jnp.mean(gd * xhat, axis=-1, keepdims=True)
            tg_ref[part, :] = (dat_ref[there, :].astype(f32) + scale * (gd - a - xhat * b)).astype(bf)
            vec_ref[0:1, :] += sum0(d * xhat)
            vec_ref[1:2, :] += sum0(d)

    @pl.when(jnp.logical_and(c == chunks - 1, r == last_row))
    def _():
        ones = jnp.ones((8, length), f32)
        flat = lambda v: nt(ones, v, HI)
        g = de3[...] * state_ref[7]
        gsm_ref[0] = flat(g * state_ref[8])
        g = g * column(oo_ref)
        gsm_ref[1] = flat(g)
        gow_ref[...] = nt(state_ref[3], g, HI)
        g = nn(ow_ref[...], g, HI) * state_ref[4]
        gsm_ref[2] = flat(g * state_ref[5])
        g = g * column(io_ref)
        gsm_ref[3] = flat(g)
        giw_ref[...] = nt(state_ref[0], g, HI)
        g = nn(iw_ref[...], g, HI) * state_ref[1]
        gsm_ref[4] = flat(g * state_ref[2])
        g = g * column(eo_ref)
        gsm_ref[5] = flat(g)
        gew_ref[...] = nt(zt_ref[...], g, HI)
        if links:
            pair_finish(c)
            for job in jobs:
                job.finish(len(job.order) - 1)


MOMENTS = 6


def backward_mixer(links, weg, wrg, wog, dat, tok, segments, g1, wo, longc, mixed, proj, trans, spec, ntr, wm, sw, skip, state, filt, zt, rates,
        tabs, tabst):
    rows_here, length = segments.shape
    total, width = tok.shape
    n = length // 3
    count = width // CHUNK
    ew, eb, eo, iw, ib, io, ow, ob, oo, fw = filt
    hidden = fw.shape[0]
    sds = jax.ShapeDtypeStruct
    plan, grads, moved, scratch = [], [], [], []
    wide_blocks = width // LANES
    wm_shape = (3, wide_blocks, width, LANES)
    if links:
        rows_n, pos_n = links
        alive = [d for d in alive_dims(rows_n, pos_n) if d != ("rows", 0)]
        pair = (3, CHUNK // LANES, rows_n // 2, width // rows_n, LANES)
        wm_shape = (3, wide_blocks, *pair[2:])
        scratch = [pltpu.VMEM((2, *pair), bf), pltpu.VMEM((2, *pair), bf), pltpu.SemaphoreType.DMA, pltpu.SemaphoreType.DMA((2,))]
        full = alive_dims(rows_n, pos_n)
        rows_of = wrg.shape[1] * wrg.shape[2] * wrg.shape[3] * 2
        grads = [weg.reshape(grad_shape(weg.shape[0], width, rows_n, pos_n, False)),
            wrg.reshape(grad_shape(wrg.shape[0], rows_of, rows_n, pos_n, False)),
            wog.reshape(grad_shape(wog.shape[0], width, rows_n, pos_n, True))]
        e_blocks, r_blocks, o_blocks = (g.shape[bits_of(pos_n)] for g in grads)
        first, second, third = three_orders(rows_n, pos_n)
        cut_e, cut_r = 2 * e_blocks // 3, 2 * r_blocks // 3
        plan = [(0, (0, cut_e), alive, first, (0, 3, 4, 5)), (1, (0, cut_r), alive, second, (0, 3, 4, 5)),
            (0, (cut_e, e_blocks - cut_e), alive, third, (0, 3, 4, 5)), (1, (cut_r, r_blocks - cut_r), alive, third, (0, 3, 4, 5)),
            (2, (0, o_blocks), full, [("rows", 0)] + first, (0, 1, 3, 4, 5))]
        for src, (_, blocks), dims, order, _ in plan:
            left = job_shapes(grads[src].shape, blocks, dims, order)
            moved.append(left[-1])
            scratch += job_scratch(left, False) + [pltpu.SemaphoreType.DMA]
    side = dict(collective_id=2, has_side_effects=True) if links else {}
    late = lambda c, r: (jnp.where(c == count - 1, r, 0), 0)
    ins = [*grads, dat, tok, segments, g1, wo, longc, mixed, proj, trans, spec, ntr, wm, wm, wm, sw, sw, sw, skip, state, zt,
        iw, ow, eo, io, oo, fw, rates, *tabs, *tabst]
    specs = [pl.BlockSpec(memory_space=pl.ANY) for g in grads] + [whole_spec(dat), pl.BlockSpec((length, width), late, pipeline_mode=pl.Buffered(1)), whole_spec(segments), whole_spec(g1),
        pl.BlockSpec((CHUNK, width), lambda c, r: (c, 0)), part_spec(length), stack_spec(3, length), stack_spec(3, length),
        pl.BlockSpec((1, DOCS, 2 * length, CHUNK), lambda c, r: (r, 0, 0, c)), column_spec(2 * length + n // 2, 0, count),
        pl.BlockSpec(memory_space=pl.ANY)]
    specs += [column_spec(width, k, count) for k in range(3)] + [column_spec(3, k, count) for k in range(3)]
    specs += [whole_spec(skip), pl.BlockSpec(memory_space=pl.ANY)] + [whole_spec(a) for a in (zt, iw, ow, eo, io, oo)]
    specs += [column_spec(hidden, 0, count), column_spec(1, 0, count)] + [whole_spec(a) for a in (*tabs, *tabst)]
    return pl.pallas_call(
        functools.partial(backward_kernel, links, plan, len(grads)), grid=(count, rows_here), in_specs=specs,
        out_specs=[pl.BlockSpec((length, width), late),
            single(*wm_shape),
            pl.BlockSpec((3, 8, CHUNK), lambda c, r: (0, 0, c)), fixed_spec(8, width), fixed_spec(zt.shape[0], hidden),
            fixed_spec(hidden, hidden), fixed_spec(hidden, hidden), column_spec(hidden, 0, count), fixed_spec(6, 8, hidden)]
            + [single(*s) for s in moved],
        out_shape=[sds((total, width), bf), sds(wm_shape, bf), sds((3, 8, width), f32),
            sds((8, width), f32), sds((zt.shape[0], hidden), f32), sds((hidden, hidden), f32), sds((hidden, hidden), f32),
            sds((hidden, width), f32), sds((6, 8, hidden), f32)]
            + [sds(s, bf) for s in moved],
        scratch_shapes=[pltpu.VMEM((total, width), f32), pltpu.VMEM((hidden, length), f32), pltpu.VMEM((3, total, CHUNK), bf),
            pltpu.VMEM((6 * n + n // 2, CHUNK), f32), pltpu.VMEM(ntr.shape, bf), pltpu.VMEM(state.shape, f32),
            pltpu.SemaphoreType.DMA((2,))] + scratch,
        compiler_params=pltpu.CompilerParams(vmem_limit_bytes=VMEM_BYTES, **side),
        cost_estimate=pl.CostEstimate(
            flops=total * width * (14 * width + 4 * 2 * 5 * n), bytes_accessed=50 * total * width, transcendentals=0),
        name="mixer_backward")(*ins)


def scatter_blocks(grad, rows_n, pos_n, first):
    blocks, height, wide = grad.shape
    if blocks % pos_n:
        flat = grad.transpose(1, 0, 2).reshape(height, blocks * wide)
        wide = blocks * wide // pos_n
        blocks = pos_n
        grad = flat.reshape(height, blocks, wide).transpose(1, 0, 2)
    high = height // rows_n
    rbits, pbits = bits_of(rows_n), bits_of(pos_n)
    acc = grad.reshape((2,) * pbits + (blocks // pos_n,) + (2,) * rbits + (high, wide))
    alive = alive_dims(rows_n, pos_n)
    for axis, bit in order_of(rows_n, pos_n, first):
        dim = alive.index((axis, bit))
        mine = (lax.axis_index(axis) >> bit) & 1
        size = rows_n if axis == "rows" else pos_n
        send = lax.dynamic_index_in_dim(acc, 1 - mine, dim, keepdims=False)
        keep = lax.dynamic_index_in_dim(acc, mine, dim, keepdims=False)
        got = lax.ppermute(send, axis, [(i, i ^ (1 << bit)) for i in range(size)])
        acc = (keep.astype(f32) + got.astype(f32)).astype(bf)
        alive.pop(dim)
    return acc


def pack_places(width, hidden, emb, ff):
    per = width // PACK
    at = {"filter": 0, "square": hidden * per}
    row = at["square"] + hidden
    for name, vectors in (("vec1", 2), ("vec2", 4), ("sgrad", 15), ("skip", 1), ("ebias", ff // width)):
        at[name] = row
        row += vectors * per
    at["small"] = row
    return at, row + 6


def pack_small(at, pk, beg, vec2, sgrad, vec1, gew, giw, gow, gfw, gsm):
    width = vec1.shape[1]
    hidden = giw.shape[0]
    per = width // PACK

    def put(row, value):
        for h in range(per):
            pk[row + h:row + h + 1, :] = value[:, h * PACK:(h + 1) * PACK]

    for k in range(beg.shape[1] // width):
        put(at["ebias"] + k * per, beg[:, k * width:(k + 1) * width])
    for k in range(4):
        put(at["vec2"] + k * per, vec2[k:k + 1, :])
    for i in range(3):
        for k in range(5):
            put(at["sgrad"] + (i * 5 + k) * per, sgrad[i, k:k + 1, :])
    put(at["skip"], sgrad[0, 5:6, :])
    for k in range(2):
        put(at["vec1"] + k * per, vec1[k:k + 1, :])
    for lane, ref in ((0, gew), (128, giw), (256, gow)):
        high = min(ref.shape[0], hidden)
        pk[at["square"]:at["square"] + high, lane:lane + hidden] = ref[0:high, :]
    for h in range(per):
        pk[at["filter"] + h * hidden:at["filter"] + (h + 1) * hidden, :] = gfw[:, h * PACK:(h + 1) * PACK]
    for k in range(6):
        pk[at["small"] + k:at["small"] + k + 1, 0:hidden] = gsm[k, 0:1, :]


def exchange_kernel(sizes, at, plan, count, *refs):
    rows_n, pos_n = sizes
    small = refs[:9]
    grads = refs[9:9 + count]
    pos = 9 + count
    packed_out = refs[pos]
    outs = refs[pos + 1:pos + 1 + len(plan)]
    scratch = list(refs[pos + 1 + len(plan):])
    pk, from_twin, half, rbuf, red, gath, ss1, rs1, ss2, rs2, pair_sems = scratch[:11]
    rest = scratch[11:]
    jobs = []
    for (src, blocks, alive, order), out in zip(plan, outs):
        m = len(order)
        jobs.append(Halving(grads[src], blocks, alive, order, rest[:2 * m - 1] + [out] + rest[2 * m - 1:2 * m + 1]))
        rest = rest[2 * m + 1:]
    n = rows_n * pos_n // 2
    side = pk.shape[0] // 2
    chunk = side // n
    place = lax.axis_index("rows")
    core = lax.rem(place, 2)
    me = (place // 2) * pos_n + lax.axis_index("pos")
    twin = {"rows": place + 1 - 2 * core}

    def ident(t):
        return {"rows": (t // pos_n) * 2 + core, "pos": t % pos_n}

    def each(f):
        def body(k, carry):
            f(lax.rem(me + k, n))
            return carry

        lax.fori_loop(1, n, body, 0)

    def own(t):
        return pl.ds(pl.multiple_of(t * chunk, chunk), chunk)

    def at_side(which, t=None):
        if t is None:
            return pl.ds(pl.multiple_of(which * side, side), side)
        return pl.ds(pl.multiple_of(which * side + t * chunk, chunk), chunk)

    barrier = pltpu.get_barrier_semaphore()
    pl.semaphore_signal(barrier, inc=1, device_id=twin, device_id_type=MESH)
    each(lambda t: pl.semaphore_signal(barrier, inc=1, device_id=ident(t), device_id_type=MESH))
    pk[...] = jnp.zeros_like(pk)
    pack_small(at, pk, *small)
    pl.semaphore_wait(barrier, n)

    to_twin = pltpu.make_async_remote_copy(
        src_ref=pk.at[at_side(1 - core), :], dst_ref=from_twin, send_sem=pair_sems.at[0], recv_sem=pair_sems.at[1],
        device_id=twin, device_id_type=MESH)
    back_twin = pltpu.make_async_remote_copy(
        src_ref=gath.at[at_side(core), :], dst_ref=gath.at[at_side(core), :], send_sem=pair_sems.at[2],
        recv_sem=pair_sems.at[3], device_id=twin, device_id_type=MESH)

    def scatter(t, slot):
        return pltpu.make_async_remote_copy(
            src_ref=half.at[own(t), :], dst_ref=rbuf.at[slot], send_sem=ss1.at[t], recv_sem=rs1.at[slot], device_id=ident(t),
            device_id_type=MESH)

    def publish(t, slot):
        return pltpu.make_async_remote_copy(
            src_ref=red, dst_ref=gath.at[at_side(core, slot), :], send_sem=ss2.at[t], recv_sem=rs2.at[slot],
            device_id=ident(t), device_id_type=MESH)

    def advance(stage):
        for job in jobs:
            if stage < len(job.order):
                job.finish(stage)
                if stage + 1 < len(job.order):
                    job.start(stage + 1)

    to_twin.start()
    for job in jobs:
        job.start(0)
    to_twin.wait()
    half[...] = pk[at_side(core), :] + from_twin[...]
    each(lambda t: scatter(t, me).start())
    rbuf[me] = half[own(me), :]
    advance(0)
    each(lambda t: scatter(t, t).wait())
    total = rbuf[0]
    for s in range(1, n):
        total = total + rbuf[s]
    red[...] = total
    gath[at_side(core, me), :] = total
    each(lambda t: publish(t, me).start())
    stages = max(len(job.order) for job in jobs)
    for stage in range(1, stages - 1):
        advance(stage)
    each(lambda t: publish(t, t).wait())
    back_twin.start()
    advance(stages - 1)
    back_twin.wait()
    packed_out[...] = gath[...]


def exchange(sizes, at, used, small, grads, plan):
    rows_n, pos_n = sizes
    n = rows_n * pos_n
    total = -(-used // (8 * n)) * 8 * n
    chunk = total // n
    vm = pl.BlockSpec(memory_space=pltpu.VMEM)
    tall = lambda rows: pltpu.VMEM((rows, PACK), f32)
    scratch = [tall(total), tall(total // 2), tall(total // 2), pltpu.VMEM((n // 2, chunk, PACK), f32), tall(chunk), tall(total)]
    scratch += [pltpu.SemaphoreType.DMA((n // 2,))] * 4 + [pltpu.SemaphoreType.DMA((4,))]
    shapes = [jax.ShapeDtypeStruct((total, PACK), f32)]
    for src, (start, blocks), alive, order in plan:
        left = job_shapes(grads[src].shape, blocks, alive, order)
        shapes.append(jax.ShapeDtypeStruct(left[-1], bf))
        scratch += job_scratch(left, False)
    return pl.pallas_call(
        functools.partial(exchange_kernel, sizes, at, plan, len(grads)), out_shape=shapes,
        in_specs=[vm] * (9 + len(grads)), out_specs=[vm] * len(shapes), scratch_shapes=scratch,
        compiler_params=pltpu.CompilerParams(collective_id=0, has_side_effects=True, vmem_limit_bytes=VMEM_BYTES),
        name="exchange")(*small, *grads)


def unpack(at, packed, results, blocks, width, hidden, emb, ff):
    per = width // PACK
    counts = [len(parts) for parts in blocks]
    flat = [p for parts in blocks for p in parts]

    def kernel(pk, *refs):
        m = len(results)
        for a, b in zip(refs[:m], refs[len(refs) - m:]):
            b[...] = a[...]

        @pl.when(pl.program_id(0) == 0)
        def _():
            small(pk, *refs[m:len(refs) - m])

    def small(pk, *refs):
        ins = list(refs[:len(flat)])
        fg, fs, mb, sw, sb, ew, eb, eo, iw, ib, io, ow, ob, oo, fw, sk, obias, sg, ss, eb2, rb = refs[len(flat):len(flat) + 21]
        outs = refs[len(flat) + 21:]

        def get(ref, lane, row):
            for h in range(per):
                ref[lane + h * PACK:lane + (h + 1) * PACK] = pk[row + h, :]

        get(fg, 0, at["vec1"])
        get(fs, 0, at["vec1"] + per)
        for i in range(3):
            base = at["sgrad"] + i * 5 * per
            for k in range(3):
                for h in range(per):
                    lane = i * width + h * PACK
                    sw[k:k + 1, lane:lane + PACK] = pk[base + k * per + h:base + k * per + h + 1, :]
            get(sb, i * width, base + 3 * per)
            get(mb, i * width, base + 4 * per)
        q = at["square"]
        ew[...] = pk[q:q + emb, 0:hidden]
        iw[...] = pk[q:q + hidden, 128:128 + hidden]
        ow[...] = pk[q:q + hidden, 256:256 + hidden]
        for k, ref in enumerate((oo, ob, io, ib, eo, eb)):
            ref[...] = pk[at["small"] + k, 0:hidden]
        for h in range(per):
            fw[:, h * PACK:(h + 1) * PACK] = pk[at["filter"] + h * hidden:at["filter"] + (h + 1) * hidden, :]
        get(sk, 0, at["skip"])
        for k, ref in enumerate((sg, ss, obias, rb)):
            get(ref, 0, at["vec2"] + k * per)
        for k in range(ff // width):
            get(eb2, k * width, at["ebias"] + k * per)
        for parts, out in zip(counts, outs):
            lane = 0
            for _ in range(parts):
                src = ins.pop(0)
                for b in range(src.shape[0]):
                    out[:, lane:lane + src.shape[2]] = src[b].astype(f32)
                    lane += src.shape[2]

    s = lambda *d: jax.ShapeDtypeStruct(d, f32)
    shapes = [s(width), s(width), s(3 * width), s(3, 3 * width), s(3 * width), s(emb, hidden), s(hidden), s(hidden),
        s(hidden, hidden), s(hidden), s(hidden), s(hidden, hidden), s(hidden), s(hidden), s(hidden, width), s(width), s(width),
        s(width), s(width), s(ff), s(width)]
    shapes += [s(parts[0].shape[1], sum(p.shape[0] for p in parts) * parts[0].shape[2]) for parts in blocks]
    steps = 2 if results else 1
    whole = lambda a: pl.BlockSpec(a.shape, lambda i: (0,) * len(a.shape))
    part = [pl.BlockSpec((a.shape[0] // steps, a.shape[1]), lambda i: (i, 0)) for a in results]
    return pl.pallas_call(
        kernel, grid=(steps,), out_shape=shapes + [jax.ShapeDtypeStruct(a.shape, a.dtype) for a in results],
        in_specs=[whole(packed)] + part + [whole(a) for a in flat], out_specs=[whole(a) for a in shapes] + part,
        compiler_params=pltpu.CompilerParams(vmem_limit_bytes=VMEM_BYTES), name="unpack")(packed, *results, *flat)


def on_device(sizes, tokens, segments, cotangent, first_gain, first_shift, mixer_weight, mixer_bias, short_weight, short_bias,
        embed_weight, embed_bias, embed_omega, inner_weight, inner_bias, inner_omega, outer_weight, outer_bias, outer_omega,
        filter_weight, skip_gain, output_weight, output_bias, second_gain, second_shift, expand_weight, expand_bias,
        reduce_weight, reduce_bias):
    rows_n, pos_n = sizes
    length, width = tokens.shape[1:]
    emb, hidden = embed_weight.shape
    ff = expand_weight.shape[1]
    tok = tokens.reshape(-1, width)
    cot = cotangent.reshape(-1, width)
    filt = [embed_weight, embed_bias, embed_omega, inner_weight, inner_bias, inner_omega, outer_weight, outer_bias, outer_omega,
        filter_weight]
    tabs, tabst = radix_tables(length)
    zt, rates = filter_inputs(length, emb, width)
    proj, mixed, longc, mix, trans, spec, state, ntr = forward_mixer(
        tok, segments, first_gain, first_shift, mixer_weight, mixer_bias, short_weight, short_bias, skip_gain, filt, zt, rates,
        tabs, tabst)
    direct = rows_n * pos_n == 32 and pos_n == 2 and width % (16 * rows_n) == 0 and width // LANES % pos_n == 0 and ff // rows_n * 4 == width
    links = sizes if direct else None
    out, dat, wog, weg, wrg, beg, vec2 = mlp(
        links, mix, tok, cot, output_weight, output_bias, second_gain, second_shift, expand_weight, expand_bias, reduce_weight,
        reduce_bias)
    tgrad, wmg, sgrad, vec1, gew, giw, gow, gfw, gsm, *early = backward_mixer(
        links, weg, wrg, wog, dat, tok, segments, first_gain, output_weight, longc, mixed, proj, trans, spec, ntr, mixer_weight,
        short_weight, skip_gain, state, filt, zt, rates, tabs, tabst)
    small = (beg, vec2, sgrad, vec1, gew, giw, gow, gfw, gsm)
    at, used = pack_places(width, hidden, emb, ff)
    blocks_m, blocks_o = 3 * width // LANES, width // LANES
    if direct:
        paired = [d for d in alive_dims(rows_n, pos_n) if d != ("rows", 0)]
        third = blocks_m // pos_n // 3
        grads = [wmg.reshape(grad_shape(blocks_m, width, rows_n, pos_n, False))]
        plan = [(0, (k * third, third), paired, order) for k, order in enumerate(three_orders(rows_n, pos_n))]
        packed, *m_parts = exchange(sizes, at, used, small, grads, plan)
        e_a, r_a, e_b, r_b, o_part = early
        blocks = [m_parts, [o_part], [e_a, e_b], [r_a, r_b]]
    else:
        packed = lax.psum(pack_only(at, used, small), ("rows", "pos"))
        grads = [wmg.reshape(blocks_m, width, LANES), wog, weg, wrg]
        blocks = [[scatter_blocks(g, rows_n, pos_n, f)] for g, f in zip(grads, ("pos", "rows", "pos", "rows"))]
    (fg, fs, mb, sw, sb, ew, eb, eo, iw, ib, io, ow, ob, oo, fw, sk, obias, sg, ss, eb2, rb, m_grad, o_grad, e_grad, r_grad, *results) = unpack(
        at, packed, [out, tgrad] if direct else [], blocks, width, hidden, emb, ff)
    if results:
        out, tgrad = results
    return (out.reshape(tokens.shape), tgrad.reshape(tokens.shape), fg, fs, m_grad, mb, sw, sb, ew, eb, eo, iw, ib, io, ow, ob,
        oo, fw, sk, o_grad, obias, sg, ss, e_grad, eb2, r_grad, rb)


def pack_only(at, used, small):
    def kernel(*refs):
        refs[-1][...] = jnp.zeros_like(refs[-1])
        pack_small(at, refs[-1], *refs[:-1])

    vm = pl.BlockSpec(memory_space=pltpu.VMEM)
    return pl.pallas_call(
        kernel, out_shape=jax.ShapeDtypeStruct((used, PACK), f32), in_specs=[vm] * len(small), out_specs=vm, name="pack")(*small)


def solution(mesh):
    both = ("rows", "pos")
    split = P(both, None, None)
    grid = P("rows", "pos")
    in_specs = (split, P(both, None), split) + (P(),) * 25
    out_specs = (split, split, P(), P(), grid) + (P(),) * 14 + (grid, P(), P(), P(), grid, P(), grid, P())
    sizes = (mesh.shape["rows"], mesh.shape["pos"])
    return jax.shard_map(
        functools.partial(on_device, sizes), mesh=mesh, in_specs=in_specs, out_specs=out_specs, check_vma=False)
```
